256 devices in a mesh: fsdp: 64 (over x_lo, z, y), tp: 4 (over x_hi, core).
Axes of the slice: x: 4 (x_hi: 2, x_lo: 2; x = x_hi * 2 + x_lo), y: 4, z: 8, core: 2. Of those that a mesh axis runs over, the one named last changes fastest.
Arguments:
- hidden: bfloat16 [16384, 4096], P('fsdp', 'tp')
- gain: float32 [4096], P('tp'), may hold values from 0.4 to 1.6
- head: bfloat16 [4096, 4096], P('fsdp', 'tp')
- targets: int32 [16384], P('fsdp'), may hold values from 0 to 4095
- row_weight: int32 [16384], P('fsdp'), may hold values from 1 to 3
Outputs:
- loss: float32 [], replicated
- grad_head: float32 [4096, 4096], P('fsdp', 'tp')
- grad_gain: float32 [4096], P('tp')
- grad_hidden: bfloat16 [16384, 4096], P('fsdp', 'tp')
The draws below stay inside these ranges and needn't reach their ends.
All inputs are finite; a program needn't handle non-finite values.
Results may differ from the reference program's by a relative error of at most 0.0024.
The reference program's roundings to bfloat16 on the way (of `normed` and `dlogits`) count: a program that leaves them out, or rounds other values in their place, can miss the bound.
Values may be sent and summed in bfloat16 or wider, within the bound.
A program may use at most 64 MiB of HBM per device.

```python
import math
import jax
import jax.numpy as jnp
from jax import lax

D = 4096
VCH = 4096
TOKENS = 16384


def shared_directions(key):
    direction_key = jax.random.fold_in(key, 5)
    signs = jax.random.bernoulli(direction_key, 0.5, (4, D))
    return jnp.where(signs, jnp.float32(1.0), jnp.float32(-1.0))


def ranks_of(key, count):
    order = jax.random.permutation(key, count)
    return jnp.zeros((count,), jnp.int32).at[order].set(jnp.arange(count, dtype=jnp.int32))


def draw_hidden(key, part):
    directions = shared_directions(key)
    key = jax.random.fold_in(key, 11)
    base_key, row_key, col_key, pick_key = jax.random.split(key, 4)
    base = jax.random.normal(base_key, (TOKENS, D), jnp.float32)
    row_part = jnp.exp(jax.random.uniform(row_key, (TOKENS,), jnp.float32, 0.0, math.log(10.0)))
    col_part = jnp.exp(jax.random.uniform(col_key, (D,), jnp.float32, 0.0, math.log(10.0)))
    spread = base * row_part[:, None] * col_part[None, :]
    ranks = ranks_of(pick_key, TOKENS)
    chosen = ranks < max(TOKENS // 64, 4)
    aligned = directions[ranks % 4] * row_part[:, None]
    return jnp.where(chosen[:, None], aligned, spread).astype(jnp.bfloat16)


def draw_head(key, part):
    directions = shared_directions(key)
    key = jax.random.fold_in(key, 23)
    base_key = jax.random.fold_in(key, 0)
    column_key = jax.random.fold_in(key, 3)
    offset_key = jax.random.fold_in(key, 4)
    base = jax.random.normal(base_key, (D, VCH), jnp.float32) * (3.0 / math.sqrt(D))
    ranks = ranks_of(column_key, VCH)
    chosen = ranks < 8
    levels = jnp.array([120.0, 180.0, 250.0, 310.0], jnp.float32)
    which = ranks % 4
    offset = jax.random.uniform(offset_key, (VCH,), jnp.float32, 1.0, 3.0)
    amplitude = levels[which] - jnp.where(ranks >= 4, offset, jnp.float32(0.0))
    amplitude = jnp.where(chosen, amplitude, jnp.float32(0.0)) / D
    added = directions[which].T * amplitude[None, :]
    return (base + added).astype(jnp.bfloat16)


def place_ends(values, own_key, smallest, top_value):
    longest = values.shape.index(max(values.shape))
    spots = []
    for shift in (0, 1):
        where = [jax.random.randint(jax.random.fold_in(own_key, axis), (), 0, length) for axis, length in enumerate(values.shape)]
        where[longest] = (where[longest] + shift) % values.shape[longest]
        spots.append(tuple(where))
    return values.at[spots[0]].set(smallest).at[spots[1]].set(top_value)


def setup_inputs(seed: int = 0) -> dict:
    key_of = jax.random.split(jax.random.key(seed), 6)
    hidden = draw_hidden(jax.random.fold_in(key_of[5], 71), 0)
    gain = jnp.clip(1.0 + 0.12 * jax.random.normal(key_of[1], (D,), jnp.float32), 0.4, 1.6)
    head = draw_head(jax.random.fold_in(key_of[5], 71), 0)
    targets = place_ends(jax.random.randint(key_of[3], (TOKENS,), 0, VCH), jax.random.fold_in(key_of[3], 1), 0, VCH - 1).astype(jnp.int32)
    row_weight = place_ends(jax.random.randint(key_of[4], (TOKENS,), 1, 4), jax.random.fold_in(key_of[4], 1), 1, 3).astype(jnp.int32)
    return {"hidden": hidden, "gain": gain, "head": head, "targets": targets, "row_weight": row_weight}


epsilon = 1e-05

def reference(hidden, gain, head, targets, row_weight):
    hidden_wide = hidden.astype(jnp.float32)
    inverse_rms = lax.rsqrt(lax.optimization_barrier(jnp.mean(hidden_wide * hidden_wide, axis=1)) + epsilon)
    normed = (hidden_wide * inverse_rms[:, None] * gain[None, :]).astype(jnp.bfloat16)
    row_scale = row_weight.astype(jnp.float32)
    total = jnp.sum(row_scale)
    block = math.gcd(TOKENS, 512)
    count = TOKENS // block
    normed_blocks = normed.reshape(count, block, D)
    target_blocks = targets.reshape(count, block)
    scale_blocks = row_scale.reshape(count, block)
    columns = jnp.arange(VCH, dtype=jnp.int32)

    def step(carry, items):
        head_sum, loss_sum = carry
        rows, wanted, scale = items
        logits = jnp.dot(rows, head, preferred_element_type=jnp.float32)
        largest = lax.optimization_barrier(jnp.max(logits, axis=1))
        lse = largest + jnp.log(lax.optimization_barrier(jnp.sum(jnp.exp(logits - largest[:, None]), axis=1)))
        target_mask = wanted[:, None] == columns[None, :]
        picked = lax.optimization_barrier(jnp.sum(jnp.where(target_mask, logits, jnp.float32(0.0)), axis=1))
        loss_sum = loss_sum + jnp.sum(scale * (lse - picked))
        probs = jnp.exp(logits - lse[:, None])
        dlogits = (scale[:, None] * (probs - target_mask.astype(jnp.float32))).astype(jnp.bfloat16)
        head_sum = head_sum + lax.dot_general(rows, dlogits, (((0,), (0,)), ((), ())), preferred_element_type=jnp.float32)
        dnormed = lax.dot_general(dlogits, head, (((1,), (1,)), ((), ())), preferred_element_type=jnp.float32)
        return ((head_sum, loss_sum), dnormed)
    start = (jnp.zeros((D, VCH), jnp.float32), jnp.float32(0.0))
    (head_sum, loss_sum), dnormed = lax.scan(step, start, (normed_blocks, target_blocks, scale_blocks))
    dnormed = dnormed.reshape(TOKENS, D) / total
    grad_head = head_sum / total
    loss = loss_sum / total
    grad_gain = lax.optimization_barrier(jnp.sum(dnormed * hidden_wide * inverse_rms[:, None], axis=0))
    gained = gain[None, :] * dnormed
    rowdot = lax.optimization_barrier(jnp.sum(gained * hidden_wide, axis=1))
    grad_hidden = inverse_rms[:, None] * gained - hidden_wide * (inverse_rms ** 3 * rowdot / D)[:, None]
    return (loss, grad_head, grad_gain, grad_hidden.astype(jnp.bfloat16))
```

```python
import functools

import jax
import jax.numpy as jnp
from jax import lax
from jax.experimental import pallas as pl
from jax.experimental.pallas import tpu as pltpu
from jax.sharding import PartitionSpec as P

D = 4096
EPS = 1e-05
MESH = pl.DeviceIdType.MESH
F32 = jnp.float32
BF16 = jnp.bfloat16

DY = (1, 3, 2)
SZ = (1, 7)
PEERS = ((1, 0), (3, 0), (2, 0), (0, 1), (1, 1), (3, 1), (2, 1))
FAR_Z = (4, 3, 5, 2, 6, 1, 7, 0)
NEAR_Z = (0, 7, 1, 6, 2, 5, 3, 4)


def kernel(
    hid, gain, hin, tgt, wgt,
    o_loss, o_gh, o_gg, o_hid,
    hb, xg, nm, gg4, tw, ssq, invb, tgtb, wb, lg, dl, dlt,
    st, qt, lseb, stat,
    ght, sba, rba, sa2, ra2, sbb, rbb, syb, ryb, fa, fb, ghs, ghr,
    dno, dns, dnr, dxs, dxr, rbx, tsum2, gps, gxr, msg, ary, arz, tsum, tot_y, tot_z,
    xh_s, xh_r, tw_s, tw_r, gn_s, gn_r, hx_s, hx_r, hf_s, hf_r,
    az_s, az_r, ay_s, ay_r, by_s, by_r, bz_s, bz_r,
    st_s, st_r, qt_s, qt_r, ty_s, ty_r, tz_s, tz_r,
    ra_s, ra_r, rz_s, rz_r, rb_s, rb_r, ry_s, ry_r, fx_s, fx_r,
    dc_s, dc_r, dx_s, dx_r, gx_s, gx_r, gy_s, gy_r, gz_s, gz_r,
):
    f = lax.axis_index("fsdp")
    t = lax.axis_index("tp")
    xl = f // 32
    z = (f // 4) % 8
    y = f % 4
    xh = t // 2
    c = t % 2
    x = xh * 2 + xl

    def dev(x_, y_, z_, c_):
        return (((x_ % 2) * 8 + z_) * 4 + y_, (x_ // 2) * 2 + c_)

    def at_x(dx, dc=0):
        return dev((x + dx) % 4, y, z, (c + dc) % 2)

    def at_y(dy):
        return dev(x, (y + dy) % 4, z, c)

    def at_z(dz):
        return dev(x, y, (z + dz) % 8, c)

    mate = dev(xh * 2 + (1 - xl), y, z, c)

    def yy(k):
        return (y + k) % 4

    def zz(k):
        return (z + k) % 8

    partners = [at_x(dx, dc) for dx, dc in PEERS] + [at_y(d) for d in DY] + [at_z(d) for d in range(1, 8)]
    barrier = pltpu.get_barrier_semaphore()
    for p in partners:
        pl.semaphore_signal(barrier, inc=1, device_id=p, device_id_type=MESH)
    pl.semaphore_wait(barrier, len(partners))

    sent = []

    def rc(src, dst, ss, rs, to):
        return pltpu.make_async_remote_copy(
            src_ref=src, dst_ref=dst, send_sem=ss, recv_sem=rs, device_id=to, device_id_type=MESH
        )

    def send(src, dst, ss, rs, to):
        cp = rc(src, dst, ss, rs, to)
        cp.start()
        sent.append(cp)

    def got(dst, rs):
        rc(dst, dst, rs, rs, at_y(1)).wait_recv()

    oth = pl.multiple_of((1 - xl) * 512, 512)
    own = pl.multiple_of(xl * 512, 512)
    send(hin.at[:, pl.ds(oth, 512)], hb.at[z, y, xl], xh_s, xh_r, mate)
    hb[z, y, xl] = hin[:, pl.ds(own, 512)]

    def b_hop(s, d, k, yk):
        ref = hb.at[zz(-SZ[s] * d), yk, xl]
        send(ref, ref, bz_s.at[s, d, k], bz_r.at[s, d, k], at_z(SZ[s]))

    for j in range(3):
        ref = hb.at[z, y, xl]
        send(ref, ref, by_s.at[j], by_r.at[j], at_y(DY[j]))
    for s in range(2):
        b_hop(s, 0, 0, y)

    tw[xl, 0:2, :] = tgt[...].astype(F32)
    tw[xl, 2:4, :] = wgt[...].astype(F32)
    send(tw.at[xl], tw.at[xl], tw_s, tw_r, mate)
    gg4[t] = gain[...]
    GP = ((0, 1), (2, 0), (2, 1))
    for i, (dx, dc) in enumerate(GP):
        send(gg4.at[t], gg4.at[t], gn_s.at[i], gn_r.at[i], at_x(dx, dc))

    for i, (dx, dc) in enumerate(((1, 0), (3, 0), (2, 0), (0, 1))):
        send(hid, xg.at[xl, t], hx_s.at[i], hx_r.at[i], at_x(dx, dc))
    xg[xl, t] = hid[...]

    def a_hop(s, d):
        ref = hb.at[zz(-SZ[s] * d), y, 1 - xl]
        send(ref, ref, az_s.at[s, d], az_r.at[s, d], at_z(SZ[s]))

    def a_out(k):
        ref = hb.at[zz(k), y, 1 - xl]
        for j in range(3):
            send(ref, ref, ay_s.at[k, j], ay_r.at[k, j], at_y(DY[j]))

    def ywas(j):
        return yy(-DY[j])

    for j in range(3):
        ref = hb.at[z, ywas(j), xl]
        got(ref, by_r.at[j])
        for s in range(2):
            b_hop(s, 0, j + 1, ywas(j))
    got(hb.at[z, y, 1 - xl], xh_r)
    a_hop(0, 0)
    a_hop(1, 0)
    a_out(0)

    got(tw.at[1 - xl], tw_r)

    def ssq_block(xl_, t_):
        def step(i, carry):
            rows = pl.ds(i * 32, 32)
            v = xg[xl_, t_, rows, :].astype(F32)
            v = v * v
            acc = v[:, 0:128]
            for k in range(1, 8):
                acc = acc + v[:, k * 128:(k + 1) * 128]
            ssq[xl_, rows, :] += acc
            return carry
        lax.fori_loop(0, 8, step, 0)

    ssq[...] = jnp.zeros_like(ssq)
    ssq_block(xl, t)

    w_all = tw[0, 2:4, :] + tw[1, 2:4, :]
    tsum[...] = jnp.zeros_like(tsum)
    tsum[0:2, :] = w_all
    for j in range(3):
        send(tsum, tot_y.at[j], ty_s.at[j], ty_r.at[j], at_y(DY[j]))

    def col(row):
        return jnp.transpose(jnp.broadcast_to(row, (128, 128)))

    for a in range(2):
        for k in range(2):
            tgtb[a, k * 128:(k + 1) * 128, :] = col(tw[a, k:k + 1, :])
            wb[a, k * 128:(k + 1) * 128, :] = col(tw[a, 2 + k:3 + k, :])

    def limit(s, k):
        if k < 0:
            return 4 if s == 0 else 3
        return 4 if (k < 2) == (s == 0) else 3

    def a_arrive(s, d):
        got(hb.at[zz(-SZ[s] * d), y, 1 - xl], az_r.at[s, d - 1])
        if d < limit(s, -1):
            a_hop(s, d)
        a_out((-SZ[s] * d) % 8)

    def b_arrive(s, d, k):
        yk = y if k == 0 else ywas(k - 1)
        got(hb.at[zz(-SZ[s] * d), yk, xl], bz_r.at[s, d - 1, k])
        if d < limit(s, k):
            b_hop(s, d, k, yk)

    def b_arrivals(d):
        for k in range(4):
            for s in range(2):
                if d <= limit(s, k):
                    b_arrive(s, d, k)

    a_arrive(0, 1)
    a_arrive(1, 1)
    b_arrivals(1)
    a_arrive(0, 2)
    a_arrive(1, 2)
    for j in range(3):
        got(tot_y.at[j], ty_r.at[j])
    tsum2[...] = tsum[...] + tot_y[0] + tot_y[1] + tot_y[2]
    for d in range(1, 8):
        send(tsum2, tot_z.at[d - 1], tz_s.at[d - 1], tz_r.at[d - 1], at_z(d))
    b_arrivals(2)
    a_arrive(0, 3)
    a_arrive(1, 3)
    a_arrive(0, 4)

    XD = (1, 3, 2)

    def xblock(i):
        xs = (x - XD[i] + 4) % 4
        return xs % 2, (xs // 2) * 2

    def x_forward(i):
        a, b = xblock(i)
        ref = xg.at[a, b + c]
        got(ref, hx_r.at[i])
        send(ref, ref, hf_s.at[i], hf_r.at[i], at_x(0, 1))
        ssq_block(a, b + c)

    def x_second(i):
        a, b = xblock(i)
        got(xg.at[a, b + 1 - c], hf_r.at[i])
        ssq_block(a, b + 1 - c)

    got(xg.at[xl, xh * 2 + 1 - c], hx_r.at[3])
    ssq_block(xl, xh * 2 + 1 - c)
    b_arrivals(3)
    for i in range(3):
        x_forward(i)
    for i in range(3):
        x_second(i)
    for i, (dx, dc) in enumerate(GP):
        ts = ((xh + (dx // 2)) % 2) * 2 + (c + dc) % 2
        got(gg4.at[ts], gn_r.at[i])

    for a in range(2):
        s_ = jnp.sum(ssq[a], axis=1, keepdims=True)
        invb[a] = jnp.broadcast_to(lax.rsqrt(s_ * (1.0 / D) + EPS), (256, 128))

    def norm_z(zb):
        t0 = zb // 4
        off = (zb % 4) * 256

        def step(i, carry):
            a = i // 8
            r = pl.multiple_of((i % 8) * 32, 32)
            rows = pl.ds(r, 32)
            inv = invb[a, rows, :]
            low = lax.broadcasted_iota(jnp.int32, (32, 128), 1) < 64
            for p in range(2):
                cols = slice(off + p * 128, off + (p + 1) * 128)
                u = xg[a, t0, rows, cols].astype(F32) * inv * gg4[t0, :, cols]
                v = xg[a, t0 + 2, rows, cols].astype(F32) * inv * gg4[t0 + 2, :, cols]
                ur = pltpu.roll(u, 64, 1)
                vr = pltpu.roll(v, 64, 1)
                out = pl.ds(pl.multiple_of(i * 32, 32), 32)
                nm[zb, out, (2 * p) * 128:(2 * p + 1) * 128] = jnp.where(low, u, vr).astype(BF16)
                nm[zb, out, (2 * p + 1) * 128:(2 * p + 2) * 128] = jnp.where(low, ur, v).astype(BF16)
            return carry
        lax.fori_loop(0, 16, step, 0)

    for zb in range(8):
        norm_z(zb)

    for n, k in enumerate(NEAR_Z):
        for j in range(3):
            got(hb.at[zz(k), ywas(j), 1 - xl], ay_r.at[k, j])
        if k == 4:
            b_arrivals(4)
        part = jnp.dot(nm[zz(k)], hb[zz(k)].reshape(512, 512), preferred_element_type=F32)
        if n == 0:
            lg[...] = part
        else:
            lg[...] += part

    col0 = (t * 1024 + xl * 512).astype(F32)
    me = x * 2 + c

    def stat_step(i, carry):
        rows = pl.ds(pl.multiple_of(i * 64, 64), 64)
        l = lg[rows, :]
        m = jnp.max(l, axis=1, keepdims=True)
        e = jnp.sum(jnp.exp(l - m), axis=1, keepdims=True)
        a = i // 4
        tb = tgtb[a, pl.ds(pl.multiple_of((i % 4) * 64, 64), 64), :][:, 0:1] - col0
        cols = lax.broadcasted_iota(jnp.int32, (64, 512), 1).astype(F32)
        pk = jnp.sum(jnp.where(cols == tb, l, 0.0), axis=1, keepdims=True)
        lane = lax.broadcasted_iota(jnp.int32, (64, 128), 1)
        stat[rows, :] = jnp.where(lane == 0, m, jnp.where(lane == 1, e, jnp.where(lane == 2, pk, 0.0)))
        return carry

    lax.fori_loop(0, 8, stat_step, 0)
    for k in range(4):
        st[me, k] = jnp.transpose(stat[k * 128:(k + 1) * 128, :])[0:8, :]
    for i, (dx, dc) in enumerate(PEERS):
        send(st.at[me], st.at[me], st_s.at[i], st_r.at[i], at_x(dx, dc))

    def peer_was(i):
        dx, dc = PEERS[i]
        return ((x - dx + 4) % 4) * 2 + (c + dc) % 2

    for i in range(7):
        got(st.at[peer_was(i)], st_r.at[i])
    allst = st[...]
    mx = jnp.max(allst[:, :, 0:1, :], axis=0)
    es = jnp.sum(allst[:, :, 1:2, :] * jnp.exp(allst[:, :, 0:1, :] - mx[None]), axis=0)
    pk = jnp.sum(allst[:, :, 2:3, :], axis=0)
    lse = mx + jnp.log(es)
    loss_row = jnp.zeros((1, 128), F32)
    for k in range(4):
        loss_row = loss_row + tw[k // 2, 2 + k % 2:3 + k % 2, :] * (lse[k] - pk[k])
        lseb[k * 128:(k + 1) * 128, :] = col(lse[k])

    def dl_step(i, carry):
        a = i // 8
        r = pl.multiple_of((i % 8) * 32, 32)
        rows = pl.ds(r, 32)
        g = pl.ds(pl.multiple_of(i * 32, 32), 32)
        l = lg[g, :]
        tb = tgtb[a, rows, :][:, 0:1] - col0
        w = wb[a, rows, :][:, 0:1]
        cols = lax.broadcasted_iota(jnp.int32, (32, 512), 1).astype(F32)
        p = jnp.exp(l - lseb[g, :][:, 0:1])
        d = (w * (p - jnp.where(cols == tb, 1.0, 0.0))).astype(BF16)
        dl[a, rows, :] = d
        q = jnp.sum(d.astype(F32) * l, axis=1, keepdims=True)
        stat[g, :] = jnp.broadcast_to(q, (32, 128))
        return carry

    lax.fori_loop(0, 16, dl_step, 0)
    for a in range(2):
        dlt[:, a * 256:(a + 1) * 256] = jnp.transpose(dl[a])

    def head_grad(k):
        g = jnp.dot(dlt[...], nm[zz(k)], preferred_element_type=F32)
        for b in range(4):
            ght[k, b] = g[:, b * 128:(b + 1) * 128]
        for j in range(3):
            sba[k, j] = ght[k, yy(DY[j]), 0:256, :].astype(BF16)
            send(sba.at[k, j], rba.at[k, j], ra_s.at[k, j], ra_r.at[k, j], at_y(DY[j]))

    def qrows(q):
        return slice(256 + q * 128, 384 + q * 128)

    def b_chain(s, d, q):
        k = (SZ[s] * d) % 8
        v = ght[k, :, qrows(q), :]
        if d < (4 if q == s else 3):
            got(rbb.at[s, q, d], rb_r.at[s, q, d])
            v = v + rbb[s, q, d].astype(F32)
        sbb[s, q, d - 1] = v.astype(BF16)
        send(sbb.at[s, q, d - 1], rbb.at[s, q, d - 1], rb_s.at[s, q, d - 1], rb_r.at[s, q, d - 1], at_z(SZ[s]))

    def a_sum(k):
        v = ght[k, y, 0:256, :]
        for j in range(3):
            got(rba.at[k, j], ra_r.at[k, j])
            v = v + rba[k, j].astype(F32)
        return v

    def a_chain4():
        fa[...] = a_sum(4)
        for s in range(2):
            h = slice(s * 128, (s + 1) * 128)
            sa2[s, 3, h] = fa[h, :]
            send(sa2.at[s, 3, h], ra2.at[s, 3, h], rz_s.at[s, 3], rz_r.at[s, 3], at_z(SZ[s]))

    def a_chain(s, d):
        v = a_sum((SZ[s] * d) % 8)
        if d == 3:
            h = slice(s * 128, (s + 1) * 128)
            sa2[s, 2] = v
            got(ra2.at[s, 3, h], rz_r.at[s, 3])
            sa2[s, 2, h] = v[h] + ra2[s, 3, h]
        else:
            got(ra2.at[s, d], rz_r.at[s, d])
            sa2[s, d - 1] = v + ra2[s, d]
        send(sa2.at[s, d - 1], ra2.at[s, d - 1], rz_s.at[s, d - 1], rz_r.at[s, d - 1], at_z(SZ[s]))

    XO = (2, 1, 3, 0)

    def xdest(n):
        xs = (x + XO[n]) % 4
        return xs % 2, xs // 2

    def dn_part(out, n, cc):
        a, b = xdest(n)
        for i in range(4):
            h = hb[4 * cc + i, :, b].reshape(256, 512)
            out[n, :, i * 256:(i + 1) * 256] = lax.dot_general(
                dl[a], h, (((1,), (1,)), ((), ())), preferred_element_type=F32
            )

    def dn_start(n):
        dn_part(dns, n, 1 - c)
        send(dns.at[n], dnr.at[n], dc_s.at[n], dc_r.at[n], at_x(0, 1))
        dn_part(dno, n, c)

    def dn_sum(n):
        got(dnr.at[n], dc_r.at[n])
        a, b = xdest(n)
        tx = b * 2 + c

        def step(i, acc):
            rows = pl.ds(pl.multiple_of(i * 16, 16), 16)
            s_ = dno[n, rows, :] + dnr[n, rows, :]
            dno[n, rows, :] = s_
            if XO[n] == 2:
                dxs[rows, :] = s_.astype(BF16)
            xv = xg[a, tx, rows, :].astype(F32) * invb[a, rows, :][:, 0:1]
            pr = s_ * xv
            return acc + pr[0:8] + pr[8:16]
        acc = lax.fori_loop(0, 16, step, jnp.zeros((8, 1024), F32))
        gps[b * 2 + a] = jnp.sum(acc, axis=0, keepdims=True)
        if XO[n] == 2:
            send(dxs, dxr, dx_s.at[2], dx_r.at[2], at_x(2))
        elif XO[n] == 1:
            send(dno.at[n], rbx.at[0], dx_s.at[0], dx_r.at[0], at_x(1))
        elif XO[n] == 3:
            send(dno.at[n], rbx.at[1], dx_s.at[1], dx_r.at[1], at_x(3))

    dn_start(0)
    head_grad(4)
    b_chain(0, 4, 0)
    b_chain(1, 4, 1)
    dn_sum(0)
    head_grad(3)
    b_chain(0, 3, 1)
    head_grad(5)
    b_chain(1, 3, 0)
    dn_start(1)
    dn_start(2)
    a_chain4()
    dn_sum(1)
    dn_sum(2)
    head_grad(2)
    head_grad(6)
    b_chain(0, 3, 0)
    b_chain(1, 3, 1)
    head_grad(1)
    head_grad(7)
    head_grad(0)
    b_chain(0, 2, 1)
    b_chain(1, 2, 0)
    a_chain(0, 3)
    a_chain(1, 3)
    dn_start(3)
    dn_sum(3)

    def gpair(b):
        return gps[2 * b] + gps[2 * b + 1]

    for b in range(2):
        gxr[3 + b] = gpair(b)
    for i, dx in enumerate((1, 3, 2)):
        b = ((x + dx) % 4) // 2
        send(gxr.at[3 + b], gxr.at[i], gx_s.at[i], gx_r.at[i], at_x(dx))

    for k in range(4):
        qt[me, k] = jnp.transpose(stat[k * 128:(k + 1) * 128, :])[0:8, :]
    for i, (dx, dc) in enumerate(PEERS):
        send(qt.at[me], qt.at[me], qt_s.at[i], qt_r.at[i], at_x(dx, dc))

    b_chain(0, 2, 0)
    b_chain(1, 2, 1)
    for i in range(3):
        got(gxr.at[i], gx_r.at[i])
    msg[0] = gxr[3 + xh] + gxr[0] + gxr[1] + gxr[2]
    msg[1] = jnp.zeros((1, 1024), F32)
    msg[1, :, 0:128] = loss_row
    for j in range(3):
        send(msg, ary.at[j], gy_s.at[j], gy_r.at[j], at_y(DY[j]))

    b_chain(0, 1, 1)
    b_chain(1, 1, 0)
    a_chain(0, 2)
    a_chain(1, 2)
    for j in range(3):
        got(ary.at[j], gy_r.at[j])
    msg_sum = msg[...] + ary[0] + ary[1] + ary[2]
    ary[3] = msg_sum
    for d in range(1, 8):
        send(ary.at[3], arz.at[d - 1], gz_s.at[d - 1], gz_r.at[d - 1], at_z(d))
    for d in range(1, 8):
        got(tot_z.at[d - 1], tz_r.at[d - 1])
    tot = tsum2[...]
    for d in range(7):
        tot = tot + tot_z[d]
    inv_total = 1.0 / jnp.sum(jnp.sum(tot, axis=1, keepdims=True), axis=0, keepdims=True)

    for i in range(7):
        got(qt.at[peer_was(i)], qt_r.at[i])
    qsum = qt[0]
    for i in range(1, 8):
        qsum = qsum + qt[i]
    for k in range(4):
        lseb[k * 128:(k + 1) * 128, :] = col(qsum[k, 0:1, :])

    b_chain(0, 1, 0)
    b_chain(1, 1, 1)
    a_chain(0, 1)
    a_chain(1, 1)
    va = a_sum(0)
    for s in range(2):
        got(ra2.at[s, 0], rz_r.at[s, 0])
        va = va + ra2[s, 0]
    fa[...] = va
    ft = jnp.transpose(fa[...])
    for a in range(2):
        ghs[a, :, 0:256] = ft[a * 64:(a + 1) * 64]
    for q in (1, 0):
        v = ght[0, :, qrows(q), :]
        for s in range(2):
            got(rbb.at[s, q, 0], rb_r.at[s, q, 0])
            v = v + rbb[s, q, 0].astype(F32)
        syb[q] = v
        for j in range(3):
            src = syb.at[q, yy(DY[j])]
            send(src, ryb.at[q, j], ry_s.at[q, j], ry_r.at[q, j], at_y(DY[j]))
    for q in (1, 0):
        v = syb[q, y]
        for j in range(3):
            got(ryb.at[q, j], ry_r.at[q, j])
            v = v + ryb[q, j]
        fb[q] = v
        ft = jnp.transpose(fb[q])
        for a in range(2):
            ghs[a, :, 256 + q * 128:384 + q * 128] = ft[a * 64:(a + 1) * 64]
    send(ghs.at[1 - xl], ghr, fx_s, fx_r, mate)

    for d in range(1, 8):
        got(arz.at[d - 1], gz_r.at[d - 1])
    gl = ary[3]
    for d in range(7):
        gl = gl + arz[d]
    o_gg[...] = gl[0] * inv_total
    o_loss[...] = jnp.broadcast_to(jnp.sum(gl[1], axis=1, keepdims=True) * inv_total, (8, 128))
    o_gh[:, pl.ds(own, 512)] = ghs[xl] * inv_total

    got(rbx.at[0], dx_r.at[0])
    got(rbx.at[1], dx_r.at[1])
    got(dxr, dx_r.at[2])
    gt = gg4[t]

    def fin(i, carry):
        rows = pl.ds(pl.multiple_of(i * 16, 16), 16)
        qrow = pl.ds(pl.multiple_of(xl * 256 + i * 16, 16), 16)
        dn = dno[3, rows, :] + rbx[0, rows, :] + rbx[1, rows, :] + dxr[rows, :].astype(F32)
        inv = invb[xl, rows, :][:, 0:1]
        q = lseb[qrow, :][:, 0:1]
        xv = hid[rows, :].astype(F32)
        u = inv * inv_total
        o_hid[rows, :] = (dn * gt * u - xv * (inv * u * q * (1.0 / D))).astype(BF16)
        return carry

    lax.fori_loop(0, 16, fin, 0)
    got(ghr, fx_r)
    o_gh[:, pl.ds(oth, 512)] = ghr[...] * inv_total
    for cp in sent:
        cp.wait_send()


def body(hidden, gain, head, targets, row_weight):
    V = pltpu.VMEM
    S = pltpu.SemaphoreType.DMA
    vm = pl.BlockSpec(memory_space=pltpu.VMEM)
    scratch = [
        V((8, 4, 2, 64, 512), BF16),
        V((2, 4, 256, 1024), BF16),
        V((8, 512, 512), BF16),
        V((4, 1, 1024), F32),
        V((2, 8, 128), F32),
        V((2, 256, 128), F32),
        V((2, 256, 128), F32),
        V((2, 256, 128), F32),
        V((2, 256, 128), F32),
        V((512, 512), F32),
        V((2, 256, 512), BF16),
        V((512, 512), BF16),
        V((8, 4, 8, 128), F32),
        V((8, 4, 8, 128), F32),
        V((512, 128), F32),
        V((512, 128), F32),
        V((8, 4, 512, 128), F32),
        V((8, 3, 256, 128), BF16),
        V((8, 3, 256, 128), BF16),
        V((2, 4, 256, 128), F32),
        V((2, 4, 256, 128), F32),
        V((2, 2, 4, 4, 128, 128), BF16),
        V((2, 2, 4, 4, 128, 128), BF16),
        V((2, 4, 128, 128), F32),
        V((2, 3, 128, 128), F32),
        V((256, 128), F32),
        V((2, 128, 128), F32),
        V((2, 64, 512), F32),
        V((64, 512), F32),
        V((4, 256, 1024), F32),
        V((4, 256, 1024), F32),
        V((4, 256, 1024), F32),
        V((256, 1024), BF16),
        V((256, 1024), BF16),
        V((2, 256, 1024), F32),
        V((8, 128), F32),
        V((4, 1, 1024), F32),
        V((5, 1, 1024), F32),
        V((2, 1, 1024), F32),
        V((4, 2, 1, 1024), F32),
        V((7, 2, 1, 1024), F32),
        V((8, 128), F32),
        V((3, 8, 128), F32),
        V((7, 8, 128), F32),
    ]
    shapes = [
        (), (), (3,), (4,), (3,),
        (2, 4), (8, 3), (3,), (2, 4, 4),
        (7,), (7,), (3,), (7,),
        (8, 3), (2, 4), (2, 2, 4), (2, 3), (),
        (4,), (3,), (3,), (3,), (7,),
    ]
    for sh in shapes:
        scratch += [S(sh), S(sh)] if sh else [S, S]
    loss, gh, gg, gx = pl.pallas_call(
        kernel,
        out_shape=(
            jax.ShapeDtypeStruct((8, 128), F32),
            jax.ShapeDtypeStruct((64, 1024), F32),
            jax.ShapeDtypeStruct((1, 1024), F32),
            jax.ShapeDtypeStruct((256, 1024), BF16),
        ),
        in_specs=[vm] * 5,
        out_specs=(vm, vm, vm, vm),
        scratch_shapes=scratch,
        compiler_params=pltpu.CompilerParams(
            collective_id=0, has_side_effects=True, vmem_limit_bytes=62 << 20
        ),
    )(hidden, gain.reshape(1, 1024), head, targets.reshape(2, 128), row_weight.reshape(2, 128))
    return (loss[0, 0], gh, gg.reshape(1024), gx)


def solution(mesh):
    in_specs = (P("fsdp", "tp"), P("tp"), P("fsdp", "tp"), P("fsdp"), P("fsdp"))
    out_specs = (P(), P("fsdp", "tp"), P("tp"), P("fsdp", "tp"))
    return jax.shard_map(body, mesh=mesh, in_specs=in_specs, out_specs=out_specs, check_vma=False)
```

```python
import functools

import jax
import jax.numpy as jnp
from jax import lax
from jax.experimental import pallas as pl
from jax.experimental.pallas import tpu as pltpu
from jax.sharding import PartitionSpec as P

D = 4096
EPS = 1e-05
MESH = pl.DeviceIdType.MESH
F32 = jnp.float32
BF16 = jnp.bfloat16

DY = (1, 3, 2)
SZ = (1, 7)
PEERS = ((1, 0), (3, 0), (2, 0), (0, 1), (1, 1), (3, 1), (2, 1))
GATHER = (
    ("xe",), ("by", 1), ("bz", 0, 1, 0), ("bz", 1, 1, 0), ("by", 2), ("az", 0, 1), ("az", 1, 1), ("xo",),
    ("bz", 0, 1, 1), ("bz", 1, 1, 1), ("bz", 0, 2, 0), ("bz", 1, 2, 0), ("xf", 1), ("xf", 0), ("by", 3),
    ("az", 0, 2), ("az", 1, 2), ("xs", 1), ("xs", 0), ("ty",), ("bz", 0, 1, 2), ("bz", 1, 1, 2), ("iv", 1),
    ("nm", 1, 0), ("nm", 1, 1), ("nm", 1, 2), ("nm", 1, 3), ("bz", 0, 2, 1), ("bz", 1, 2, 1), ("nm", 1, 4),
    ("nm", 1, 5), ("nm", 1, 6), ("nm", 1, 7), ("bz", 0, 3, 0), ("bz", 1, 3, 0), ("az", 0, 3), ("az", 1, 3),
    ("bz", 0, 1, 3), ("bz", 1, 1, 3), ("bz", 0, 2, 2), ("bz", 1, 2, 2), ("xf", 2), ("bz", 0, 3, 1), ("bz", 1, 3, 1),
    ("tz", 1), ("xs", 2), ("iv", 0), ("nm", 0, 0), ("nm", 0, 1), ("nm", 0, 2), ("bz", 0, 4, 0), ("bz", 1, 2, 3),
    ("nm", 0, 3), ("nm", 0, 4), ("nm", 0, 5), ("az", 0, 4), ("bz", 1, 3, 2), ("nm", 0, 6), ("nm", 0, 7), ("lg", 0),
    ("bz", 0, 2, 3), ("bz", 1, 3, 3), ("lg", 7), ("lg", 1), ("bz", 0, 3, 2), ("bz", 1, 4, 2), ("lg", 6), ("tz", 2),
    ("lg", 2), ("bz", 0, 4, 1), ("lg", 3), ("bz", 0, 3, 3), ("bz", 1, 4, 3), ("lg", 5), ("lg", 4),
)
SCATTER = (
    ("hg", 4), ("bc", 0, 4, 0), ("bc", 1, 4, 1), ("bc", 0, 4, 2), ("bc", 1, 4, 3), ("hg", 3), ("bc", 0, 3, 1),
    ("bc", 0, 3, 3), ("hg", 5), ("bc", 1, 3, 0), ("bc", 1, 3, 2), ("ds", 0), ("hg", 2), ("ds", 1), ("du", 0),
    ("bc", 0, 3, 0), ("bc", 1, 3, 1), ("ds", 2), ("bc", 0, 3, 2), ("bc", 1, 3, 3), ("hg", 6), ("a4",), ("du", 1),
    ("bc", 0, 2, 1), ("bc", 1, 2, 0), ("ds", 3), ("du", 2), ("bc", 0, 2, 3), ("bc", 1, 2, 2), ("du", 3), ("gy",),
    ("hg", 1), ("bc", 0, 2, 0), ("bc", 1, 2, 1), ("hg", 7), ("hg", 0), ("xr", 1), ("xr", 2), ("ac", 0, 3),
    ("ac", 1, 3), ("bc", 0, 2, 2), ("bc", 1, 2, 3), ("bc", 0, 1, 1), ("bc", 1, 1, 0), ("tz", 3), ("bc", 0, 1, 3),
    ("bc", 1, 1, 2), ("bc", 0, 1, 0), ("bc", 1, 1, 1), ("ac", 0, 2), ("ac", 1, 2), ("gz",), ("bc", 0, 1, 2),
    ("bc", 1, 1, 3), ("tz", 4), ("qt",), ("bf", 0), ("bf", 1), ("ac", 0, 1), ("ac", 1, 1), ("bf", 2), ("bf", 3),
    ("gx",), ("bg", 0), ("bg", 1), ("af",), ("fi",), ("gf",), ("gh",),
)


def kernel(
    hid, gain, hin_hbm, tgt_hbm, wgt_hbm,
    r_loss, r_gh, r_gg, r_hid,
    tgt, wgt, o_loss, o_gh, o_gg, o_hid, hin, hb, xg, nm, gg4, tw, ssq, invb, tgtb, wb, lg, ex, dl, dlt,
    st, qt, lseb, stat,
    ght, sba, rba, sa4, ra4, sa3, ra3, sa2, ra2, sbb, rbb, syb, ryb, fa, fb, ghs, ghr,
    dno, dns, dnr, dxs, dxr, dos, dor, rbx, gps, gxs, gxr, msg, ary, arz, tsum, tsum2, tot_y, tot_z,
    in_s, out_s,
    xh_s, xh_r, tw_s, tw_r, gn_s, gn_r, hx_s, hx_r, hh_s, hh_r, hf_s, hf_r,
    az_s, az_r, ay_s, ay_r, by_s, by_r, bz_s, bz_r,
    st_s, st_r, qt_s, qt_r, ty_s, ty_r, tz_s, tz_r,
    ra_s, ra_r, rz_s, rz_r, rb_s, rb_r, ry_s, ry_r, fx_s, fx_r,
    dc_s, dc_r, d2_s, d2_r, dx_s, dx_r, do_s, do_r, gx_s, gx_r, gy_s, gy_r, gz_s, gz_r,
):
    f = lax.axis_index("fsdp")
    t = lax.axis_index("tp")
    xl = f // 32
    z = (f // 4) % 8
    y = f % 4
    xh = t // 2
    c = t % 2
    x = xh * 2 + xl

    def dev(x_, y_, z_, c_):
        return (((x_ % 2) * 8 + z_) * 4 + y_, (x_ // 2) * 2 + c_)

    def at_x(dx, dc=0):
        return dev((x + dx) % 4, y, z, (c + dc) % 2)

    def at_y(dy):
        return dev(x, (y + dy) % 4, z, c)

    def at_z(dz):
        return dev(x, y, (z + dz) % 8, c)

    mate = dev(xh * 2 + (1 - xl), y, z, c)

    def yy(k):
        return (y + k) % 4

    def zz(k):
        return (z + k) % 8

    partners = [at_x(dx, dc) for dx, dc in PEERS] + [at_y(d) for d in DY] + [at_z(d) for d in SZ]
    barrier = pltpu.get_barrier_semaphore()
    for p in partners:
        pl.semaphore_signal(barrier, inc=1, device_id=p, device_id_type=MESH)
    in_hid = pltpu.make_async_copy(hid, xg.at[xl, t], in_s.at[0])
    in_head = pltpu.make_async_copy(hin_hbm, hin, in_s.at[1])
    in_small = [
        pltpu.make_async_copy(src, dst, in_s.at[2 + i])
        for i, (src, dst) in enumerate(((tgt_hbm, tgt), (wgt_hbm, wgt), (gain, gg4.at[t])))
    ]
    in_head.start()
    in_hid.start()
    for cp in in_small:
        cp.start()
    oth = pl.multiple_of((1 - xl) * 512, 512)
    own = pl.multiple_of(xl * 512, 512)
    in_head.wait()
    hb[z, y, xl] = hin[:, pl.ds(own, 512)]
    pl.semaphore_wait(barrier, len(partners))

    sent = []

    def rc(src, dst, ss, rs, to):
        return pltpu.make_async_remote_copy(
            src_ref=src, dst_ref=dst, send_sem=ss, recv_sem=rs, device_id=to, device_id_type=MESH
        )

    def send(src, dst, ss, rs, to):
        cp = rc(src, dst, ss, rs, to)
        cp.start()
        sent.append(cp)

    def got(dst, rs):
        rc(dst, dst, rs, rs, at_y(1)).wait_recv()

    def b_hop(s, d, k):
        yk = y if k == 0 else ywas(k - 1)
        ref = hb.at[zz(-SZ[s] * d), yk, xl]
        send(ref, ref, bz_s.at[s, d, k], bz_r.at[s, d, k], at_z(SZ[s]))

    def a_hop(s, d):
        ref = hb.at[zz(-SZ[s] * d), y, 1 - xl]
        send(ref, ref, az_s.at[s, d], az_r.at[s, d], at_z(SZ[s]))

    def a_out(k):
        ref = hb.at[zz(k), y, 1 - xl]
        for j in range(3):
            send(ref, ref, ay_s.at[k, j], ay_r.at[k, j], at_y(DY[j]))

    def ywas(j):
        return yy(-DY[j])

    def limit(s, k):
        if k < 0:
            return 4 if s == 0 else 3
        return 4 if (k < 2) == (s == 0) else 3

    def ring_limit(s):
        return 4 if s == 0 else 3

    send(hin.at[:, pl.ds(oth, 512)], hb.at[z, y, xl], xh_s, xh_r, mate)
    def b_out(j):
        ref = hb.at[z, y, xl]
        send(ref, ref, by_s.at[j], by_r.at[j], at_y(DY[j]))

    b_out(0)
    b_out(1)
    for s in range(2):
        b_hop(s, 0, 0)
    for cp in in_small:
        cp.wait()
    tw[xl, 0:2, :] = tgt[...].astype(F32)
    tw[xl, 2:4, :] = wgt[...].astype(F32)
    send(tw.at[xl], tw.at[xl], tw_s, tw_r, mate)
    GP = ((0, 1), (2, 0), (2, 1))
    for i, (dx, dc) in enumerate(GP):
        send(gg4.at[t], gg4.at[t], gn_s.at[i], gn_r.at[i], at_x(dx, dc))
    in_hid.wait()
    for i, dx, dc in ((3, 0, 1), (0, 1, 0), (1, 3, 0)):
        send(xg.at[xl, t], xg.at[xl, t], hx_s.at[i], hx_r.at[i], at_x(dx, dc))

    def ssq_block(xl_, t_):
        def step(i, carry):
            rows = pl.ds(pl.multiple_of(i * 32, 32), 32)
            v = xg[xl_, t_, rows, :].astype(F32)
            v = v * v
            acc = v[:, 0:128]
            for k in range(1, 8):
                acc = acc + v[:, k * 128:(k + 1) * 128]
            ssq[xl_, rows, :] += acc
            return carry
        lax.fori_loop(0, 8, step, 0, unroll=4)

    def col(row):
        return jnp.transpose(jnp.broadcast_to(row, (128, 128)))

    ssq[...] = jnp.zeros_like(ssq)
    ssq_block(xl, t)

    def tokens():
        got(tw.at[1 - xl], tw_r)
        tsum[...] = jnp.zeros_like(tsum)
        tsum[0:2, :] = tw[0, 2:4, :] + tw[1, 2:4, :]
        for j in range(3):
            send(tsum, tot_y.at[j], ty_s.at[j], ty_r.at[j], at_y(DY[j]))
        for a in range(2):
            for k in range(2):
                tgtb[a, k * 128:(k + 1) * 128, :] = col(tw[a, k:k + 1, :])
                wb[a, k * 128:(k + 1) * 128, :] = col(tw[a, 2 + k:3 + k, :])

    def t_hop(src, s, d):
        send(src, tot_z.at[s, d], tz_s.at[s, d], tz_r.at[s, d], at_z(SZ[s]))

    def do_ty():
        for j in range(3):
            got(tot_y.at[j], ty_r.at[j])
        tsum2[...] = tsum[...] + tot_y[0] + tot_y[1] + tot_y[2]
        for s in range(2):
            t_hop(tsum2, s, 0)

    def do_tz(d):
        for s in range(2):
            if d <= ring_limit(s):
                got(tot_z.at[s, d - 1], tz_r.at[s, d - 1])
                if d < ring_limit(s):
                    t_hop(tot_z.at[s, d - 1], s, d)

    def do_xe():
        got(hb.at[z, y, 1 - xl], xh_r)
        a_hop(0, 0)
        a_hop(1, 0)
        b_out(2)
        a_out(0)

    def do_by(k):
        got(hb.at[z, ywas(k - 1), xl], by_r.at[k - 1])
        for s in range(2):
            b_hop(s, 0, k)

    def do_az(s, d):
        got(hb.at[zz(-SZ[s] * d), y, 1 - xl], az_r.at[s, d - 1])
        if d < limit(s, -1):
            a_hop(s, d)
        a_out((-SZ[s] * d) % 8)

    def do_bz(s, d, k):
        yk = y if k == 0 else ywas(k - 1)
        got(hb.at[zz(-SZ[s] * d), yk, xl], bz_r.at[s, d - 1, k])
        if d < limit(s, k):
            b_hop(s, d, k)

    def rows_of(i):
        return slice(i * 128, (i + 1) * 128)

    XD = (1, 3, 2)

    def xblock(i):
        xs = (x - XD[i] + 4) % 4
        return xs % 2, (xs // 2) * 2

    def do_xf(i):
        a, b = xblock(i)
        ref = xg.at[a, b + c]
        if i < 2:
            got(ref, hx_r.at[i])
            part = xg.at[a, b + c, rows_of(i)]
            send(part, part, hh_s.at[i], hh_r.at[i], at_x((1, 3)[i]))
        else:
            for h in range(2):
                got(xg.at[a, b + c, rows_of(h)], hh_r.at[h])
        send(ref, ref, hf_s.at[i], hf_r.at[i], at_x(0, 1))
        ssq_block(a, b + c)

    def do_xs(i):
        a, b = xblock(i)
        got(xg.at[a, b + 1 - c], hf_r.at[i])
        ssq_block(a, b + 1 - c)

    def do_xo():
        got(xg.at[xl, xh * 2 + 1 - c], hx_r.at[3])
        ssq_block(xl, xh * 2 + 1 - c)
        for i, (dx, dc) in enumerate(GP):
            ts = ((xh + (dx // 2)) % 2) * 2 + (c + dc) % 2
            got(gg4.at[ts], gn_r.at[i])

    def half(h):
        return (xl + h) % 2

    def do_iv(h):
        a = half(h)
        s_ = jnp.sum(ssq[a], axis=1, keepdims=True)
        invb[a] = jnp.broadcast_to(lax.rsqrt(s_ * (1.0 / D) + EPS), (256, 128))

    def do_nm(h, zb):
        a = half(h)
        t0 = zb // 4
        off = (zb % 4) * 256

        def step(i, carry):
            rows = pl.ds(pl.multiple_of(i * 32, 32), 32)
            out = pl.ds(pl.multiple_of(a * 256 + i * 32, 32), 32)
            inv = invb[a, rows, :]
            low = lax.broadcasted_iota(jnp.int32, (32, 128), 1) < 64
            for p in range(2):
                cols = slice(off + p * 128, off + (p + 1) * 128)
                u = xg[a, t0, rows, cols].astype(F32) * inv * gg4[t0, :, cols]
                v = xg[a, t0 + 2, rows, cols].astype(F32) * inv * gg4[t0 + 2, :, cols]
                ur = pltpu.roll(u, 64, 1)
                vr = pltpu.roll(v, 64, 1)
                nm[zb, out, (2 * p) * 128:(2 * p + 1) * 128] = jnp.where(low, u, vr).astype(BF16)
                nm[zb, out, (2 * p + 1) * 128:(2 * p + 2) * 128] = jnp.where(low, ur, v).astype(BF16)
            return carry
        lax.fori_loop(0, 8, step, 0, unroll=4)

    def do_lg(k):
        for j in range(3):
            got(hb.at[zz(k), ywas(j), 1 - xl], ay_r.at[k, j])
        part = jnp.dot(nm[zz(k)], hb[zz(k)].reshape(512, 512), preferred_element_type=F32)
        if k == 0:
            lg[...] = part
        else:
            lg[...] += part

    steps = dict(
        xe=do_xe, by=do_by, az=do_az, bz=do_bz, xf=do_xf, xs=do_xs, xo=do_xo,
        iv=do_iv, nm=do_nm, lg=do_lg, ty=do_ty, tz=do_tz,
    )
    tokens_done = False
    for name, *arg in GATHER:
        steps[name](*arg)
        if name == "by" and not tokens_done:
            tokens_done = True
            tokens()

    col0 = (t * 1024 + xl * 512).astype(F32)
    me = x * 2 + c

    def stat_step(i, carry):
        rows = pl.ds(pl.multiple_of(i * 32, 32), 32)
        l = lg[rows, :]
        m = jnp.max(l, axis=1, keepdims=True)
        ev = jnp.exp(l - m)
        ex[rows, :] = ev
        e = jnp.sum(ev, axis=1, keepdims=True)
        a = i // 8
        tb = tgtb[a, pl.ds(pl.multiple_of((i % 8) * 32, 32), 32), :][:, 0:1] - col0
        cols = lax.broadcasted_iota(jnp.int32, (32, 512), 1).astype(F32)
        pk = jnp.sum(jnp.where(cols == tb, l, 0.0), axis=1, keepdims=True)
        lane = lax.broadcasted_iota(jnp.int32, (32, 128), 1)
        stat[rows, :] = jnp.where(lane == 0, m, jnp.where(lane == 1, e, jnp.where(lane == 2, pk, 0.0)))
        return carry

    lax.fori_loop(0, 16, stat_step, 0, unroll=4)
    for k in range(4):
        st[me, k] = jnp.transpose(stat[k * 128:(k + 1) * 128, :])[0:8, :]
    for i, (dx, dc) in enumerate(PEERS):
        send(st.at[me], st.at[me], st_s.at[i], st_r.at[i], at_x(dx, dc))

    def peer_was(i):
        dx, dc = PEERS[i]
        return ((x - dx + 4) % 4) * 2 + (c + dc) % 2

    for i in range(7):
        got(st.at[peer_was(i)], st_r.at[i])
    allst = st[...]
    mx = jnp.max(allst[:, :, 0:1, :], axis=0)
    es = jnp.sum(allst[:, :, 1:2, :] * jnp.exp(allst[:, :, 0:1, :] - mx[None]), axis=0)
    pk = jnp.sum(allst[:, :, 2:3, :], axis=0)
    lse = mx + jnp.log(es)
    loss_row = jnp.zeros((1, 128), F32)
    for k in range(4):
        loss_row = loss_row + tw[k // 2, 2 + k % 2:3 + k % 2, :] * (lse[k] - pk[k])
        lseb[k * 128:(k + 1) * 128, :] = col(lse[k])

    def dl_step(i, carry):
        a = i // 8
        rows = pl.ds(pl.multiple_of((i % 8) * 32, 32), 32)
        g = pl.ds(pl.multiple_of(i * 32, 32), 32)
        l = lg[g, :]
        tb = tgtb[a, rows, :][:, 0:1] - col0
        w = wb[a, rows, :][:, 0:1]
        cols = lax.broadcasted_iota(jnp.int32, (32, 512), 1).astype(F32)
        p = ex[g, :] * jnp.exp(stat[g, :][:, 0:1] - lseb[g, :][:, 0:1])
        d = (w * (p - jnp.where(cols == tb, 1.0, 0.0))).astype(BF16)
        dl[a, rows, :] = d
        q = jnp.sum(d.astype(F32) * l, axis=1, keepdims=True)
        stat[g, :] = jnp.broadcast_to(q, (32, 128))
        return carry

    lax.fori_loop(0, 16, dl_step, 0, unroll=4)
    for a in range(2):
        dlt[:, a * 256:(a + 1) * 256] = jnp.transpose(dl[a])

    for k in range(4):
        qt[me, k] = jnp.transpose(stat[k * 128:(k + 1) * 128, :])[0:8, :]
    for i, (dx, dc) in enumerate(PEERS):
        send(qt.at[me], qt.at[me], qt_s.at[i], qt_r.at[i], at_x(dx, dc))

    def do_hg(k):
        g = jnp.dot(dlt[...], nm[zz(k)], preferred_element_type=F32)
        for b in range(4):
            ght[k, b] = g[:, b * 128:(b + 1) * 128]
        for j in range(3):
            sba[k, j] = ght[k, yy(DY[j]), 0:256, :].astype(BF16)
            send(sba.at[k, j], rba.at[k, j], ra_s.at[k, j], ra_r.at[k, j], at_y(DY[j]))

    def qrows(q):
        return slice(256 + q * 64, 320 + q * 64)

    def do_bc(s, d, q):
        k = (SZ[s] * d) % 8
        v = ght[k, :, qrows(q), :]
        if d < (4 if q % 2 == s else 3):
            got(rbb.at[s, q, d], rb_r.at[s, q, d])
            v = v + rbb[s, q, d].astype(F32)
        sbb[s, q, d - 1] = v.astype(BF16)
        send(sbb.at[s, q, d - 1], rbb.at[s, q, d - 1], rb_s.at[s, q, d - 1], rb_r.at[s, q, d - 1], at_z(SZ[s]))

    def a_sum(k):
        v = ght[k, y, 0:256, :]
        for j in range(3):
            got(rba.at[k, j], ra_r.at[k, j])
            v = v + rba[k, j].astype(F32)
        return v

    def do_a4():
        fa[...] = a_sum(4)
        for s in range(2):
            h = slice(s * 128, (s + 1) * 128)
            sa4[s] = fa[h, :].astype(BF16)
            send(sa4.at[s], ra4.at[s], rz_s.at[s, 3], rz_r.at[s, 3], at_z(SZ[s]))

    def do_ac(s, d):
        v = a_sum((SZ[s] * d) % 8)
        if d == 3:
            h = slice(s * 128, (s + 1) * 128)
            sa3[s] = v.astype(BF16)
            got(ra4.at[s], rz_r.at[s, 3])
            sa3[s, h] = (v[h] + ra4[s].astype(F32)).astype(BF16)
            send(sa3.at[s], ra3.at[s], rz_s.at[s, 2], rz_r.at[s, 2], at_z(SZ[s]))
            return
        if d == 2:
            got(ra3.at[s], rz_r.at[s, 2])
            sa2[s, 1] = v + ra3[s].astype(F32)
        else:
            got(ra2.at[s, 1], rz_r.at[s, 1])
            sa2[s, 0] = v + ra2[s, 1]
        send(sa2.at[s, d - 1], ra2.at[s, d - 1], rz_s.at[s, d - 1], rz_r.at[s, d - 1], at_z(SZ[s]))

    XO = (2, 1, 3, 0)

    def xdest(n):
        xs = (x + XO[n]) % 4
        return xs % 2, xs // 2

    def dn_part(out, n, cc):
        a, b = xdest(n)
        for i in range(4):
            h = hb[4 * cc + i, :, b].reshape(256, 512)
            out[n, :, i * 256:(i + 1) * 256] = lax.dot_general(
                dl[a], h, (((1,), (1,)), ((), ())), preferred_element_type=F32
            )

    def do_ds(n):
        dn_part(dns, n, 1 - c)
        send(dns.at[n], dnr.at[n], dc_s.at[n], dc_r.at[n], at_x(0, 1))
        dn_part(dno, n, c)

    def x_out(i):
        src = dno.at[1 + i, rows_of(i)]
        send(src, rbx.at[i], dx_s.at[i], dx_r.at[i], at_x((1, 3)[i]))

    def x_one(i):
        dos[i] = dno[1 + i, rows_of(1 - i), :].astype(BF16)
        send(dos.at[i], dor.at[1 - i], do_s.at[i], do_r.at[i], at_x((1, 3)[i]))

    def do_du(n):
        got(dnr.at[n], dc_r.at[n])
        a, b = xdest(n)
        tx = b * 2 + c

        def step(i, acc):
            rows = pl.ds(pl.multiple_of(i * 16, 16), 16)
            s_ = dno[n, rows, :] + dnr[n, rows, :]
            if n == 0:
                dxs[rows, :] = s_.astype(BF16)
            else:
                dno[n, rows, :] = s_
            xv = xg[a, tx, rows, :].astype(F32) * invb[a, rows, :][:, 0:1]
            pr = s_ * xv
            return acc + pr[0:8] + pr[8:16]
        acc = lax.fori_loop(0, 16, step, jnp.zeros((8, 1024), F32), unroll=2)
        gps[b * 2 + a] = jnp.sum(acc, axis=0, keepdims=True)
        if n == 0:
            for i in range(2):
                send(dxs.at[rows_of(i)], dxr.at[i], d2_s.at[i], d2_r.at[i], at_x((1, 3)[i]))
        elif n == 1:
            x_one(0)
        elif n == 2:
            x_one(1)

    def do_xr(n):
        i = n - 1
        got(dxr.at[i], d2_r.at[i])
        dno[n, rows_of(i), :] = dno[n, rows_of(i), :] + dxr[i].astype(F32)
        x_out(i)

    results = []

    def result(src, dst, i):
        cp = pltpu.make_async_copy(src, dst, out_s.at[i])
        cp.start()
        results.append(cp)

    def do_gy():
        for b in range(2):
            msg[b] = gps[2 * b] + gps[2 * b + 1]
        msg[2] = jnp.zeros((1, 1024), F32)
        msg[2, :, 0:128] = loss_row
        for j in range(3):
            send(msg, ary.at[j], gy_s.at[j], gy_r.at[j], at_y(DY[j]))

    def do_gz():
        for j in range(3):
            got(ary.at[j], gy_r.at[j])
        ary[3] = msg[...] + ary[0] + ary[1] + ary[2]
        for d in range(1, 8):
            send(ary.at[3], arz.at[d - 1], gz_s.at[d - 1], gz_r.at[d - 1], at_z(d))

    def do_gx():
        g = ary[3]
        for d in range(7):
            got(arz.at[d], gz_r.at[d])
            g = g + arz[d]
        gxs[...] = g
        for i, dx in enumerate((1, 3, 2)):
            b = ((x + dx) % 4) // 2
            send(gxs.at[b], gxr.at[i], gx_s.at[i], gx_r.at[i], at_x(dx))

    def total_inverse():
        tot = tsum2[...]
        for s in range(2):
            for d in range(ring_limit(s)):
                tot = tot + tot_z[s, d]
        return 1.0 / jnp.sum(jnp.sum(tot, axis=1, keepdims=True), axis=0, keepdims=True)

    def do_gf():
        for i in range(3):
            got(gxr.at[i], gx_r.at[i])
        o_gg[...] = (gxs[xh] + gxr[0] + gxr[1] + gxr[2]) * inv_total
        o_loss[...] = jnp.sum(gxs[2], axis=1, keepdims=True) * inv_total
        result(o_loss, r_loss, 0)
        result(o_gg, r_gg, 1)

    def do_qt():
        for i in range(7):
            got(qt.at[peer_was(i)], qt_r.at[i])
        qsum = qt[0]
        for i in range(1, 8):
            qsum = qsum + qt[i]
        for k in range(4):
            lseb[k * 128:(k + 1) * 128, :] = col(qsum[k, 0:1, :])

    PARTS = (slice(0, 256), slice(256, 384), slice(384, 512))

    def turn(i, v):
        ft = jnp.transpose(v)
        for a in range(2):
            ghs[a, :, PARTS[i]] = ft[a * 64:(a + 1) * 64]
        send(ghs.at[1 - xl, :, PARTS[i]], ghr.at[:, PARTS[i]], fx_s.at[i], fx_r.at[i], mate)

    def do_af():
        va = a_sum(0)
        for s in range(2):
            got(ra2.at[s, 0], rz_r.at[s, 0])
            va = va + ra2[s, 0]
        fa[...] = va
        turn(0, fa[...])

    def do_bf(q):
        v = ght[0, :, qrows(q), :]
        for s in range(2):
            got(rbb.at[s, q, 0], rb_r.at[s, q, 0])
            v = v + rbb[s, q, 0].astype(F32)
        syb[q] = v
        for j in range(3):
            src = syb.at[q, yy(DY[j])]
            send(src, ryb.at[q, j], ry_s.at[q, j], ry_r.at[q, j], at_y(DY[j]))

    def do_bg(p):
        for h in range(2):
            q = 2 * p + h
            v = syb[q, y]
            for j in range(3):
                got(ryb.at[q, j], ry_r.at[q, j])
                v = v + ryb[q, j]
            fb[p, h * 64:(h + 1) * 64, :] = v
        turn(1 + p, fb[p])

    def do_gh():
        o_gh[:, pl.ds(own, 512)] = ghs[xl] * inv_total
        for i in range(3):
            got(ghr.at[:, PARTS[i]], fx_r.at[i])
        o_gh[:, pl.ds(oth, 512)] = ghr[...] * inv_total
        result(o_gh, r_gh, 2)

    def do_fi():
        for i in range(2):
            got(rbx.at[i], dx_r.at[i])
            got(dor.at[1 - i], do_r.at[i])
        gt = gg4[t]

        def fin(i, carry):
            rows = pl.ds(pl.multiple_of(i * 16, 16), 16)
            qrow = pl.ds(pl.multiple_of(xl * 256 + i * 16, 16), 16)
            h = i // 8
            half_rows = pl.ds(pl.multiple_of((i % 8) * 16, 16), 16)
            dn = dno[3, rows, :] + rbx[h, half_rows, :] + dor[h, half_rows, :].astype(F32)
            inv = invb[xl, rows, :][:, 0:1]
            q = lseb[qrow, :][:, 0:1]
            xv = xg[xl, t, rows, :].astype(F32)
            u = inv * inv_total
            o_hid[rows, :] = (dn * gt * u - xv * (inv * u * q * (1.0 / D))).astype(BF16)
            return carry

        lax.fori_loop(0, 16, fin, 0, unroll=2)
        result(o_hid, r_hid, 3)

    steps = dict(
        ds=do_ds, hg=do_hg, bc=do_bc, du=do_du, a4=do_a4, ac=do_ac, xr=do_xr, gy=do_gy, gz=do_gz,
        gx=do_gx, gf=do_gf, qt=do_qt, tz=do_tz, af=do_af, bf=do_bf, bg=do_bg, gh=do_gh, fi=do_fi,
    )
    for name, *arg in SCATTER:
        steps[name](*arg)
        if name == "tz" and arg[0] == 4:
            inv_total = total_inverse()
    for cp in sent:
        cp.wait_send()
    for cp in results:
        cp.wait()


def finish(*refs):
    ins, outs, bufs, sem_in, sem_out = refs[0:4], refs[4:8], refs[8:12], refs[12], refs[13]
    first = [pltpu.make_async_copy(ins[i], bufs[i], sem_in.at[i]) for i in range(4)]
    second = [pltpu.make_async_copy(bufs[i], outs[i], sem_out.at[i]) for i in range(4)]
    for cp in first:
        cp.start()
    for one, two in zip(first, second):
        one.wait()
        two.start()
    for cp in second:
        cp.wait()


def body(hidden, gain, head, targets, row_weight):
    V = pltpu.VMEM
    S = pltpu.SemaphoreType.DMA
    hbm = pl.BlockSpec(memory_space=pl.ANY)
    scratch = [
        V((2, 128), jnp.int32),
        V((2, 128), jnp.int32),
        V((1, 1), F32),
        V((64, 1024), F32),
        V((1, 1024), F32),
        V((256, 1024), BF16),
        V((64, 1024), BF16),
        V((8, 4, 2, 64, 512), BF16),
        V((2, 4, 256, 1024), BF16),
        V((8, 512, 512), BF16),
        V((4, 1, 1024), F32),
        V((2, 8, 128), F32),
        V((2, 256, 128), F32),
        V((2, 256, 128), F32),
        V((2, 256, 128), F32),
        V((2, 256, 128), F32),
        V((512, 512), F32),
        V((512, 512), F32),
        V((2, 256, 512), BF16),
        V((512, 512), BF16),
        V((8, 4, 8, 128), F32),
        V((8, 4, 8, 128), F32),
        V((512, 128), F32),
        V((512, 128), F32),
        V((8, 4, 512, 128), F32),
        V((8, 3, 256, 128), BF16),
        V((8, 3, 256, 128), BF16),
        V((2, 128, 128), BF16),
        V((2, 128, 128), BF16),
        V((2, 256, 128), BF16),
        V((2, 256, 128), BF16),
        V((2, 2, 256, 128), F32),
        V((2, 2, 256, 128), F32),
        V((2, 4, 4, 4, 64, 128), BF16),
        V((2, 4, 4, 4, 64, 128), BF16),
        V((4, 4, 64, 128), F32),
        V((4, 3, 64, 128), F32),
        V((256, 128), F32),
        V((2, 128, 128), F32),
        V((2, 64, 512), F32),
        V((64, 512), F32),
        V((4, 256, 1024), F32),
        V((4, 256, 1024), F32),
        V((4, 256, 1024), F32),
        V((256, 1024), BF16),
        V((2, 128, 1024), BF16),
        V((2, 128, 1024), BF16),
        V((2, 128, 1024), BF16),
        V((2, 128, 1024), F32),
        V((4, 1, 1024), F32),
        V((3, 1, 1024), F32),
        V((3, 1, 1024), F32),
        V((3, 1, 1024), F32),
        V((4, 3, 1, 1024), F32),
        V((7, 3, 1, 1024), F32),
        V((8, 128), F32),
        V((8, 128), F32),
        V((3, 8, 128), F32),
        V((2, 4, 8, 128), F32),
        S((5,)),
        S((4,)),
    ]
    shapes = [
        (), (), (3,), (4,), (2,), (3,),
        (2, 4), (8, 3), (3,), (2, 4, 4),
        (7,), (7,), (3,), (2, 4),
        (8, 3), (2, 4), (2, 4, 4), (4, 3), (3,),
        (4,), (2,), (2,), (2,), (3,), (3,), (7,),
    ]
    for sh in shapes:
        scratch += [S(sh), S(sh)] if sh else [S, S]
    loss, gh, gg, gx = pl.pallas_call(
        kernel,
        out_shape=(
            jax.ShapeDtypeStruct((1, 1), F32),
            jax.ShapeDtypeStruct((64, 1024), F32),
            jax.ShapeDtypeStruct((1, 1024), F32),
            jax.ShapeDtypeStruct((256, 1024), BF16),
        ),
        in_specs=[hbm] * 5,
        out_specs=(hbm,) * 4,
        scratch_shapes=scratch,
        compiler_params=pltpu.CompilerParams(
            collective_id=0, has_side_effects=True, vmem_limit_bytes=62 << 20
        ),
    )(hidden, gain.reshape(1, 1024), head, targets.reshape(2, 128), row_weight.reshape(2, 128))
    loss, gh, gg, gx = pl.pallas_call(
        finish,
        out_shape=tuple(jax.ShapeDtypeStruct(a.shape, a.dtype) for a in (loss, gh, gg, gx)),
        in_specs=[hbm] * 4,
        out_specs=(hbm,) * 4,
        scratch_shapes=[V(a.shape, a.dtype) for a in (loss, gh, gg, gx)] + [S((4,)), S((4,))],
        compiler_params=pltpu.CompilerParams(vmem_limit_bytes=62 << 20),
    )(loss, gh, gg, gx)
    return (loss.reshape(()), gh, gg.reshape(1024), gx)


def solution(mesh):
    in_specs = (P("fsdp", "tp"), P("tp"), P("fsdp", "tp"), P("fsdp"), P("fsdp"))
    out_specs = (P(), P("fsdp", "tp"), P("tp"), P("fsdp", "tp"))
    return jax.shard_map(body, mesh=mesh, in_specs=in_specs, out_specs=out_specs, check_vma=False)
```

```python
import functools

import jax
import jax.numpy as jnp
from jax import lax
from jax.experimental import pallas as pl
from jax.experimental.pallas import tpu as pltpu
from jax.sharding import PartitionSpec as P

D = 4096
EPS = 1e-05
MESH = pl.DeviceIdType.MESH
F32 = jnp.float32
BF16 = jnp.bfloat16

DY = (1, 3, 2)
SZ = (1, 7)
PEERS = ((1, 0), (3, 0), (2, 0), (0, 1), (1, 1), (3, 1), (2, 1))
GATHER = (
    ("xe",), ("by", 1), ("bz", 0, 1, 0), ("bz", 1, 1, 0), ("by", 2), ("az", 0, 1), ("az", 1, 1), ("xo",),
    ("bz", 0, 1, 1), ("bz", 1, 1, 1), ("bz", 0, 2, 0), ("bz", 1, 2, 0), ("xf", 1), ("xf", 0), ("by", 3),
    ("az", 0, 2), ("az", 1, 2), ("xs", 1), ("xs", 0), ("ty",), ("bz", 0, 1, 2), ("bz", 1, 1, 2), ("iv", 1),
    ("nm", 1, 0), ("nm", 1, 1), ("nm", 1, 2), ("nm", 1, 3), ("bz", 0, 2, 1), ("bz", 1, 2, 1), ("nm", 1, 4),
    ("nm", 1, 5), ("nm", 1, 6), ("nm", 1, 7), ("bz", 0, 3, 0), ("bz", 1, 3, 0), ("az", 0, 3), ("az", 1, 3),
    ("bz", 0, 1, 3), ("bz", 1, 1, 3), ("bz", 0, 2, 2), ("bz", 1, 2, 2), ("xf", 2), ("bz", 0, 3, 1), ("bz", 1, 3, 1),
    ("tz", 1), ("xs", 2), ("iv", 0), ("nm", 0, 0), ("nm", 0, 1), ("nm", 0, 2), ("bz", 0, 4, 0), ("bz", 1, 2, 3),
    ("nm", 0, 3), ("nm", 0, 4), ("nm", 0, 5), ("az", 0, 4), ("bz", 1, 3, 2), ("nm", 0, 6), ("nm", 0, 7), ("lg", 0),
    ("bz", 0, 2, 3), ("bz", 1, 3, 3), ("lg", 7), ("lg", 1), ("bz", 0, 3, 2), ("bz", 1, 4, 2), ("lg", 6), ("tz", 2),
    ("lg", 2), ("bz", 0, 4, 1), ("lg", 3), ("bz", 0, 3, 3), ("bz", 1, 4, 3), ("lg", 5), ("lg", 4),
)
SCATTER = (
    ("hg", 4), ("bc", 0, 4, 0), ("bc", 1, 4, 1), ("bc", 0, 4, 2), ("bc", 1, 4, 3), ("hg", 3), ("bc", 0, 3, 1),
    ("bc", 0, 3, 3), ("hg", 5), ("bc", 1, 3, 0), ("bc", 1, 3, 2), ("ds", 0), ("hg", 2), ("ds", 1), ("du", 0),
    ("bc", 0, 3, 0), ("bc", 1, 3, 1), ("ds", 2), ("bc", 0, 3, 2), ("bc", 1, 3, 3), ("hg", 6), ("a4",), ("du", 1),
    ("bc", 0, 2, 1), ("bc", 1, 2, 0), ("ds", 3), ("du", 2), ("bc", 0, 2, 3), ("bc", 1, 2, 2), ("du", 3), ("gx",),
    ("hg", 1), ("bc", 0, 2, 0), ("bc", 1, 2, 1), ("hg", 7), ("hg", 0), ("xr", 1), ("xr", 2), ("ac", 0, 3),
    ("ac", 1, 3), ("bc", 0, 2, 2), ("bc", 1, 2, 3), ("bc", 0, 1, 1), ("bc", 1, 1, 0), ("tz", 3), ("bc", 0, 1, 3),
    ("bc", 1, 1, 2), ("bc", 0, 1, 0), ("bc", 1, 1, 1), ("bc", 0, 1, 2), ("bc", 1, 1, 3), ("ac", 0, 2),
    ("ac", 1, 2), ("gy",), ("tz", 4), ("qt",), ("bf", 0), ("bf", 1), ("ac", 0, 1), ("ac", 1, 1), ("gz",), ("bf", 2),
    ("bf", 3), ("bg", 0), ("bg", 1), ("af",), ("fi",), ("gf",), ("gh",),
)


def kernel(
    hid, gain, hin_hbm, tgt_hbm, wgt_hbm,
    r_loss, r_gh, r_gg, r_hid,
    tgt, wgt, o_loss, o_gh, o_gg, o_hid, hin, hb, xg, nm, gg4, tw, ssq, invb, tgtb, wb, lg, ex, dl, dlt,
    st, qt, lseb, stat,
    ght, sba, rba, sa4, ra4, sa3, ra3, sa2, ra2, sbb, rbb, syb, ryb, fa, fb, ghs, ghr,
    dno, dns, dnr, dxs, dxr, dos, dor, rbx, gps, gxs, gxr, msg, ary, arz, tsum, tsum2, tot_y, tot_z,
    in_s, out_s, send_s,
    xh_r, tw_r, gn_r, hx_r, hh_r, hf_r, az_r, ay_r, by_r, bz_r, st_r, qt_r, ty_r, tz_r,
    ra_r, rz_r, rb_r, ry_r, fx_r, dc_r, d2_r, dx_r, do_r, gx_r, gy_r, gz_r,
):
    f = lax.axis_index("fsdp")
    t = lax.axis_index("tp")
    xl = f // 32
    z = (f // 4) % 8
    y = f % 4
    xh = t // 2
    c = t % 2
    x = xh * 2 + xl

    def dev(x_, y_, z_, c_):
        return (((x_ % 2) * 8 + z_) * 4 + y_, (x_ // 2) * 2 + c_)

    def at_x(dx, dc=0):
        return dev((x + dx) % 4, y, z, (c + dc) % 2)

    def at_y(dy):
        return dev(x, (y + dy) % 4, z, c)

    def at_z(dz):
        return dev(x, y, (z + dz) % 8, c)

    mate = dev(xh * 2 + (1 - xl), y, z, c)

    def yy(k):
        return (y + k) % 4

    def zz(k):
        return (z + k) % 8

    partners = [at_x(dx, dc) for dx, dc in PEERS] + [at_y(d) for d in DY] + [at_z(d) for d in SZ]
    barrier = pltpu.get_barrier_semaphore()
    for p in partners:
        pl.semaphore_signal(barrier, inc=1, device_id=p, device_id_type=MESH)
    in_hid = pltpu.make_async_copy(hid, xg.at[xl, t], in_s.at[0])
    in_head = pltpu.make_async_copy(hin_hbm, hin, in_s.at[1])
    in_small = [
        pltpu.make_async_copy(src, dst, in_s.at[2 + i])
        for i, (src, dst) in enumerate(((tgt_hbm, tgt), (wgt_hbm, wgt), (gain, gg4.at[t])))
    ]
    in_head.start()
    in_hid.start()
    for cp in in_small:
        cp.start()
    oth = pl.multiple_of((1 - xl) * 512, 512)
    own = pl.multiple_of(xl * 512, 512)
    in_head.wait()
    hb[z, y, xl] = hin[:, pl.ds(own, 512)]
    pl.semaphore_wait(barrier, len(partners))

    sent = [0, 0, 0]
    GATHER_S, SEND_S, X_S = range(3)

    def rc(src, dst, ss, rs, to):
        return pltpu.make_async_remote_copy(
            src_ref=src, dst_ref=dst, send_sem=ss, recv_sem=rs, device_id=to, device_id_type=MESH
        )

    def send(src, dst, group, rs, to):
        rc(src, dst, send_s.at[group], rs, to).start()
        size = jnp.dtype(src.dtype).itemsize
        for n in src.shape:
            size *= n
        sent[group] += size

    def got(dst, rs):
        rc(dst, dst, rs, rs, at_y(1)).wait_recv()

    def b_hop(s, d, k):
        yk = y if k == 0 else ywas(k - 1)
        ref = hb.at[zz(-SZ[s] * d), yk, xl]
        send(ref, ref, GATHER_S, bz_r.at[s, d, k], at_z(SZ[s]))

    def a_hop(s, d):
        ref = hb.at[zz(-SZ[s] * d), y, 1 - xl]
        send(ref, ref, GATHER_S, az_r.at[s, d], at_z(SZ[s]))

    def a_out(k):
        ref = hb.at[zz(k), y, 1 - xl]
        for j in range(3):
            send(ref, ref, GATHER_S, ay_r.at[k], at_y(DY[j]))

    def ywas(j):
        return yy(-DY[j])

    def limit(s, k):
        if k < 0:
            return 4 if s == 0 else 3
        return 4 if (k < 2) == (s == 0) else 3

    def ring_limit(s):
        return 4 if s == 0 else 3

    send(hin.at[:, pl.ds(oth, 512)], hb.at[z, y, xl], GATHER_S, xh_r, mate)
    def b_out(j):
        ref = hb.at[z, y, xl]
        send(ref, ref, GATHER_S, by_r.at[j], at_y(DY[j]))

    b_out(0)
    b_out(1)
    for s in range(2):
        b_hop(s, 0, 0)
    for cp in in_small:
        cp.wait()
    tw[xl, 0:2, :] = tgt[...].astype(F32)
    tw[xl, 2:4, :] = wgt[...].astype(F32)
    send(tw.at[xl], tw.at[xl], GATHER_S, tw_r, mate)
    GP = ((0, 1), (2, 0), (2, 1))
    for i, (dx, dc) in enumerate(GP):
        send(gg4.at[t], gg4.at[t], GATHER_S, gn_r, at_x(dx, dc))
    in_hid.wait()
    for i, dx, dc in ((3, 0, 1), (0, 1, 0), (1, 3, 0)):
        send(xg.at[xl, t], xg.at[xl, t], GATHER_S, hx_r.at[i], at_x(dx, dc))

    def ssq_block(xl_, t_):
        def step(i, carry):
            rows = pl.ds(pl.multiple_of(i * 32, 32), 32)
            v = xg[xl_, t_, rows, :].astype(F32)
            v = v * v
            acc = v[:, 0:128]
            for k in range(1, 8):
                acc = acc + v[:, k * 128:(k + 1) * 128]
            ssq[xl_, rows, :] += acc
            return carry
        lax.fori_loop(0, 8, step, 0, unroll=4)

    def col(row):
        return jnp.transpose(jnp.broadcast_to(row, (128, 128)))

    ssq[...] = jnp.zeros_like(ssq)
    ssq_block(xl, t)

    def tokens():
        got(tw.at[1 - xl], tw_r)
        tsum[...] = jnp.zeros_like(tsum)
        tsum[0:2, :] = tw[0, 2:4, :] + tw[1, 2:4, :]
        for j in range(3):
            send(tsum, tot_y.at[j], SEND_S, ty_r, at_y(DY[j]))
        for a in range(2):
            for k in range(2):
                tgtb[a, k * 128:(k + 1) * 128, :] = col(tw[a, k:k + 1, :])
                wb[a, k * 128:(k + 1) * 128, :] = col(tw[a, 2 + k:3 + k, :])

    def t_hop(src, s, d):
        send(src, tot_z.at[s, d], SEND_S, tz_r.at[s, d], at_z(SZ[s]))

    def do_ty():
        got(tot_y, ty_r)
        tsum2[...] = tsum[...] + tot_y[0] + tot_y[1] + tot_y[2]
        for s in range(2):
            t_hop(tsum2, s, 0)

    def do_tz(d):
        for s in range(2):
            if d <= ring_limit(s):
                got(tot_z.at[s, d - 1], tz_r.at[s, d - 1])
                if d < ring_limit(s):
                    t_hop(tot_z.at[s, d - 1], s, d)

    def do_xe():
        got(hb.at[z, y, 1 - xl], xh_r)
        a_hop(0, 0)
        a_hop(1, 0)
        b_out(2)
        a_out(0)

    def do_by(k):
        got(hb.at[z, ywas(k - 1), xl], by_r.at[k - 1])
        for s in range(2):
            b_hop(s, 0, k)

    def do_az(s, d):
        got(hb.at[zz(-SZ[s] * d), y, 1 - xl], az_r.at[s, d - 1])
        if d < limit(s, -1):
            a_hop(s, d)
        a_out((-SZ[s] * d) % 8)

    def do_bz(s, d, k):
        yk = y if k == 0 else ywas(k - 1)
        got(hb.at[zz(-SZ[s] * d), yk, xl], bz_r.at[s, d - 1, k])
        if d < limit(s, k):
            b_hop(s, d, k)

    def rows_of(i):
        return slice(i * 128, (i + 1) * 128)

    XD = (1, 3, 2)

    def xblock(i):
        xs = (x - XD[i] + 4) % 4
        return xs % 2, (xs // 2) * 2

    def do_xf(i):
        a, b = xblock(i)
        ref = xg.at[a, b + c]
        if i < 2:
            got(ref, hx_r.at[i])
            part = xg.at[a, b + c, rows_of(i)]
            send(part, part, GATHER_S, hh_r.at[i], at_x((1, 3)[i]))
        else:
            for h in range(2):
                got(xg.at[a, b + c, rows_of(h)], hh_r.at[h])
        send(ref, ref, GATHER_S, hf_r.at[i], at_x(0, 1))
        ssq_block(a, b + c)

    def do_xs(i):
        a, b = xblock(i)
        got(xg.at[a, b + 1 - c], hf_r.at[i])
        ssq_block(a, b + 1 - c)

    def do_xo():
        got(xg.at[xl, xh * 2 + 1 - c], hx_r.at[3])
        ssq_block(xl, xh * 2 + 1 - c)
        got(gg4.at[0:3], gn_r)

    def half(h):
        return (xl + h) % 2

    def do_iv(h):
        a = half(h)
        s_ = jnp.sum(ssq[a], axis=1, keepdims=True)
        invb[a] = jnp.broadcast_to(lax.rsqrt(s_ * (1.0 / D) + EPS), (256, 128))

    def do_nm(h, zb):
        a = half(h)
        t0 = zb // 4
        off = (zb % 4) * 256

        def step(i, carry):
            rows = pl.ds(pl.multiple_of(i * 32, 32), 32)
            out = pl.ds(pl.multiple_of(a * 256 + i * 32, 32), 32)
            inv = invb[a, rows, :]
            low = lax.broadcasted_iota(jnp.int32, (32, 128), 1) < 64
            for p in range(2):
                cols = slice(off + p * 128, off + (p + 1) * 128)
                u = xg[a, t0, rows, cols].astype(F32) * inv * gg4[t0, :, cols]
                v = xg[a, t0 + 2, rows, cols].astype(F32) * inv * gg4[t0 + 2, :, cols]
                ur = pltpu.roll(u, 64, 1)
                vr = pltpu.roll(v, 64, 1)
                nm[zb, out, (2 * p) * 128:(2 * p + 1) * 128] = jnp.where(low, u, vr).astype(BF16)
                nm[zb, out, (2 * p + 1) * 128:(2 * p + 2) * 128] = jnp.where(low, ur, v).astype(BF16)
            return carry
        lax.fori_loop(0, 8, step, 0, unroll=4)

    def do_lg(k):
        got(hb.at[0:3, 0, 0], ay_r.at[k])
        part = jnp.dot(nm[zz(k)], hb[zz(k)].reshape(512, 512), preferred_element_type=F32)
        if k == 0:
            lg[...] = part
        else:
            lg[...] += part

    steps = dict(
        xe=do_xe, by=do_by, az=do_az, bz=do_bz, xf=do_xf, xs=do_xs, xo=do_xo,
        iv=do_iv, nm=do_nm, lg=do_lg, ty=do_ty, tz=do_tz,
    )
    tokens_done = False
    for name, *arg in GATHER:
        steps[name](*arg)
        if name == "by" and not tokens_done:
            tokens_done = True
            tokens()

    col0 = (t * 1024 + xl * 512).astype(F32)
    me = x * 2 + c

    def stat_step(i, carry):
        rows = pl.ds(pl.multiple_of(i * 32, 32), 32)
        l = lg[rows, :]
        m = jnp.max(l, axis=1, keepdims=True)
        ev = jnp.exp(l - m)
        ex[rows, :] = ev
        e = jnp.sum(ev, axis=1, keepdims=True)
        a = i // 8
        tb = tgtb[a, pl.ds(pl.multiple_of((i % 8) * 32, 32), 32), :][:, 0:1] - col0
        cols = lax.broadcasted_iota(jnp.int32, (32, 512), 1).astype(F32)
        pk = jnp.sum(jnp.where(cols == tb, l, 0.0), axis=1, keepdims=True)
        lane = lax.broadcasted_iota(jnp.int32, (32, 128), 1)
        stat[rows, :] = jnp.where(lane == 0, m, jnp.where(lane == 1, e, jnp.where(lane == 2, pk, 0.0)))
        return carry

    lax.fori_loop(0, 16, stat_step, 0, unroll=4)
    for k in range(4):
        st[me, k] = jnp.transpose(stat[k * 128:(k + 1) * 128, :])[0:8, :]
    for i, (dx, dc) in enumerate(PEERS):
        send(st.at[me], st.at[me], SEND_S, st_r, at_x(dx, dc))

    got(st.at[0:7], st_r)
    allst = st[...]
    mx = jnp.max(allst[:, :, 0:1, :], axis=0)
    es = jnp.sum(allst[:, :, 1:2, :] * jnp.exp(allst[:, :, 0:1, :] - mx[None]), axis=0)
    pk = jnp.sum(allst[:, :, 2:3, :], axis=0)
    lse = mx + jnp.log(es)
    loss_row = jnp.zeros((1, 128), F32)
    for k in range(4):
        loss_row = loss_row + tw[k // 2, 2 + k % 2:3 + k % 2, :] * (lse[k] - pk[k])
        lseb[k * 128:(k + 1) * 128, :] = col(lse[k])

    def dl_step(i, carry):
        a = i // 8
        rows = pl.ds(pl.multiple_of((i % 8) * 32, 32), 32)
        g = pl.ds(pl.multiple_of(i * 32, 32), 32)
        l = lg[g, :]
        tb = tgtb[a, rows, :][:, 0:1] - col0
        w = wb[a, rows, :][:, 0:1]
        cols = lax.broadcasted_iota(jnp.int32, (32, 512), 1).astype(F32)
        p = ex[g, :] * jnp.exp(stat[g, :][:, 0:1] - lseb[g, :][:, 0:1])
        d = (w * (p - jnp.where(cols == tb, 1.0, 0.0))).astype(BF16)
        dl[a, rows, :] = d
        q = jnp.sum(d.astype(F32) * l, axis=1, keepdims=True)
        stat[g, :] = jnp.broadcast_to(q, (32, 128))
        return carry

    lax.fori_loop(0, 16, dl_step, 0, unroll=4)
    for a in range(2):
        dlt[:, a * 256:(a + 1) * 256] = jnp.transpose(dl[a])

    for k in range(4):
        qt[me, k] = jnp.transpose(stat[k * 128:(k + 1) * 128, :])[0:8, :]
    for i, (dx, dc) in enumerate(PEERS):
        send(qt.at[me], qt.at[me], SEND_S, qt_r, at_x(dx, dc))

    def a_rows(k, b):
        return pl.ds(pl.multiple_of((k * 4 + b) * 512, 512), 256)

    def b_rows(k, q):
        return [ght[(k * 4 + b) * 512 + 256 + q * 64:(k * 4 + b) * 512 + 320 + q * 64, :] for b in range(4)]

    def do_hg(k):
        g = jnp.dot(dlt[...], nm[zz(k)], preferred_element_type=F32)
        for b in range(4):
            ght[(k * 4 + b) * 512:(k * 4 + b + 1) * 512, :] = g[:, b * 128:(b + 1) * 128]
        for j in range(3):
            sba[k, j] = ght[a_rows(k, yy(DY[j])), :].astype(BF16)
            send(sba.at[k, j], rba.at[k, j], SEND_S, ra_r.at[k], at_y(DY[j]))

    def do_bc(s, d, q):
        v = b_rows((SZ[s] * d) % 8, q)
        if d < (4 if q % 2 == s else 3):
            got(rbb.at[s, q, d], rb_r.at[s, q, d])
            v = [v[b] + rbb[s, q, d, b].astype(F32) for b in range(4)]
        for b in range(4):
            sbb[s, q, d - 1, b] = v[b].astype(BF16)
        send(sbb.at[s, q, d - 1], rbb.at[s, q, d - 1], SEND_S, rb_r.at[s, q, d - 1], at_z(SZ[s]))

    def a_sum(k):
        v = ght[a_rows(k, y), :]
        got(rba.at[k], ra_r.at[k])
        for j in range(3):
            v = v + rba[k, j].astype(F32)
        return v

    def do_a4():
        fa[...] = a_sum(4)
        for s in range(2):
            h = slice(s * 128, (s + 1) * 128)
            sa4[s] = fa[h, :].astype(BF16)
            send(sa4.at[s], ra4.at[s], SEND_S, rz_r.at[s, 3], at_z(SZ[s]))

    def do_ac(s, d):
        v = a_sum((SZ[s] * d) % 8)
        if d == 3:
            h = slice(s * 128, (s + 1) * 128)
            sa3[s] = v.astype(BF16)
            got(ra4.at[s], rz_r.at[s, 3])
            sa3[s, h] = (v[h] + ra4[s].astype(F32)).astype(BF16)
            send(sa3.at[s], ra3.at[s], SEND_S, rz_r.at[s, 2], at_z(SZ[s]))
            return
        if d == 2:
            got(ra3.at[s], rz_r.at[s, 2])
            sa2[s, 1] = v + ra3[s].astype(F32)
        else:
            got(ra2.at[s, 1], rz_r.at[s, 1])
            sa2[s, 0] = v + ra2[s, 1]
        send(sa2.at[s, d - 1], ra2.at[s, d - 1], SEND_S, rz_r.at[s, d - 1], at_z(SZ[s]))

    XO = (2, 1, 3, 0)

    def xdest(n):
        xs = (x + XO[n]) % 4
        return xs % 2, xs // 2

    def dn_part(out, n, cc):
        a, b = xdest(n)
        for i in range(4):
            h = hb[4 * cc + i, :, b].reshape(256, 512)
            out[n, :, i * 256:(i + 1) * 256] = lax.dot_general(
                dl[a], h, (((1,), (1,)), ((), ())), preferred_element_type=F32
            )

    def do_ds(n):
        dn_part(dns, n, 1 - c)
        send(dns.at[n], dnr.at[n], X_S, dc_r.at[n], at_x(0, 1))
        dn_part(dno, n, c)

    def x_out(i):
        src = dno.at[1 + i, rows_of(i)]
        send(src, rbx.at[i], X_S, dx_r.at[i], at_x((1, 3)[i]))

    def x_one(i):
        dos[i] = dno[1 + i, rows_of(1 - i), :].astype(BF16)
        send(dos.at[i], dor.at[1 - i], X_S, do_r.at[i], at_x((1, 3)[i]))

    def do_du(n):
        got(dnr.at[n], dc_r.at[n])
        a, b = xdest(n)
        tx = b * 2 + c

        def step(i, acc):
            rows = pl.ds(pl.multiple_of(i * 16, 16), 16)
            s_ = dno[n, rows, :] + dnr[n, rows, :]
            if n == 0:
                dxs[rows, :] = s_.astype(BF16)
            else:
                dno[n, rows, :] = s_
            xv = xg[a, tx, rows, :].astype(F32) * invb[a, rows, :][:, 0:1]
            pr = s_ * xv
            return acc + pr[0:8] + pr[8:16]
        acc = lax.fori_loop(0, 16, step, jnp.zeros((8, 1024), F32), unroll=2)
        gps[b * 2 + a] = jnp.sum(acc, axis=0, keepdims=True)
        if n == 0:
            for i in range(2):
                send(dxs.at[rows_of(i)], dxr.at[i], X_S, d2_r.at[i], at_x((1, 3)[i]))
        elif n == 1:
            x_one(0)
        elif n == 2:
            x_one(1)

    def do_xr(n):
        i = n - 1
        got(dxr.at[i], d2_r.at[i])
        dno[n, rows_of(i), :] = dno[n, rows_of(i), :] + dxr[i].astype(F32)
        x_out(i)

    results = []

    def result(src, dst, i):
        cp = pltpu.make_async_copy(src, dst, out_s.at[i])
        cp.start()
        results.append(cp)

    def do_gx():
        for b in range(2):
            gxs[b] = gps[2 * b] + gps[2 * b + 1]
        for i, dx in enumerate((1, 3, 2)):
            b = ((x + dx) % 4) // 2
            send(gxs.at[b], gxr.at[i], SEND_S, gx_r, at_x(dx))

    def do_gy():
        got(gxr, gx_r)
        msg[:, 0:1024] = gxs[xh] + gxr[0] + gxr[1] + gxr[2]
        msg[:, 1024:1152] = loss_row
        for j in range(3):
            send(msg, ary.at[j], SEND_S, gy_r, at_y(DY[j]))

    def do_gz():
        got(ary.at[0:3], gy_r)
        ary[3] = msg[...] + ary[0] + ary[1] + ary[2]
        for d in range(1, 8):
            send(ary.at[3], arz.at[d - 1], SEND_S, gz_r, at_z(d))

    def total_inverse():
        tot = tsum2[...]
        for s in range(2):
            for d in range(ring_limit(s)):
                tot = tot + tot_z[s, d]
        return 1.0 / jnp.sum(jnp.sum(tot, axis=1, keepdims=True), axis=0, keepdims=True)

    def do_gf():
        got(arz, gz_r)
        g = ary[3]
        for d in range(7):
            g = g + arz[d]
        o_gg[...] = g[:, 0:1024] * inv_total
        o_loss[...] = jnp.sum(g[:, 1024:1152], axis=1, keepdims=True) * inv_total
        result(o_loss, r_loss, 0)
        result(o_gg, r_gg, 1)

    def do_qt():
        got(qt.at[0:7], qt_r)
        qsum = qt[0]
        for i in range(1, 8):
            qsum = qsum + qt[i]
        for k in range(4):
            lseb[k * 128:(k + 1) * 128, :] = col(qsum[k, 0:1, :])

    PARTS = (slice(0, 256), slice(256, 384), slice(384, 512))

    def turn(i, v):
        ft = jnp.transpose(v)
        for a in range(2):
            ghs[a, :, PARTS[i]] = ft[a * 64:(a + 1) * 64]
        send(ghs.at[1 - xl, :, PARTS[i]], ghr.at[:, PARTS[i]], SEND_S, fx_r.at[i], mate)

    def do_af():
        va = a_sum(0)
        for s in range(2):
            got(ra2.at[s, 0], rz_r.at[s, 0])
            va = va + ra2[s, 0]
        fa[...] = va
        turn(0, fa[...])

    def do_bf(q):
        v = b_rows(0, q)
        for s in range(2):
            got(rbb.at[s, q, 0], rb_r.at[s, q, 0])
            v = [v[b] + rbb[s, q, 0, b].astype(F32) for b in range(4)]
        for b in range(4):
            syb[q, b] = v[b]
        for j in range(3):
            src = syb.at[q, yy(DY[j])]
            send(src, ryb.at[q, j], SEND_S, ry_r.at[q], at_y(DY[j]))

    def do_bg(p):
        for h in range(2):
            q = 2 * p + h
            v = syb[q, y]
            got(ryb.at[q], ry_r.at[q])
            for j in range(3):
                v = v + ryb[q, j]
            fb[p, h * 64:(h + 1) * 64, :] = v
        turn(1 + p, fb[p])

    def do_gh():
        o_gh[:, pl.ds(own, 512)] = ghs[xl] * inv_total
        for i in range(3):
            got(ghr.at[:, PARTS[i]], fx_r.at[i])
        o_gh[:, pl.ds(oth, 512)] = ghr[...] * inv_total
        result(o_gh, r_gh, 2)

    def do_fi():
        for i in range(2):
            got(rbx.at[i], dx_r.at[i])
            got(dor.at[1 - i], do_r.at[i])
        gt = gg4[t]

        def fin(i, carry):
            rows = pl.ds(pl.multiple_of(i * 16, 16), 16)
            qrow = pl.ds(pl.multiple_of(xl * 256 + i * 16, 16), 16)
            h = i // 8
            half_rows = pl.ds(pl.multiple_of((i % 8) * 16, 16), 16)
            dn = dno[3, rows, :] + rbx[h, half_rows, :] + dor[h, half_rows, :].astype(F32)
            inv = invb[xl, rows, :][:, 0:1]
            q = lseb[qrow, :][:, 0:1]
            xv = xg[xl, t, rows, :].astype(F32)
            u = inv * inv_total
            o_hid[rows, :] = (dn * gt * u - xv * (inv * u * q * (1.0 / D))).astype(BF16)
            return carry

        lax.fori_loop(0, 16, fin, 0, unroll=2)
        result(o_hid, r_hid, 3)

    steps = dict(
        ds=do_ds, hg=do_hg, bc=do_bc, du=do_du, a4=do_a4, ac=do_ac, xr=do_xr, gy=do_gy, gz=do_gz,
        gx=do_gx, gf=do_gf, qt=do_qt, tz=do_tz, af=do_af, bf=do_bf, bg=do_bg, gh=do_gh, fi=do_fi,
    )
    for name, *arg in SCATTER:
        steps[name](*arg)
        if name == "tz" and arg[0] == 4:
            inv_total = total_inverse()
    for group, size in enumerate(sent):
        whole = ght.at[pl.ds(0, size // 512)]
        rc(whole, whole, send_s.at[group], send_s.at[group], at_y(1)).wait_send()
    for cp in results:
        cp.wait()


def finish(*refs):
    copies = [pltpu.make_async_copy(refs[i], refs[4 + i], refs[8].at[i]) for i in range(4)]
    for cp in copies:
        cp.start()
    for cp in copies:
        cp.wait()


def body(hidden, gain, head, targets, row_weight):
    V = pltpu.VMEM
    S = pltpu.SemaphoreType.DMA
    hbm = pl.BlockSpec(memory_space=pl.ANY)
    scratch = [
        V((2, 128), jnp.int32),
        V((2, 128), jnp.int32),
        V((1, 1), F32),
        V((64, 1024), F32),
        V((1, 1024), F32),
        V((256, 1024), BF16),
        V((64, 1024), BF16),
        V((8, 4, 2, 64, 512), BF16),
        V((2, 4, 256, 1024), BF16),
        V((8, 512, 512), BF16),
        V((4, 1, 1024), F32),
        V((2, 8, 128), F32),
        V((2, 256, 128), F32),
        V((2, 256, 128), F32),
        V((2, 256, 128), F32),
        V((2, 256, 128), F32),
        V((512, 512), F32),
        V((512, 512), F32),
        V((2, 256, 512), BF16),
        V((512, 512), BF16),
        V((8, 4, 8, 128), F32),
        V((8, 4, 8, 128), F32),
        V((512, 128), F32),
        V((512, 128), F32),
        V((16384, 128), F32),
        V((8, 3, 256, 128), BF16),
        V((8, 3, 256, 128), BF16),
        V((2, 128, 128), BF16),
        V((2, 128, 128), BF16),
        V((2, 256, 128), BF16),
        V((2, 256, 128), BF16),
        V((2, 2, 256, 128), F32),
        V((2, 2, 256, 128), F32),
        V((2, 4, 4, 4, 64, 128), BF16),
        V((2, 4, 4, 4, 64, 128), BF16),
        V((4, 4, 64, 128), F32),
        V((4, 3, 64, 128), F32),
        V((256, 128), F32),
        V((2, 128, 128), F32),
        V((2, 64, 512), F32),
        V((64, 512), F32),
        V((4, 256, 1024), F32),
        V((4, 256, 1024), F32),
        V((4, 256, 1024), F32),
        V((256, 1024), BF16),
        V((2, 128, 1024), BF16),
        V((2, 128, 1024), BF16),
        V((2, 128, 1024), BF16),
        V((2, 128, 1024), F32),
        V((4, 1, 1024), F32),
        V((2, 1, 1024), F32),
        V((3, 1, 1024), F32),
        V((1, 1152), F32),
        V((4, 1, 1152), F32),
        V((7, 1, 1152), F32),
        V((8, 128), F32),
        V((8, 128), F32),
        V((3, 8, 128), F32),
        V((2, 4, 8, 128), F32),
        S((5,)),
        S((4,)),
        S((3,)),
    ]
    shapes = [
        (), (), (), (4,), (2,), (3,), (2, 4), (8,), (3,), (2, 4, 4),
        (), (), (), (2, 4), (8,), (2, 4), (2, 4, 4), (4,), (3,),
        (4,), (2,), (2,), (2,), (), (), (),
    ]
    scratch += [S(sh) if sh else S for sh in shapes]
    loss, gh, gg, gx = pl.pallas_call(
        kernel,
        out_shape=(
            jax.ShapeDtypeStruct((1, 1), F32),
            jax.ShapeDtypeStruct((64, 1024), F32),
            jax.ShapeDtypeStruct((1, 1024), F32),
            jax.ShapeDtypeStruct((256, 1024), BF16),
        ),
        in_specs=[pl.BlockSpec(memory_space=pltpu.HBM)] * 5,
        out_specs=(hbm,) * 4,
        scratch_shapes=scratch,
        compiler_params=pltpu.CompilerParams(
            collective_id=0, has_side_effects=True, vmem_limit_bytes=53 << 20
        ),
    )(*[
        pltpu.with_memory_space_constraint(a, pltpu.HBM)
        for a in (hidden, gain.reshape(1, 1024), head, targets.reshape(2, 128), row_weight.reshape(2, 128))
    ])
    loss, gh, gg, gx = pl.pallas_call(
        finish,
        out_shape=tuple(jax.ShapeDtypeStruct(a.shape, a.dtype) for a in (loss, gh, gg, gx)),
        in_specs=[hbm] * 4,
        out_specs=(hbm,) * 4,
        scratch_shapes=[S((4,))],
        compiler_params=pltpu.CompilerParams(vmem_limit_bytes=2 << 20),
    )(loss, gh, gg, gx)
    return (loss.reshape(()), gh, gg.reshape(1024), gx)


def solution(mesh):
    in_specs = (P("fsdp", "tp"), P("tp"), P("fsdp", "tp"), P("fsdp"), P("fsdp"))
    out_specs = (P(), P("fsdp", "tp"), P("tp"), P("fsdp", "tp"))
    return jax.shard_map(body, mesh=mesh, in_specs=in_specs, out_specs=out_specs, check_vma=False)
```

```python
import functools

import jax
import jax.numpy as jnp
from jax import lax
from jax.experimental import pallas as pl
from jax.experimental.pallas import tpu as pltpu
from jax.sharding import PartitionSpec as P

D = 4096
EPS = 1e-05
MESH = pl.DeviceIdType.MESH
F32 = jnp.float32
BF16 = jnp.bfloat16

DY = (1, 3, 2)
SZ = (1, 7)
PEERS = ((1, 0), (3, 0), (2, 0), (0, 1), (1, 1), (3, 1), (2, 1))
GATHER = (
    ("xe",), ("by", 1), ("bz", 0, 1, 0), ("bz", 1, 1, 0), ("az", 0, 1), ("az", 1, 1), ("by", 2), ("xo",),
    ("bz", 0, 1, 1), ("bz", 1, 1, 1), ("bz", 0, 2, 0), ("bz", 1, 2, 0), ("xf", 1), ("xf", 0),
    ("az", 0, 2), ("az", 1, 2), ("by", 3), ("xs", 1), ("xs", 0), ("ty",), ("bz", 0, 1, 2), ("bz", 1, 1, 2), ("iv", 1),
    ("nm", 1, 0), ("nm", 1, 1), ("nm", 1, 2), ("nm", 1, 3), ("bz", 0, 2, 1), ("bz", 1, 2, 1), ("nm", 1, 4),
    ("nm", 1, 5), ("nm", 1, 6), ("nm", 1, 7), ("bz", 0, 3, 0), ("bz", 1, 3, 0), ("az", 0, 3), ("az", 1, 3),
    ("bz", 0, 1, 3), ("bz", 1, 1, 3), ("bz", 0, 2, 2), ("bz", 1, 2, 2), ("xf", 2), ("bz", 0, 3, 1), ("bz", 1, 3, 1),
    ("tz", 1), ("xs", 2), ("iv", 0), ("nm", 0, 0), ("nm", 0, 1), ("nm", 0, 2), ("bz", 0, 4, 0), ("bz", 1, 2, 3),
    ("nm", 0, 3), ("nm", 0, 4), ("nm", 0, 5), ("az", 0, 4), ("bz", 1, 3, 2), ("nm", 0, 6), ("nm", 0, 7), ("lg", 0),
    ("bz", 0, 2, 3), ("bz", 1, 3, 3), ("lg", 7), ("lg", 1), ("bz", 0, 3, 2), ("bz", 1, 4, 2), ("lg", 6), ("tz", 2),
    ("lg", 2), ("bz", 0, 4, 1), ("lg", 3), ("bz", 0, 3, 3), ("bz", 1, 4, 3), ("lg", 5), ("lg", 4),
)
SCATTER = (
    ("hg", 4), ("ai", 4), ("bc", 0, 4, 0), ("bc", 1, 4, 1), ("hg", 3), ("ai", 3), ("bc", 0, 3, 1), ("ds", 0),
    ("hg", 5), ("ai", 5), ("bc", 1, 3, 0), ("bc", 0, 4, 2), ("bc", 1, 4, 2), ("ds", 1), ("du", 0), ("ds", 2),
    ("yr", 4), ("bc", 0, 3, 0), ("bc", 1, 3, 1), ("hg", 2), ("ai", 2), ("yr", 3), ("du", 1), ("bc", 0, 2, 1),
    ("hg", 6), ("ai", 6), ("yr", 5), ("bc", 1, 2, 0), ("bc", 0, 3, 2), ("bc", 1, 3, 2), ("ds", 3), ("du", 2),
    ("hg", 1), ("ai", 1), ("a4",), ("bc", 0, 2, 0), ("bc", 1, 2, 1), ("hg", 0), ("ai", 0), ("hg", 7), ("ai", 7),
    ("du", 3), ("yr", 2), ("gx",), ("qs",), ("bc", 0, 1, 1), ("bc", 1, 1, 0), ("bc", 0, 2, 2), ("bc", 1, 2, 2),
    ("xr", 1), ("xr", 2), ("yr", 6), ("ac", 0, 3), ("ac", 1, 3), ("bc", 0, 1, 0), ("bc", 1, 1, 1), ("yr", 1),
    ("yr", 7), ("yr", 0), ("tz", 3), ("ac", 0, 2), ("bc", 0, 1, 2), ("bc", 1, 1, 2), ("ac", 1, 2), ("qt",), ("gy",),
    ("bf", 0), ("bf", 1), ("tz", 4), ("bf", 2), ("al",), ("gz",), ("bg",), ("fi",), ("af", 0), ("af", 1), ("bm",),
    ("gf",), ("gh",),
)


def kernel(
    hid, gain, hin_hbm, tgt_hbm, wgt_hbm,
    r_loss, r_gh, r_gg, r_hid,
    tgt, wgt, o_loss, o_gh, o_gg, o_hid, hin, hb, xg, nm, gg4, tw, ssq, invb, tgtb, wb, lg, ex, dl, dlt,
    st, qt, lseb, stat, pick, lser,
    ght, sbf, rbf, sba, rba, sa4, ra4, sa3, ra3, sa2, ra2, sb4, rb4, sbb, rbb, syb, ryb, fa, fb, ghs, ghr,
    dno, dns, dnr, dxs, dxr, dos, dor, rbx, gps, gxs, gxr, msg, ary, arz, tsum, tsum2, tot_y, tot_z,
    in_s, out_s, send_s,
    xh_r, tw_r, gn_r, hx_r, hh_r, hf_r, az_r, ay_r, by_r, bz_r, st_r, qt_r, ty_r, tz_r,
    rf_r, ra_r, rz_r, rl_r, rb_r, ry_r, fx_r, dc_r, d2_r, dx_r, do_r, gx_r, gy_r, gz_r,
):
    f = lax.axis_index("fsdp")
    t = lax.axis_index("tp")
    xl = f // 32
    z = (f // 4) % 8
    y = f % 4
    xh = t // 2
    c = t % 2
    x = xh * 2 + xl

    def dev(x_, y_, z_, c_):
        return (((x_ % 2) * 8 + z_) * 4 + y_, (x_ // 2) * 2 + c_)

    def at_x(dx, dc=0):
        return dev((x + dx) % 4, y, z, (c + dc) % 2)

    def at_y(dy):
        return dev(x, (y + dy) % 4, z, c)

    def at_z(dz):
        return dev(x, y, (z + dz) % 8, c)

    mate = dev(xh * 2 + (1 - xl), y, z, c)

    def yy(k):
        return (y + k) % 4

    def zz(k):
        return (z + k) % 8

    partners = [at_x(dx, dc) for dx, dc in PEERS] + [at_y(d) for d in DY] + [at_z(d) for d in SZ]
    barrier = pltpu.get_barrier_semaphore()
    for p in partners:
        pl.semaphore_signal(barrier, inc=1, device_id=p, device_id_type=MESH)
    in_hid = pltpu.make_async_copy(hid, xg.at[xl, t], in_s.at[0])
    in_head = pltpu.make_async_copy(hin_hbm, hin, in_s.at[1])
    in_small = [
        pltpu.make_async_copy(src, dst, in_s.at[2 + i])
        for i, (src, dst) in enumerate(((tgt_hbm, tgt), (wgt_hbm, wgt), (gain, gg4.at[t])))
    ]
    in_head.start()
    in_hid.start()
    for cp in in_small:
        cp.start()
    oth = pl.multiple_of((1 - xl) * 512, 512)
    own = pl.multiple_of(xl * 512, 512)
    in_head.wait()
    hb[z, y, xl] = hin[:, pl.ds(own, 512)]
    pl.semaphore_wait(barrier, len(partners))

    sent = [0, 0, 0]
    GATHER_S, SEND_S, X_S = range(3)

    def rc(src, dst, ss, rs, to):
        return pltpu.make_async_remote_copy(
            src_ref=src, dst_ref=dst, send_sem=ss, recv_sem=rs, device_id=to, device_id_type=MESH
        )

    def send(src, dst, group, rs, to):
        rc(src, dst, send_s.at[group], rs, to).start()
        size = jnp.dtype(src.dtype).itemsize
        for n in src.shape:
            size *= n
        sent[group] += size

    def got(dst, rs):
        rc(dst, dst, rs, rs, at_y(1)).wait_recv()

    def b_hop(s, d, k):
        yk = y if k == 0 else ywas(k - 1)
        ref = hb.at[zz(-SZ[s] * d), yk, xl]
        send(ref, ref, GATHER_S, bz_r.at[s, d, k], at_z(SZ[s]))

    def a_hop(s, d):
        ref = hb.at[zz(-SZ[s] * d), y, 1 - xl]
        send(ref, ref, GATHER_S, az_r.at[s, d], at_z(SZ[s]))

    def a_out(k):
        ref = hb.at[zz(k), y, 1 - xl]
        for j in range(3):
            send(ref, ref, GATHER_S, ay_r.at[k], at_y(DY[j]))

    def ywas(j):
        return yy(-DY[j])

    def limit(s, k):
        if k < 0:
            return 4 if s == 0 else 3
        return 4 if (k < 2) == (s == 0) else 3

    def ring_limit(s):
        return 4 if s == 0 else 3

    send(hin.at[:, pl.ds(oth, 512)], hb.at[z, y, xl], GATHER_S, xh_r, mate)
    def b_out(j):
        ref = hb.at[z, y, xl]
        send(ref, ref, GATHER_S, by_r.at[j], at_y(DY[j]))

    b_out(0)
    b_out(1)
    for s in range(2):
        b_hop(s, 0, 0)
    for cp in in_small:
        cp.wait()
    tw[xl, 0:2, :] = tgt[...].astype(F32)
    tw[xl, 2:4, :] = wgt[...].astype(F32)
    send(tw.at[xl], tw.at[xl], GATHER_S, tw_r, mate)
    GP = ((0, 1), (2, 0), (2, 1))
    for i, (dx, dc) in enumerate(GP):
        send(gg4.at[t], gg4.at[t], GATHER_S, gn_r, at_x(dx, dc))
    in_hid.wait()
    for i, dx, dc in ((3, 0, 1), (0, 1, 0), (1, 3, 0)):
        send(xg.at[xl, t], xg.at[xl, t], GATHER_S, hx_r.at[i], at_x(dx, dc))

    def ssq_block(xl_, t_):
        def step(i, carry):
            rows = pl.ds(pl.multiple_of(i * 32, 32), 32)
            v = xg[xl_, t_, rows, :].astype(F32)
            v = v * v
            acc = v[:, 0:128]
            for k in range(1, 8):
                acc = acc + v[:, k * 128:(k + 1) * 128]
            ssq[xl_, rows, :] += acc
            return carry
        lax.fori_loop(0, 8, step, 0, unroll=4)

    def col(row):
        return jnp.transpose(jnp.broadcast_to(row, (128, 128)))

    ssq[...] = jnp.zeros_like(ssq)
    ssq_block(xl, t)

    def tokens():
        got(tw.at[1 - xl], tw_r)
        tsum[...] = jnp.zeros_like(tsum)
        tsum[0:2, :] = tw[0, 2:4, :] + tw[1, 2:4, :]
        for j in range(3):
            send(tsum, tot_y.at[j], SEND_S, ty_r, at_y(DY[j]))
        for a in range(2):
            for k in range(2):
                tgtb[a, k * 128:(k + 1) * 128, :] = col(tw[a, k:k + 1, :])
                wb[a, k * 128:(k + 1) * 128, :] = col(tw[a, 2 + k:3 + k, :])

    def t_hop(src, s, d):
        send(src, tot_z.at[s, d], SEND_S, tz_r.at[s, d], at_z(SZ[s]))

    def do_ty():
        got(tot_y, ty_r)
        tsum2[...] = tsum[...] + tot_y[0] + tot_y[1] + tot_y[2]
        for s in range(2):
            t_hop(tsum2, s, 0)

    def do_tz(d):
        for s in range(2):
            if d <= ring_limit(s):
                got(tot_z.at[s, d - 1], tz_r.at[s, d - 1])
                if d < ring_limit(s):
                    t_hop(tot_z.at[s, d - 1], s, d)

    def do_xe():
        got(hb.at[z, y, 1 - xl], xh_r)
        a_hop(0, 0)
        a_hop(1, 0)
        b_out(2)
        a_out(0)

    def do_by(k):
        got(hb.at[z, ywas(k - 1), xl], by_r.at[k - 1])
        for s in range(2):
            b_hop(s, 0, k)

    def do_az(s, d):
        got(hb.at[zz(-SZ[s] * d), y, 1 - xl], az_r.at[s, d - 1])
        if d < limit(s, -1):
            a_hop(s, d)
        a_out((-SZ[s] * d) % 8)

    def do_bz(s, d, k):
        yk = y if k == 0 else ywas(k - 1)
        got(hb.at[zz(-SZ[s] * d), yk, xl], bz_r.at[s, d - 1, k])
        if d < limit(s, k):
            b_hop(s, d, k)

    def rows_of(i):
        return slice(i * 128, (i + 1) * 128)

    XD = (1, 3, 2)

    def xblock(i):
        xs = (x - XD[i] + 4) % 4
        return xs % 2, (xs // 2) * 2

    def do_xf(i):
        a, b = xblock(i)
        ref = xg.at[a, b + c]
        if i < 2:
            got(ref, hx_r.at[i])
            part = xg.at[a, b + c, rows_of(i)]
            send(part, part, GATHER_S, hh_r.at[i], at_x((1, 3)[i]))
        else:
            for h in range(2):
                got(xg.at[a, b + c, rows_of(h)], hh_r.at[h])
        send(ref, ref, GATHER_S, hf_r.at[i], at_x(0, 1))
        ssq_block(a, b + c)

    def do_xs(i):
        a, b = xblock(i)
        got(xg.at[a, b + 1 - c], hf_r.at[i])
        ssq_block(a, b + 1 - c)

    def do_xo():
        got(xg.at[xl, xh * 2 + 1 - c], hx_r.at[3])
        ssq_block(xl, xh * 2 + 1 - c)
        got(gg4.at[0:3], gn_r)

    def half(h):
        return (xl + h) % 2

    def do_iv(h):
        a = half(h)
        s_ = jnp.sum(ssq[a], axis=1, keepdims=True)
        invb[a] = jnp.broadcast_to(lax.rsqrt(s_ * (1.0 / D) + EPS), (256, 128))

    def do_nm(h, zb):
        a = half(h)
        t0 = zb // 4
        off = (zb % 4) * 256

        def step(i, carry):
            rows = pl.ds(pl.multiple_of(i * 32, 32), 32)
            out = pl.ds(pl.multiple_of(a * 256 + i * 32, 32), 32)
            inv = invb[a, rows, :]
            low = lax.broadcasted_iota(jnp.int32, (32, 128), 1) < 64
            for p in range(2):
                cols = slice(off + p * 128, off + (p + 1) * 128)
                u = xg[a, t0, rows, cols].astype(F32) * inv * gg4[t0, :, cols]
                v = xg[a, t0 + 2, rows, cols].astype(F32) * inv * gg4[t0 + 2, :, cols]
                ur = pltpu.roll(u, 64, 1)
                vr = pltpu.roll(v, 64, 1)
                nm[zb, out, (2 * p) * 128:(2 * p + 1) * 128] = jnp.where(low, u, vr).astype(BF16)
                nm[zb, out, (2 * p + 1) * 128:(2 * p + 2) * 128] = jnp.where(low, ur, v).astype(BF16)
            return carry
        lax.fori_loop(0, 8, step, 0, unroll=4)

    def do_lg(k):
        got(hb.at[0:3, 0, 0], ay_r.at[k])
        part = jnp.dot(nm[zz(k)], hb[zz(k)].reshape(512, 512), preferred_element_type=F32)
        if k == 0:
            lg[...] = part
        else:
            lg[...] += part

    steps = dict(
        xe=do_xe, by=do_by, az=do_az, bz=do_bz, xf=do_xf, xs=do_xs, xo=do_xo,
        iv=do_iv, nm=do_nm, lg=do_lg, ty=do_ty, tz=do_tz,
    )
    tokens_done = False
    for name, *arg in GATHER:
        steps[name](*arg)
        if name == "by" and not tokens_done:
            tokens_done = True
            tokens()

    col0 = (t * 1024 + xl * 512).astype(F32)
    me = x * 2 + c

    def stat_step(i, carry):
        rows = pl.ds(pl.multiple_of(i * 32, 32), 32)
        l = lg[rows, :]
        m = jnp.max(l, axis=1, keepdims=True)
        ev = jnp.exp(l - m)
        ex[rows, :] = ev
        e = jnp.sum(ev, axis=1, keepdims=True)
        lane = lax.broadcasted_iota(jnp.int32, (32, 128), 1)
        stat[rows, :] = jnp.where(lane == 0, m, jnp.where(lane == 1, e, 0.0))
        return carry

    lax.fori_loop(0, 16, stat_step, 0, unroll=4)
    for k in range(4):
        st[me, k] = jnp.transpose(stat[k * 128:(k + 1) * 128, :])[0:8, :]
    for i, (dx, dc) in enumerate(PEERS):
        send(st.at[me], st.at[me], SEND_S, st_r, at_x(dx, dc))

    def pick_step(i, carry):
        rows = pl.ds(pl.multiple_of(i * 32, 32), 32)
        a = i // 8
        tb = tgtb[a, pl.ds(pl.multiple_of((i % 8) * 32, 32), 32), :][:, 0:1] - col0
        cols = lax.broadcasted_iota(jnp.int32, (32, 512), 1).astype(F32)
        pk = jnp.sum(jnp.where(cols == tb, lg[rows, :], 0.0), axis=1, keepdims=True)
        pick[rows, :] = jnp.broadcast_to(pk, (32, 128))
        return carry

    lax.fori_loop(0, 16, pick_step, 0, unroll=4)
    got(st.at[0:7], st_r)
    allst = st[...]
    mx = jnp.max(allst[:, :, 0:1, :], axis=0)
    es = jnp.sum(allst[:, :, 1:2, :] * jnp.exp(allst[:, :, 0:1, :] - mx[None]), axis=0)
    lse = mx + jnp.log(es)
    lser[...] = lse
    for k in range(4):
        lseb[k * 128:(k + 1) * 128, :] = col(lse[k])

    def dl_step(i, carry):
        a = i // 8
        rows = pl.ds(pl.multiple_of((i % 8) * 32, 32), 32)
        g = pl.ds(pl.multiple_of(i * 32, 32), 32)
        tb = tgtb[a, rows, :][:, 0:1] - col0
        w = wb[a, rows, :][:, 0:1]
        cols = lax.broadcasted_iota(jnp.int32, (32, 512), 1).astype(F32)
        p = ex[g, :] * jnp.exp(stat[g, :][:, 0:1] - lseb[g, :][:, 0:1])
        d = (w * (p - jnp.where(cols == tb, 1.0, 0.0))).astype(BF16)
        dl[a, rows, :] = d
        return carry

    lax.fori_loop(0, 16, dl_step, 0, unroll=4)
    for a in range(2):
        dlt[:, a * 256:(a + 1) * 256] = jnp.transpose(dl[a])

    def do_qs():
        def step(i, carry):
            a = i // 8
            g = pl.ds(pl.multiple_of(i * 32, 32), 32)
            d = dl[a, pl.ds(pl.multiple_of((i % 8) * 32, 32), 32), :]
            q = jnp.sum(d.astype(F32) * lg[g, :], axis=1, keepdims=True)
            lane = lax.broadcasted_iota(jnp.int32, (32, 128), 1)
            stat[g, :] = jnp.where(lane == 0, q, pick[g, :])
            return carry
        lax.fori_loop(0, 16, step, 0, unroll=4)
        for k in range(4):
            qt[me, k] = jnp.transpose(stat[k * 128:(k + 1) * 128, :])[0:8, :]
        for i, (dx, dc) in enumerate(PEERS):
            send(qt.at[me], qt.at[me], SEND_S, qt_r, at_x(dx, dc))

    def a_rows(k, b, h):
        return pl.ds(pl.multiple_of((k * 4 + b) * 512 + h * 160, 32), 160)

    Q_AT = (384, 448, 320)

    def b_rows(k, q):
        first = Q_AT[q]
        return [ght[(k * 4 + b) * 512 + first:(k * 4 + b) * 512 + first + 64, :] for b in range(4)]

    def do_hg(k):
        g = jnp.dot(dlt[...], nm[zz(k)], preferred_element_type=F32)
        for b in range(4):
            ght[(k * 4 + b) * 512:(k * 4 + b + 1) * 512, :] = g[:, b * 128:(b + 1) * 128]
        for i in range(2):
            sbf[k, i] = ght[a_rows(k, yy(2), i), :].astype(BF16)
            send(sbf.at[k, i], rbf.at[k, i], SEND_S, rf_r.at[k], at_y(DY[i]))

    def do_ai(k):
        for i in range(2):
            sba[k, i, 1 - i] = ght[a_rows(k, yy(DY[i]), 1 - i), :].astype(BF16)
            send(sba.at[k, i, 1 - i], rba.at[k, i, 1 - i], SEND_S, ra_r.at[k, 0], at_y(DY[i]))

    def do_yr(k):
        got(rbf.at[k], rf_r.at[k])
        for i in range(2):
            sba[k, i, i] = (ght[a_rows(k, yy(DY[i]), i), :] + rbf[k, i].astype(F32)).astype(BF16)
            send(sba.at[k, i, i], rba.at[k, i, i], SEND_S, ra_r.at[k, 1], at_y(DY[i]))

    def do_bc(s, d, q):
        v = b_rows((SZ[s] * d) % 8, q)
        h = slice(s * 32, (s + 1) * 32)
        if q == 2 and d == 4:
            for b in range(4):
                sb4[s, b] = v[b][h].astype(BF16)
            send(sb4.at[s], rb4.at[s], SEND_S, rb_r.at[s, q, 3], at_z(SZ[s]))
            return
        if q == 2 and d == 3:
            got(rb4.at[s], rb_r.at[s, q, 3])
            for b in range(4):
                sbb[s, q, 2, b] = v[b].astype(BF16)
                sbb[s, q, 2, b, h] = (v[b][h] + rb4[s, b].astype(F32)).astype(BF16)
        else:
            if d < (4 if q == s else 3):
                got(rbb.at[s, q, d], rb_r.at[s, q, d])
                v = [v[b] + rbb[s, q, d, b].astype(F32) for b in range(4)]
            for b in range(4):
                sbb[s, q, d - 1, b] = v[b].astype(BF16)
        send(sbb.at[s, q, d - 1], rbb.at[s, q, d - 1], SEND_S, rb_r.at[s, q, d - 1], at_z(SZ[s]))

    def a_sum(k):
        for i in range(2):
            got(rba.at[k, 0], ra_r.at[k, i])
        return [
            ght[a_rows(k, y, h), :] + rba[k, 0, h].astype(F32) + rba[k, 1, h].astype(F32) for h in range(2)
        ]

    def do_a4():
        v = a_sum(4)
        for s in range(2):
            sa4[s] = v[s].astype(BF16)
            send(sa4.at[s], ra4.at[s], SEND_S, rz_r.at[s, 3], at_z(SZ[s]))

    def do_ac(s, d):
        v = a_sum((SZ[s] * d) % 8)
        if d == 3:
            got(ra4.at[s], rz_r.at[s, 3])
            v[s] = v[s] + ra4[s].astype(F32)
            for h in range(2):
                sa3[s, h] = v[h].astype(BF16)
            send(sa3.at[s], ra3.at[s], SEND_S, rz_r.at[s, 2], at_z(SZ[s]))
            return
        got(ra3.at[s], rz_r.at[s, 2])
        for h in range(2):
            sa2[s, 1, h] = v[h] + ra3[s, h].astype(F32)
        send(sa2.at[s, 1], ra2.at[s, 1], SEND_S, rz_r.at[s, 1], at_z(SZ[s]))

    def do_al():
        for s in range(2):
            got(ra2.at[s, 1], rz_r.at[s, 1])
        v = [a_sum(SZ[s]) for s in range(2)]
        for h in range(2):
            for s in range(2):
                sa2[s, 0, h] = v[s][h] + ra2[s, 1, h]
                send(sa2.at[s, 0, h], ra2.at[s, 0, h], SEND_S, rl_r.at[s, h], at_z(SZ[s]))

    XO = (2, 1, 3, 0)

    def xdest(n):
        xs = (x + XO[n]) % 4
        return xs % 2, xs // 2

    def dn_part(out, n, cc):
        a, b = xdest(n)
        for i in range(4):
            h = hb[4 * cc + i, :, b].reshape(256, 512)
            out[n, :, i * 256:(i + 1) * 256] = lax.dot_general(
                dl[a], h, (((1,), (1,)), ((), ())), preferred_element_type=F32
            )

    def do_ds(n):
        dn_part(dns, n, 1 - c)
        send(dns.at[n], dnr.at[n], X_S, dc_r.at[n], at_x(0, 1))
        dn_part(dno, n, c)

    def x_out(i):
        src = dno.at[1 + i, rows_of(i)]
        send(src, rbx.at[i], X_S, dx_r.at[i], at_x((1, 3)[i]))

    def x_one(i):
        dos[i] = dno[1 + i, rows_of(1 - i), :].astype(BF16)
        send(dos.at[i], dor.at[1 - i], X_S, do_r.at[i], at_x((1, 3)[i]))

    def do_du(n):
        got(dnr.at[n], dc_r.at[n])
        a, b = xdest(n)
        tx = b * 2 + c

        def step(i, acc):
            rows = pl.ds(pl.multiple_of(i * 16, 16), 16)
            s_ = dno[n, rows, :] + dnr[n, rows, :]
            if n == 0:
                dxs[rows, :] = s_.astype(BF16)
            else:
                dno[n, rows, :] = s_
            xv = xg[a, tx, rows, :].astype(F32) * invb[a, rows, :][:, 0:1]
            pr = s_ * xv
            return acc + pr[0:8] + pr[8:16]
        acc = lax.fori_loop(0, 16, step, jnp.zeros((8, 1024), F32), unroll=2)
        gps[b * 2 + a] = jnp.sum(acc, axis=0, keepdims=True)
        if n == 0:
            for i in range(2):
                send(dxs.at[rows_of(i)], dxr.at[i], X_S, d2_r.at[i], at_x((1, 3)[i]))
        elif n == 1:
            x_one(0)
        elif n == 2:
            x_one(1)

    def do_xr(n):
        i = n - 1
        got(dxr.at[i], d2_r.at[i])
        dno[n, rows_of(i), :] = dno[n, rows_of(i), :] + dxr[i].astype(F32)
        x_out(i)

    results = []

    def result(src, dst, i):
        cp = pltpu.make_async_copy(src, dst, out_s.at[i])
        cp.start()
        results.append(cp)

    def do_gx():
        for b in range(2):
            gxs[b] = gps[2 * b] + gps[2 * b + 1]
        for i, dx in enumerate((1, 3, 2)):
            b = ((x + dx) % 4) // 2
            send(gxs.at[b], gxr.at[i], SEND_S, gx_r, at_x(dx))

    def do_gy():
        got(gxr, gx_r)
        msg[:, 0:1024] = gxs[xh] + gxr[0] + gxr[1] + gxr[2]
        for j in range(3):
            send(msg, ary.at[j], SEND_S, gy_r, at_y(DY[j]))

    def do_gz():
        got(ary.at[0:3], gy_r)
        ary[3] = msg[...] + ary[0] + ary[1] + ary[2]
        for d in range(1, 8):
            send(ary.at[3], arz.at[d - 1], SEND_S, gz_r, at_z(d))

    def total_inverse():
        tot = tsum2[...]
        for s in range(2):
            for d in range(ring_limit(s)):
                tot = tot + tot_z[s, d]
        return 1.0 / jnp.sum(jnp.sum(tot, axis=1, keepdims=True), axis=0, keepdims=True)

    def do_gf():
        got(arz, gz_r)
        g = ary[3]
        for d in range(7):
            g = g + arz[d]
        o_gg[...] = g[:, 0:1024] * inv_total
        o_loss[...] = jnp.sum(g[:, 1024:1152], axis=1, keepdims=True) * inv_total
        result(o_loss, r_loss, 0)
        result(o_gg, r_gg, 1)

    def do_qt():
        got(qt.at[0:7], qt_r)
        qsum = qt[0]
        for i in range(1, 8):
            qsum = qsum + qt[i]
        loss_row = jnp.zeros((1, 128), F32)
        for k in range(4):
            loss_row = loss_row + tw[k // 2, 2 + k % 2:3 + k % 2, :] * (lser[k] - qsum[k, 1:2, :])
            lseb[k * 128:(k + 1) * 128, :] = col(qsum[k, 0:1, :])
        msg[:, 1024:1152] = loss_row

    PARTS = tuple(slice(i * 128, (i + 1) * 128) for i in range(4))

    def turn(i, v):
        ft = jnp.transpose(v)
        for a in range(2):
            ghs[a, :, PARTS[i]] = ft[a * 64:(a + 1) * 64]
        send(ghs.at[1 - xl, :, PARTS[i]], ghr.at[:, PARTS[i]], SEND_S, fx_r.at[i], mate)

    def do_af(h):
        if h == 0:
            for i in range(2):
                got(rba.at[0, 0], ra_r.at[0, i])
        v = ght[a_rows(0, y, h), :] + rba[0, 0, h].astype(F32) + rba[0, 1, h].astype(F32)
        for s in range(2):
            got(ra2.at[s, 0, h], rl_r.at[s, h])
            v = v + ra2[s, 0, h]
        fa[h * 160:(h + 1) * 160, :] = v
        turn(h, fa[h * 128:(h + 1) * 128, :])

    def do_bf(q):
        v = b_rows(0, q)
        for s in range(2):
            got(rbb.at[s, q, 0], rb_r.at[s, q, 0])
            v = [v[b] + rbb[s, q, 0, b].astype(F32) for b in range(4)]
        for b in range(4):
            syb[q, b] = v[b]
        for j in range(3):
            src = syb.at[q, yy(DY[j])]
            send(src, ryb.at[q, j], SEND_S, ry_r.at[q], at_y(DY[j]))

    def b_sum(q):
        v = syb[q, y]
        got(ryb.at[q], ry_r.at[q])
        for j in range(3):
            v = v + ryb[q, j]
        return v

    def do_bg():
        for q in range(2):
            fb[q * 64:(q + 1) * 64, :] = b_sum(q)
        turn(3, fb[...])

    def do_bm():
        fa[320:384, :] = b_sum(2)
        turn(2, fa[256:384, :])

    def do_gh():
        o_gh[:, pl.ds(own, 512)] = ghs[xl] * inv_total
        for i in range(4):
            got(ghr.at[:, PARTS[i]], fx_r.at[i])
        o_gh[:, pl.ds(oth, 512)] = ghr[...] * inv_total
        result(o_gh, r_gh, 2)

    def do_fi():
        for i in range(2):
            got(rbx.at[i], dx_r.at[i])
            got(dor.at[1 - i], do_r.at[i])
        gt = gg4[t]

        def fin(i, carry):
            rows = pl.ds(pl.multiple_of(i * 16, 16), 16)
            qrow = pl.ds(pl.multiple_of(xl * 256 + i * 16, 16), 16)
            h = i // 8
            half_rows = pl.ds(pl.multiple_of((i % 8) * 16, 16), 16)
            dn = dno[3, rows, :] + rbx[h, half_rows, :] + dor[h, half_rows, :].astype(F32)
            inv = invb[xl, rows, :][:, 0:1]
            q = lseb[qrow, :][:, 0:1]
            xv = xg[xl, t, rows, :].astype(F32)
            u = inv * inv_total
            o_hid[rows, :] = (dn * gt * u - xv * (inv * u * q * (1.0 / D))).astype(BF16)
            return carry

        lax.fori_loop(0, 16, fin, 0, unroll=2)
        result(o_hid, r_hid, 3)

    steps = dict(
        ds=do_ds, hg=do_hg, bc=do_bc, du=do_du, a4=do_a4, ac=do_ac, xr=do_xr, gy=do_gy, gz=do_gz,
        gx=do_gx, gf=do_gf, qs=do_qs, qt=do_qt, tz=do_tz, yr=do_yr, ai=do_ai, al=do_al, af=do_af, bf=do_bf, bg=do_bg, bm=do_bm, gh=do_gh, fi=do_fi,
    )
    for name, *arg in SCATTER:
        steps[name](*arg)
        if name == "tz" and arg[0] == 4:
            inv_total = total_inverse()
    for group, size in enumerate(sent):
        whole = ght.at[pl.ds(0, size // 512)]
        rc(whole, whole, send_s.at[group], send_s.at[group], at_y(1)).wait_send()
    for cp in results:
        cp.wait()


def finish(*refs):
    copies = [pltpu.make_async_copy(refs[i], refs[4 + i], refs[8].at[i]) for i in range(4)]
    for cp in copies:
        cp.start()
    for cp in copies:
        cp.wait()


def body(hidden, gain, head, targets, row_weight):
    V = pltpu.VMEM
    S = pltpu.SemaphoreType.DMA
    hbm = pl.BlockSpec(memory_space=pl.ANY)
    scratch = [
        V((2, 128), jnp.int32),
        V((2, 128), jnp.int32),
        V((1, 1), F32),
        V((64, 1024), F32),
        V((1, 1024), F32),
        V((256, 1024), BF16),
        V((64, 1024), BF16),
        V((8, 4, 2, 64, 512), BF16),
        V((2, 4, 256, 1024), BF16),
        V((8, 512, 512), BF16),
        V((4, 1, 1024), F32),
        V((2, 8, 128), F32),
        V((2, 256, 128), F32),
        V((2, 256, 128), F32),
        V((2, 256, 128), F32),
        V((2, 256, 128), F32),
        V((512, 512), F32),
        V((512, 512), F32),
        V((2, 256, 512), BF16),
        V((512, 512), BF16),
        V((8, 4, 8, 128), F32),
        V((8, 4, 8, 128), F32),
        V((512, 128), F32),
        V((512, 128), F32),
        V((512, 128), F32),
        V((4, 1, 128), F32),
        V((16384, 128), F32),
        V((8, 2, 160, 128), BF16),
        V((8, 2, 160, 128), BF16),
        V((8, 2, 2, 160, 128), BF16),
        V((8, 2, 2, 160, 128), BF16),
        V((2, 160, 128), BF16),
        V((2, 160, 128), BF16),
        V((2, 2, 160, 128), BF16),
        V((2, 2, 160, 128), BF16),
        V((2, 2, 2, 160, 128), F32),
        V((2, 2, 2, 160, 128), F32),
        V((2, 4, 32, 128), BF16),
        V((2, 4, 32, 128), BF16),
        V((2, 3, 4, 4, 64, 128), BF16),
        V((2, 3, 4, 4, 64, 128), BF16),
        V((3, 4, 64, 128), F32),
        V((3, 3, 64, 128), F32),
        V((384, 128), F32),
        V((128, 128), F32),
        V((2, 64, 512), F32),
        V((64, 512), F32),
        V((4, 256, 1024), F32),
        V((4, 256, 1024), F32),
        V((4, 256, 1024), F32),
        V((256, 1024), BF16),
        V((2, 128, 1024), BF16),
        V((2, 128, 1024), BF16),
        V((2, 128, 1024), BF16),
        V((2, 128, 1024), F32),
        V((4, 1, 1024), F32),
        V((2, 1, 1024), F32),
        V((3, 1, 1024), F32),
        V((1, 1152), F32),
        V((4, 1, 1152), F32),
        V((7, 1, 1152), F32),
        V((8, 128), F32),
        V((8, 128), F32),
        V((3, 8, 128), F32),
        V((2, 4, 8, 128), F32),
        S((5,)),
        S((4,)),
        S((3,)),
    ]
    shapes = [
        (), (), (), (4,), (2,), (3,), (2, 4), (8,), (3,), (2, 4, 4),
        (), (), (), (2, 4), (8,), (8, 2), (2, 4), (2, 2), (2, 3, 4), (3,), (4,),
        (4,), (2,), (2,), (2,), (), (), (),
    ]
    scratch += [S(sh) if sh else S for sh in shapes]
    loss, gh, gg, gx = pl.pallas_call(
        kernel,
        out_shape=(
            jax.ShapeDtypeStruct((1, 1), F32),
            jax.ShapeDtypeStruct((64, 1024), F32),
            jax.ShapeDtypeStruct((1, 1024), F32),
            jax.ShapeDtypeStruct((256, 1024), BF16),
        ),
        in_specs=[pl.BlockSpec(memory_space=pltpu.HBM)] * 5,
        out_specs=(hbm,) * 4,
        scratch_shapes=scratch,
        compiler_params=pltpu.CompilerParams(
            collective_id=0, has_side_effects=True, vmem_limit_bytes=53 << 20
        ),
    )(*[
        pltpu.with_memory_space_constraint(a, pltpu.HBM)
        for a in (hidden, gain.reshape(1, 1024), head, targets.reshape(2, 128), row_weight.reshape(2, 128))
    ])
    loss, gh, gg, gx = pl.pallas_call(
        finish,
        out_shape=tuple(jax.ShapeDtypeStruct(a.shape, a.dtype) for a in (loss, gh, gg, gx)),
        in_specs=[hbm] * 4,
        out_specs=(hbm,) * 4,
        scratch_shapes=[S((4,))],
        compiler_params=pltpu.CompilerParams(vmem_limit_bytes=2 << 20),
    )(loss, gh, gg, gx)
    return (loss.reshape(()), gh, gg.reshape(1024), gx)


def solution(mesh):
    in_specs = (P("fsdp", "tp"), P("tp"), P("fsdp", "tp"), P("fsdp"), P("fsdp"))
    out_specs = (P(), P("fsdp", "tp"), P("tp"), P("fsdp", "tp"))
    return jax.shard_map(body, mesh=mesh, in_specs=in_specs, out_specs=out_specs, check_vma=False)
```

```python
import functools

import jax
import jax.numpy as jnp
from jax import lax
from jax.experimental import pallas as pl
from jax.experimental.pallas import tpu as pltpu
from jax.sharding import PartitionSpec as P

D = 4096
EPS = 1e-05
MESH = pl.DeviceIdType.MESH
F32 = jnp.float32
BF16 = jnp.bfloat16

DY = (1, 3, 2)
SZ = (1, 7)
PEERS = ((1, 0), (3, 0), (2, 0), (0, 1), (1, 1), (3, 1), (2, 1))
GATHER = (
    ("xe",), ("by", 1), ("bz", 0, 1, 0), ("bz", 1, 1, 0), ("az", 0, 1), ("az", 1, 1), ("by", 2), ("xo",),
    ("bz", 0, 1, 1), ("bz", 1, 1, 1), ("bz", 0, 2, 0), ("bz", 1, 2, 0), ("xf", 1), ("xf", 0),
    ("az", 0, 2), ("az", 1, 2), ("by", 3), ("xs", 1), ("xs", 0), ("ty",), ("bz", 0, 1, 2), ("bz", 1, 1, 2), ("iv", 1),
    ("nm", 1, 0), ("nm", 1, 1), ("nm", 1, 2), ("nm", 1, 3), ("bz", 0, 2, 1), ("bz", 1, 2, 1), ("nm", 1, 4),
    ("nm", 1, 5), ("nm", 1, 6), ("nm", 1, 7), ("bz", 0, 3, 0), ("bz", 1, 3, 0), ("az", 0, 3), ("az", 1, 3),
    ("bz", 0, 1, 3), ("bz", 1, 1, 3), ("bz", 0, 2, 2), ("bz", 1, 2, 2), ("xf", 2), ("bz", 0, 3, 1), ("bz", 1, 3, 1),
    ("tz", 1), ("xs", 2), ("iv", 0), ("nm", 0, 0), ("nm", 0, 1), ("nm", 0, 2), ("bz", 0, 4, 0), ("bz", 1, 2, 3),
    ("nm", 0, 3), ("nm", 0, 4), ("nm", 0, 5), ("az", 0, 4), ("bz", 1, 3, 2), ("nm", 0, 6), ("nm", 0, 7), ("lg", 0),
    ("bz", 0, 2, 3), ("bz", 1, 3, 3), ("lg", 7), ("lg", 1), ("bz", 0, 3, 2), ("bz", 1, 4, 2), ("lg", 6), ("tz", 2),
    ("lg", 2), ("bz", 0, 4, 1), ("lg", 3), ("bz", 0, 3, 3), ("bz", 1, 4, 3), ("lg", 5), ("lg", 4),
)
SCATTER = (
    ("hg", 4), ("ai", 4), ("bc", 0, 4, 0), ("bc", 1, 4, 1), ("hg", 3), ("ai", 3), ("bc", 0, 3, 1), ("ds", 0),
    ("tz", 3), ("hg", 5), ("ai", 5), ("bc", 1, 3, 0), ("bc", 0, 4, 2), ("bc", 1, 4, 2), ("ds", 1), ("du", 0),
    ("ds", 2), ("yr", 4), ("bc", 0, 3, 0), ("bc", 1, 3, 1), ("hg", 2), ("ai", 2), ("yr", 3), ("du", 1),
    ("bc", 0, 2, 1), ("hg", 6), ("ai", 6), ("yr", 5), ("bc", 1, 2, 0), ("bc", 0, 3, 2), ("bc", 1, 3, 2), ("ds", 3),
    ("tz", 4), ("a4",), ("du", 2), ("hg", 1), ("ai", 1), ("bc", 0, 2, 0), ("bc", 1, 2, 1), ("hg", 7), ("ai", 7),
    ("du", 3), ("yr", 2), ("gx",), ("qs",), ("bc", 0, 1, 1), ("bc", 1, 1, 0), ("bc", 0, 2, 2), ("bc", 1, 2, 2),
    ("xr", 1), ("xr", 2), ("yr", 6), ("ac", 0, 3), ("ac", 1, 3), ("hg", 0), ("ai", 0), ("bc", 0, 1, 0),
    ("bc", 1, 1, 1), ("yr", 1), ("yr", 7), ("bc", 0, 1, 2), ("bc", 1, 1, 2), ("ac", 0, 2), ("ac", 1, 2), ("yr", 0),
    ("qt",), ("gy",), ("bf", 0), ("bf", 1), ("al", 0), ("bf", 2), ("gz",), ("al", 1), ("bg",), ("af", 0), ("af", 1),
    ("bm",), ("fi",), ("gf",), ("gh",),
)


def kernel(
    hid, gain, hin_hbm, tgt_hbm, wgt_hbm,
    r_loss, r_gh, r_gg, r_hid,
    tgt, wgt, o_loss, o_gh, o_gg, o_hid, hin, hb, xg, nm, gg4, tw, ssq, invb, tgtb, wb, lg, ex, dl, dlt,
    st, qt, lseb, stat, pick, lser,
    ght, sbf, rbf, sba, rba, sa4, ra4, sa3, ra3, sa2, ra2, sb4, rb4, sbb, rbb, syb, ryb, fa, fb, ghs, ghr,
    dno, dns, dnr, dxs, dxr, dos, dor, rbx, gps, gxs, gxr, msg, ary, arz, tsum, tsum2, tot_y, tot_z,
    in_s, out_s, send_s,
    xh_r, tw_r, gn_r, hx_r, hh_r, hf_r, az_r, ay_r, by_r, bz_r, st_r, qt_r, ty_r, tz_r,
    rf_r, ra_r, rz_r, rl_r, rb_r, ry_r, fx_r, dc_r, d2_r, dx_r, do_r, gx_r, gy_r, gz_r,
):
    f = lax.axis_index("fsdp")
    t = lax.axis_index("tp")
    xl = f // 32
    z = (f // 4) % 8
    y = f % 4
    xh = t // 2
    c = t % 2
    x = xh * 2 + xl

    def dev(x_, y_, z_, c_):
        return (((x_ % 2) * 8 + z_) * 4 + y_, (x_ // 2) * 2 + c_)

    def at_x(dx, dc=0):
        return dev((x + dx) % 4, y, z, (c + dc) % 2)

    def at_y(dy):
        return dev(x, (y + dy) % 4, z, c)

    def at_z(dz):
        return dev(x, y, (z + dz) % 8, c)

    mate = dev(xh * 2 + (1 - xl), y, z, c)

    def yy(k):
        return (y + k) % 4

    def zz(k):
        return (z + k) % 8

    partners = [at_x(dx, dc) for dx, dc in PEERS] + [at_y(d) for d in DY] + [at_z(d) for d in SZ]
    barrier = pltpu.get_barrier_semaphore()
    for p in partners:
        pl.semaphore_signal(barrier, inc=1, device_id=p, device_id_type=MESH)
    in_hid = pltpu.make_async_copy(hid, xg.at[xl, t], in_s.at[0])
    in_head = pltpu.make_async_copy(hin_hbm, hin, in_s.at[1])
    in_small = [
        pltpu.make_async_copy(src, dst, in_s.at[2 + i])
        for i, (src, dst) in enumerate(((tgt_hbm, tgt), (wgt_hbm, wgt), (gain, gg4.at[t])))
    ]
    in_head.start()
    in_hid.start()
    for cp in in_small:
        cp.start()
    oth = pl.multiple_of((1 - xl) * 512, 512)
    own = pl.multiple_of(xl * 512, 512)
    in_head.wait()
    hb[z, y, xl] = hin[:, pl.ds(own, 512)]
    pl.semaphore_wait(barrier, len(partners))

    sent = [0, 0, 0]
    GATHER_S, SEND_S, X_S = range(3)

    def rc(src, dst, ss, rs, to):
        return pltpu.make_async_remote_copy(
            src_ref=src, dst_ref=dst, send_sem=ss, recv_sem=rs, device_id=to, device_id_type=MESH
        )

    def send(src, dst, group, rs, to):
        rc(src, dst, send_s.at[group], rs, to).start()
        size = jnp.dtype(src.dtype).itemsize
        for n in src.shape:
            size *= n
        sent[group] += size

    def got(dst, rs):
        rc(dst, dst, rs, rs, at_y(1)).wait_recv()

    def b_hop(s, d, k):
        yk = y if k == 0 else ywas(k - 1)
        ref = hb.at[zz(-SZ[s] * d), yk, xl]
        send(ref, ref, GATHER_S, bz_r.at[s, d, k], at_z(SZ[s]))

    def a_hop(s, d):
        ref = hb.at[zz(-SZ[s] * d), y, 1 - xl]
        send(ref, ref, GATHER_S, az_r.at[s, d], at_z(SZ[s]))

    def a_out(k):
        ref = hb.at[zz(k), y, 1 - xl]
        for j in range(3):
            send(ref, ref, GATHER_S, ay_r.at[k], at_y(DY[j]))

    def ywas(j):
        return yy(-DY[j])

    def limit(s, k):
        if k < 0:
            return 4 if s == 0 else 3
        return 4 if (k < 2) == (s == 0) else 3

    def ring_limit(s):
        return 4 if s == 0 else 3

    send(hin.at[:, pl.ds(oth, 512)], hb.at[z, y, xl], GATHER_S, xh_r, mate)
    def b_out(j):
        ref = hb.at[z, y, xl]
        send(ref, ref, GATHER_S, by_r.at[j], at_y(DY[j]))

    b_out(0)
    b_out(1)
    for s in range(2):
        b_hop(s, 0, 0)
    for cp in in_small:
        cp.wait()
    tw[xl, 0:2, :] = tgt[...].astype(F32)
    tw[xl, 2:4, :] = wgt[...].astype(F32)
    send(tw.at[xl], tw.at[xl], GATHER_S, tw_r, mate)
    GP = ((0, 1), (2, 0), (2, 1))
    for i, (dx, dc) in enumerate(GP):
        send(gg4.at[t], gg4.at[t], GATHER_S, gn_r, at_x(dx, dc))
    in_hid.wait()
    for i, dx, dc in ((3, 0, 1), (0, 1, 0), (1, 3, 0)):
        send(xg.at[xl, t], xg.at[xl, t], GATHER_S, hx_r.at[i], at_x(dx, dc))

    def ssq_block(xl_, t_):
        def step(i, carry):
            rows = pl.ds(pl.multiple_of(i * 32, 32), 32)
            v = xg[xl_, t_, rows, :].astype(F32)
            v = v * v
            acc = v[:, 0:128]
            for k in range(1, 8):
                acc = acc + v[:, k * 128:(k + 1) * 128]
            ssq[xl_, rows, :] += acc
            return carry
        lax.fori_loop(0, 8, step, 0, unroll=4)

    def col(row):
        return jnp.transpose(jnp.broadcast_to(row, (128, 128)))

    ssq[...] = jnp.zeros_like(ssq)
    ssq_block(xl, t)

    def tokens():
        got(tw.at[1 - xl], tw_r)
        tsum[...] = jnp.zeros_like(tsum)
        tsum[0:2, :] = tw[0, 2:4, :] + tw[1, 2:4, :]
        for j in range(3):
            send(tsum, tot_y.at[j], SEND_S, ty_r, at_y(DY[j]))
        for a in range(2):
            for k in range(2):
                tgtb[a, k * 128:(k + 1) * 128, :] = col(tw[a, k:k + 1, :])
                wb[a, k * 128:(k + 1) * 128, :] = col(tw[a, 2 + k:3 + k, :])

    def t_hop(src, s, d):
        send(src, tot_z.at[s, d], SEND_S, tz_r.at[s, d], at_z(SZ[s]))

    def do_ty():
        got(tot_y, ty_r)
        tsum2[...] = tsum[...] + tot_y[0] + tot_y[1] + tot_y[2]
        for s in range(2):
            t_hop(tsum2, s, 0)

    def do_tz(d):
        for s in range(2):
            if d <= ring_limit(s):
                got(tot_z.at[s, d - 1], tz_r.at[s, d - 1])
                if d < ring_limit(s):
                    t_hop(tot_z.at[s, d - 1], s, d)

    def do_xe():
        got(hb.at[z, y, 1 - xl], xh_r)
        a_hop(0, 0)
        a_hop(1, 0)
        b_out(2)
        a_out(0)

    def do_by(k):
        got(hb.at[z, ywas(k - 1), xl], by_r.at[k - 1])
        for s in range(2):
            b_hop(s, 0, k)

    def do_az(s, d):
        got(hb.at[zz(-SZ[s] * d), y, 1 - xl], az_r.at[s, d - 1])
        if d < limit(s, -1):
            a_hop(s, d)
        a_out((-SZ[s] * d) % 8)

    def do_bz(s, d, k):
        yk = y if k == 0 else ywas(k - 1)
        got(hb.at[zz(-SZ[s] * d), yk, xl], bz_r.at[s, d - 1, k])
        if d < limit(s, k):
            b_hop(s, d, k)

    def rows_of(i):
        return slice(i * 128, (i + 1) * 128)

    XD = (1, 3, 2)

    def xblock(i):
        xs = (x - XD[i] + 4) % 4
        return xs % 2, (xs // 2) * 2

    def do_xf(i):
        a, b = xblock(i)
        ref = xg.at[a, b + c]
        if i < 2:
            got(ref, hx_r.at[i])
            part = xg.at[a, b + c, rows_of(i)]
            send(part, part, GATHER_S, hh_r.at[i], at_x((1, 3)[i]))
        else:
            for h in range(2):
                got(xg.at[a, b + c, rows_of(h)], hh_r.at[h])
        send(ref, ref, GATHER_S, hf_r.at[i], at_x(0, 1))
        ssq_block(a, b + c)

    def do_xs(i):
        a, b = xblock(i)
        got(xg.at[a, b + 1 - c], hf_r.at[i])
        ssq_block(a, b + 1 - c)

    def do_xo():
        got(xg.at[xl, xh * 2 + 1 - c], hx_r.at[3])
        ssq_block(xl, xh * 2 + 1 - c)
        got(gg4.at[0:3], gn_r)

    def half(h):
        return (xl + h) % 2

    def do_iv(h):
        a = half(h)
        s_ = jnp.sum(ssq[a], axis=1, keepdims=True)
        invb[a] = jnp.broadcast_to(lax.rsqrt(s_ * (1.0 / D) + EPS), (256, 128))

    def do_nm(h, zb):
        a = half(h)
        t0 = zb // 4
        off = (zb % 4) * 256

        def step(i, carry):
            rows = pl.ds(pl.multiple_of(i * 32, 32), 32)
            out = pl.ds(pl.multiple_of(a * 256 + i * 32, 32), 32)
            inv = invb[a, rows, :]
            low = lax.broadcasted_iota(jnp.int32, (32, 128), 1) < 64
            for p in range(2):
                cols = slice(off + p * 128, off + (p + 1) * 128)
                u = xg[a, t0, rows, cols].astype(F32) * inv * gg4[t0, :, cols]
                v = xg[a, t0 + 2, rows, cols].astype(F32) * inv * gg4[t0 + 2, :, cols]
                ur = pltpu.roll(u, 64, 1)
                vr = pltpu.roll(v, 64, 1)
                nm[zb, out, (2 * p) * 128:(2 * p + 1) * 128] = jnp.where(low, u, vr).astype(BF16)
                nm[zb, out, (2 * p + 1) * 128:(2 * p + 2) * 128] = jnp.where(low, ur, v).astype(BF16)
            return carry
        lax.fori_loop(0, 8, step, 0, unroll=4)

    def do_lg(k):
        got(hb.at[0:3, 0, 0], ay_r.at[k])
        part = jnp.dot(nm[zz(k)], hb[zz(k)].reshape(512, 512), preferred_element_type=F32)
        if k == 0:
            lg[...] = part
        else:
            lg[...] += part

    steps = dict(
        xe=do_xe, by=do_by, az=do_az, bz=do_bz, xf=do_xf, xs=do_xs, xo=do_xo,
        iv=do_iv, nm=do_nm, lg=do_lg, ty=do_ty, tz=do_tz,
    )
    tokens_done = False
    for name, *arg in GATHER:
        steps[name](*arg)
        if name == "by" and not tokens_done:
            tokens_done = True
            tokens()

    col0 = (t * 1024 + xl * 512).astype(F32)
    me = x * 2 + c

    def stat_step(i, carry):
        rows = pl.ds(pl.multiple_of(i * 32, 32), 32)
        l = lg[rows, :]
        m = jnp.max(l, axis=1, keepdims=True)
        ev = jnp.exp(l - m)
        ex[rows, :] = ev
        e = jnp.sum(ev, axis=1, keepdims=True)
        lane = lax.broadcasted_iota(jnp.int32, (32, 128), 1)
        stat[rows, :] = jnp.where(lane == 0, m, jnp.where(lane == 1, e, 0.0))
        return carry

    lax.fori_loop(0, 16, stat_step, 0, unroll=4)
    for k in range(4):
        st[me, k] = jnp.transpose(stat[k * 128:(k + 1) * 128, :])[0:8, :]
    for i, (dx, dc) in enumerate(PEERS):
        send(st.at[me], st.at[me], SEND_S, st_r, at_x(dx, dc))

    def pick_step(i, carry):
        rows = pl.ds(pl.multiple_of(i * 32, 32), 32)
        a = i // 8
        tb = tgtb[a, pl.ds(pl.multiple_of((i % 8) * 32, 32), 32), :][:, 0:1] - col0
        cols = lax.broadcasted_iota(jnp.int32, (32, 512), 1).astype(F32)
        pk = jnp.sum(jnp.where(cols == tb, lg[rows, :], 0.0), axis=1, keepdims=True)
        pick[rows, :] = jnp.broadcast_to(pk, (32, 128))
        return carry

    lax.fori_loop(0, 16, pick_step, 0, unroll=4)
    got(st.at[0:7], st_r)
    allst = st[...]
    mx = jnp.max(allst[:, :, 0:1, :], axis=0)
    es = jnp.sum(allst[:, :, 1:2, :] * jnp.exp(allst[:, :, 0:1, :] - mx[None]), axis=0)
    lse = mx + jnp.log(es)
    lser[...] = lse
    for k in range(4):
        lseb[k * 128:(k + 1) * 128, :] = col(lse[k])

    def dl_step(i, carry):
        a = i // 8
        rows = pl.ds(pl.multiple_of((i % 8) * 32, 32), 32)
        g = pl.ds(pl.multiple_of(i * 32, 32), 32)
        tb = tgtb[a, rows, :][:, 0:1] - col0
        w = wb[a, rows, :][:, 0:1]
        cols = lax.broadcasted_iota(jnp.int32, (32, 512), 1).astype(F32)
        p = ex[g, :] * jnp.exp(stat[g, :][:, 0:1] - lseb[g, :][:, 0:1])
        d = (w * (p - jnp.where(cols == tb, 1.0, 0.0))).astype(BF16)
        dl[a, rows, :] = d
        return carry

    lax.fori_loop(0, 16, dl_step, 0, unroll=4)
    for a in range(2):
        dlt[:, a * 256:(a + 1) * 256] = jnp.transpose(dl[a])

    def do_qs():
        def step(i, carry):
            a = i // 8
            g = pl.ds(pl.multiple_of(i * 32, 32), 32)
            d = dl[a, pl.ds(pl.multiple_of((i % 8) * 32, 32), 32), :]
            q = jnp.sum(d.astype(F32) * lg[g, :], axis=1, keepdims=True)
            lane = lax.broadcasted_iota(jnp.int32, (32, 128), 1)
            stat[g, :] = jnp.where(lane == 0, q, pick[g, :])
            return carry
        lax.fori_loop(0, 16, step, 0, unroll=4)
        for k in range(4):
            qt[me, k] = jnp.transpose(stat[k * 128:(k + 1) * 128, :])[0:8, :]
        for i, (dx, dc) in enumerate(PEERS):
            send(qt.at[me], qt.at[me], SEND_S, qt_r, at_x(dx, dc))

    def a_rows(k, b, h):
        return pl.ds(pl.multiple_of((k * 4 + b) * 512 + h * 160, 32), 160)

    Q_AT = (384, 448, 320)

    def b_rows(k, q):
        first = Q_AT[q]
        return [ght[(k * 4 + b) * 512 + first:(k * 4 + b) * 512 + first + 64, :] for b in range(4)]

    def do_hg(k):
        g = jnp.dot(dlt[...], nm[zz(k)], preferred_element_type=F32)
        for b in range(4):
            ght[(k * 4 + b) * 512:(k * 4 + b + 1) * 512, :] = g[:, b * 128:(b + 1) * 128]
        for i in range(2):
            sbf[k, i] = ght[a_rows(k, yy(2), i), :].astype(BF16)
            send(sbf.at[k, i], rbf.at[k, i], SEND_S, rf_r.at[k], at_y(DY[i]))

    def do_ai(k):
        for i in range(2):
            sba[k, i, 1 - i] = ght[a_rows(k, yy(DY[i]), 1 - i), :].astype(BF16)
            send(sba.at[k, i, 1 - i], rba.at[k, i, 1 - i], SEND_S, ra_r.at[k, 0], at_y(DY[i]))

    def do_yr(k):
        got(rbf.at[k], rf_r.at[k])
        for i in range(2):
            sba[k, i, i] = (ght[a_rows(k, yy(DY[i]), i), :] + rbf[k, i].astype(F32)).astype(BF16)
            send(sba.at[k, i, i], rba.at[k, i, i], SEND_S, ra_r.at[k, 1], at_y(DY[i]))

    def do_bc(s, d, q):
        v = b_rows((SZ[s] * d) % 8, q)
        h = slice(s * 32, (s + 1) * 32)
        if q == 2 and d == 4:
            for b in range(4):
                sb4[s, b] = v[b][h].astype(BF16)
            send(sb4.at[s], rb4.at[s], SEND_S, rb_r.at[s, q, 3], at_z(SZ[s]))
            return
        if q == 2 and d == 3:
            got(rb4.at[s], rb_r.at[s, q, 3])
            for b in range(4):
                sbb[s, q, 2, b] = v[b].astype(BF16)
                sbb[s, q, 2, b, h] = (v[b][h] + rb4[s, b].astype(F32)).astype(BF16)
        else:
            if d < (4 if q == s else 3):
                got(rbb.at[s, q, d], rb_r.at[s, q, d])
                v = [v[b] + rbb[s, q, d, b].astype(F32) for b in range(4)]
            for b in range(4):
                sbb[s, q, d - 1, b] = v[b].astype(BF16)
        send(sbb.at[s, q, d - 1], rbb.at[s, q, d - 1], SEND_S, rb_r.at[s, q, d - 1], at_z(SZ[s]))

    def a_wait(k):
        for i in range(2):
            got(rba.at[k, 0], ra_r.at[k, i])

    def a_half(k, h):
        return ght[a_rows(k, y, h), :] + rba[k, 0, h].astype(F32) + rba[k, 1, h].astype(F32)

    def a_sum(k):
        a_wait(k)
        return [a_half(k, h) for h in range(2)]

    def do_a4():
        v = a_sum(4)
        for s in range(2):
            sa4[s] = v[s].astype(BF16)
            send(sa4.at[s], ra4.at[s], SEND_S, rz_r.at[s, 3], at_z(SZ[s]))

    def do_ac(s, d):
        v = a_sum((SZ[s] * d) % 8)
        if d == 3:
            got(ra4.at[s], rz_r.at[s, 3])
            v[s] = v[s] + ra4[s].astype(F32)
            for h in range(2):
                sa3[s, h] = v[h].astype(BF16)
            send(sa3.at[s], ra3.at[s], SEND_S, rz_r.at[s, 2], at_z(SZ[s]))
            return
        got(ra3.at[s], rz_r.at[s, 2])
        for h in range(2):
            sa2[s, 1, h] = v[h] + ra3[s, h].astype(F32)
            send(sa2.at[s, 1, h], ra2.at[s, 1, h], SEND_S, rl_r.at[s, 1, h], at_z(SZ[s]))

    def do_al(h):
        for s in range(2):
            if h == 0:
                a_wait(SZ[s])
            got(ra2.at[s, 1, h], rl_r.at[s, 1, h])
            sa2[s, 0, h] = a_half(SZ[s], h) + ra2[s, 1, h]
            send(sa2.at[s, 0, h], ra2.at[s, 0, h], SEND_S, rl_r.at[s, 0, h], at_z(SZ[s]))

    XO = (2, 1, 3, 0)

    def xdest(n):
        xs = (x + XO[n]) % 4
        return xs % 2, xs // 2

    def dn_part(out, n, cc):
        a, b = xdest(n)
        for i in range(4):
            h = hb[4 * cc + i, :, b].reshape(256, 512)
            out[n, :, i * 256:(i + 1) * 256] = lax.dot_general(
                dl[a], h, (((1,), (1,)), ((), ())), preferred_element_type=F32
            )

    def do_ds(n):
        dn_part(dns, n, 1 - c)
        send(dns.at[n], dnr.at[n], X_S, dc_r.at[n], at_x(0, 1))
        dn_part(dno, n, c)

    def x_out(i):
        src = dno.at[1 + i, rows_of(i)]
        send(src, rbx.at[i], X_S, dx_r.at[i], at_x((1, 3)[i]))

    def x_one(i):
        dos[i] = dno[1 + i, rows_of(1 - i), :].astype(BF16)
        send(dos.at[i], dor.at[1 - i], X_S, do_r.at[i], at_x((1, 3)[i]))

    def do_du(n):
        got(dnr.at[n], dc_r.at[n])
        a, b = xdest(n)
        tx = b * 2 + c

        def step(i, acc):
            rows = pl.ds(pl.multiple_of(i * 16, 16), 16)
            s_ = dno[n, rows, :] + dnr[n, rows, :]
            if n == 0:
                dxs[rows, :] = s_.astype(BF16)
            else:
                dno[n, rows, :] = s_
            xv = xg[a, tx, rows, :].astype(F32) * invb[a, rows, :][:, 0:1]
            pr = s_ * xv
            return acc + pr[0:8] + pr[8:16]
        acc = lax.fori_loop(0, 16, step, jnp.zeros((8, 1024), F32), unroll=2)
        gps[b * 2 + a] = jnp.sum(acc, axis=0, keepdims=True)
        if n == 0:
            for i in range(2):
                send(dxs.at[rows_of(i)], dxr.at[i], X_S, d2_r.at[i], at_x((1, 3)[i]))
        elif n == 1:
            x_one(0)
        elif n == 2:
            x_one(1)

    def do_xr(n):
        i = n - 1
        got(dxr.at[i], d2_r.at[i])
        dno[n, rows_of(i), :] = dno[n, rows_of(i), :] + dxr[i].astype(F32)
        x_out(i)

    results = []

    def result(src, dst, i):
        cp = pltpu.make_async_copy(src, dst, out_s.at[i])
        cp.start()
        results.append(cp)

    def do_gx():
        for b in range(2):
            gxs[b] = gps[2 * b] + gps[2 * b + 1]
        for i, dx in enumerate((1, 3, 2)):
            b = ((x + dx) % 4) // 2
            send(gxs.at[b], gxr.at[i], SEND_S, gx_r, at_x(dx))

    def do_gy():
        got(gxr, gx_r)
        msg[:, 0:1024] = gxs[xh] + gxr[0] + gxr[1] + gxr[2]
        for j in range(3):
            send(msg, ary.at[j], SEND_S, gy_r, at_y(DY[j]))

    def do_gz():
        got(ary.at[0:3], gy_r)
        ary[3] = msg[...] + ary[0] + ary[1] + ary[2]
        for d in range(1, 8):
            send(ary.at[3], arz.at[d - 1], SEND_S, gz_r, at_z(d))

    def total_inverse():
        tot = tsum2[...]
        for s in range(2):
            for d in range(ring_limit(s)):
                tot = tot + tot_z[s, d]
        return 1.0 / jnp.sum(jnp.sum(tot, axis=1, keepdims=True), axis=0, keepdims=True)

    def do_gf():
        got(arz, gz_r)
        g = ary[3]
        for d in range(7):
            g = g + arz[d]
        o_gg[...] = g[:, 0:1024] * inv_total
        o_loss[...] = jnp.sum(g[:, 1024:1152], axis=1, keepdims=True) * inv_total
        result(o_loss, r_loss, 0)
        result(o_gg, r_gg, 1)

    def do_qt():
        got(qt.at[0:7], qt_r)
        qsum = qt[0]
        for i in range(1, 8):
            qsum = qsum + qt[i]
        loss_row = jnp.zeros((1, 128), F32)
        for k in range(4):
            loss_row = loss_row + tw[k // 2, 2 + k % 2:3 + k % 2, :] * (lser[k] - qsum[k, 1:2, :])
            lseb[k * 128:(k + 1) * 128, :] = col(qsum[k, 0:1, :])
        msg[:, 1024:1152] = loss_row

    PARTS = tuple(slice(i * 128, (i + 1) * 128) for i in range(4))

    def turn(i, v):
        ft = jnp.transpose(v)
        for a in range(2):
            ghs[a, :, PARTS[i]] = ft[a * 64:(a + 1) * 64]
        send(ghs.at[1 - xl, :, PARTS[i]], ghr.at[:, PARTS[i]], SEND_S, fx_r.at[i], mate)

    def do_af(h):
        if h == 0:
            a_wait(0)
        v = a_half(0, h)
        for s in range(2):
            got(ra2.at[s, 0, h], rl_r.at[s, 0, h])
            v = v + ra2[s, 0, h]
        fa[h * 160:(h + 1) * 160, :] = v
        turn(h, fa[h * 128:(h + 1) * 128, :])

    def do_bf(q):
        v = b_rows(0, q)
        for s in range(2):
            got(rbb.at[s, q, 0], rb_r.at[s, q, 0])
            v = [v[b] + rbb[s, q, 0, b].astype(F32) for b in range(4)]
        for b in range(4):
            syb[q, b] = v[b]
        for j in range(3):
            src = syb.at[q, yy(DY[j])]
            send(src, ryb.at[q, j], SEND_S, ry_r.at[q], at_y(DY[j]))

    def b_sum(q):
        v = syb[q, y]
        got(ryb.at[q], ry_r.at[q])
        for j in range(3):
            v = v + ryb[q, j]
        return v

    def do_bg():
        for q in range(2):
            fb[q * 64:(q + 1) * 64, :] = b_sum(q)
        turn(3, fb[...])

    def do_bm():
        fa[320:384, :] = b_sum(2)
        turn(2, fa[256:384, :])

    def do_gh():
        o_gh[:, pl.ds(own, 512)] = ghs[xl] * inv_total
        for i in range(4):
            got(ghr.at[:, PARTS[i]], fx_r.at[i])
        o_gh[:, pl.ds(oth, 512)] = ghr[...] * inv_total
        result(o_gh, r_gh, 2)

    def do_fi():
        for i in range(2):
            got(rbx.at[i], dx_r.at[i])
            got(dor.at[1 - i], do_r.at[i])
        gt = gg4[t]

        def fin(i, carry):
            rows = pl.ds(pl.multiple_of(i * 16, 16), 16)
            qrow = pl.ds(pl.multiple_of(xl * 256 + i * 16, 16), 16)
            h = i // 8
            half_rows = pl.ds(pl.multiple_of((i % 8) * 16, 16), 16)
            dn = dno[3, rows, :] + rbx[h, half_rows, :] + dor[h, half_rows, :].astype(F32)
            inv = invb[xl, rows, :][:, 0:1]
            q = lseb[qrow, :][:, 0:1]
            xv = xg[xl, t, rows, :].astype(F32)
            u = inv * inv_total
            o_hid[rows, :] = (dn * gt * u - xv * (inv * u * q * (1.0 / D))).astype(BF16)
            return carry

        lax.fori_loop(0, 16, fin, 0, unroll=2)
        result(o_hid, r_hid, 3)

    steps = dict(
        ds=do_ds, hg=do_hg, bc=do_bc, du=do_du, a4=do_a4, ac=do_ac, xr=do_xr, gy=do_gy, gz=do_gz,
        gx=do_gx, gf=do_gf, qs=do_qs, qt=do_qt, tz=do_tz, yr=do_yr, ai=do_ai, al=do_al, af=do_af, bf=do_bf, bg=do_bg, bm=do_bm, gh=do_gh, fi=do_fi,
    )
    for name, *arg in SCATTER:
        steps[name](*arg)
        if name == "tz" and arg[0] == 4:
            inv_total = total_inverse()
    for group, size in enumerate(sent):
        whole = ght.at[pl.ds(0, size // 512)]
        rc(whole, whole, send_s.at[group], send_s.at[group], at_y(1)).wait_send()
    for cp in results:
        cp.wait()


def finish(*refs):
    copies = [pltpu.make_async_copy(refs[i], refs[4 + i], refs[8].at[i]) for i in range(4)]
    for cp in copies:
        cp.start()
    for cp in copies:
        cp.wait()


def body(hidden, gain, head, targets, row_weight):
    V = pltpu.VMEM
    S = pltpu.SemaphoreType.DMA
    hbm = pl.BlockSpec(memory_space=pl.ANY)
    scratch = [
        V((2, 128), jnp.int32),
        V((2, 128), jnp.int32),
        V((1, 1), F32),
        V((64, 1024), F32),
        V((1, 1024), F32),
        V((256, 1024), BF16),
        V((64, 1024), BF16),
        V((8, 4, 2, 64, 512), BF16),
        V((2, 4, 256, 1024), BF16),
        V((8, 512, 512), BF16),
        V((4, 1, 1024), F32),
        V((2, 8, 128), F32),
        V((2, 256, 128), F32),
        V((2, 256, 128), F32),
        V((2, 256, 128), F32),
        V((2, 256, 128), F32),
        V((512, 512), F32),
        V((512, 512), F32),
        V((2, 256, 512), BF16),
        V((512, 512), BF16),
        V((8, 4, 8, 128), F32),
        V((8, 4, 8, 128), F32),
        V((512, 128), F32),
        V((512, 128), F32),
        V((512, 128), F32),
        V((4, 1, 128), F32),
        V((16384, 128), F32),
        V((8, 2, 160, 128), BF16),
        V((8, 2, 160, 128), BF16),
        V((8, 2, 2, 160, 128), BF16),
        V((8, 2, 2, 160, 128), BF16),
        V((2, 160, 128), BF16),
        V((2, 160, 128), BF16),
        V((2, 2, 160, 128), BF16),
        V((2, 2, 160, 128), BF16),
        V((2, 2, 2, 160, 128), F32),
        V((2, 2, 2, 160, 128), F32),
        V((2, 4, 32, 128), BF16),
        V((2, 4, 32, 128), BF16),
        V((2, 3, 4, 4, 64, 128), BF16),
        V((2, 3, 4, 4, 64, 128), BF16),
        V((3, 4, 64, 128), F32),
        V((3, 3, 64, 128), F32),
        V((384, 128), F32),
        V((128, 128), F32),
        V((2, 64, 512), F32),
        V((64, 512), F32),
        V((4, 256, 1024), F32),
        V((4, 256, 1024), F32),
        V((4, 256, 1024), F32),
        V((256, 1024), BF16),
        V((2, 128, 1024), BF16),
        V((2, 128, 1024), BF16),
        V((2, 128, 1024), BF16),
        V((2, 128, 1024), F32),
        V((4, 1, 1024), F32),
        V((2, 1, 1024), F32),
        V((3, 1, 1024), F32),
        V((1, 1152), F32),
        V((4, 1, 1152), F32),
        V((7, 1, 1152), F32),
        V((8, 128), F32),
        V((8, 128), F32),
        V((3, 8, 128), F32),
        V((2, 4, 8, 128), F32),
        S((5,)),
        S((4,)),
        S((3,)),
    ]
    shapes = [
        (), (), (), (4,), (2,), (3,), (2, 4), (8,), (3,), (2, 4, 4),
        (), (), (), (2, 4), (8,), (8, 2), (2, 4), (2, 2, 2), (2, 3, 4), (3,), (4,),
        (4,), (2,), (2,), (2,), (), (), (),
    ]
    scratch += [S(sh) if sh else S for sh in shapes]
    loss, gh, gg, gx = pl.pallas_call(
        kernel,
        out_shape=(
            jax.ShapeDtypeStruct((1, 1), F32),
            jax.ShapeDtypeStruct((64, 1024), F32),
            jax.ShapeDtypeStruct((1, 1024), F32),
            jax.ShapeDtypeStruct((256, 1024), BF16),
        ),
        in_specs=[pl.BlockSpec(memory_space=pltpu.HBM)] * 5,
        out_specs=(hbm,) * 4,
        scratch_shapes=scratch,
        compiler_params=pltpu.CompilerParams(
            collective_id=0, has_side_effects=True, vmem_limit_bytes=53 << 20
        ),
    )(*[
        pltpu.with_memory_space_constraint(a, pltpu.HBM)
        for a in (hidden, gain.reshape(1, 1024), head, targets.reshape(2, 128), row_weight.reshape(2, 128))
    ])
    loss, gh, gg, gx = pl.pallas_call(
        finish,
        out_shape=tuple(jax.ShapeDtypeStruct(a.shape, a.dtype) for a in (loss, gh, gg, gx)),
        in_specs=[hbm] * 4,
        out_specs=(hbm,) * 4,
        scratch_shapes=[S((4,))],
        compiler_params=pltpu.CompilerParams(vmem_limit_bytes=2 << 20),
    )(loss, gh, gg, gx)
    return (loss.reshape(()), gh, gg.reshape(1024), gx)


def solution(mesh):
    in_specs = (P("fsdp", "tp"), P("tp"), P("fsdp", "tp"), P("fsdp"), P("fsdp"))
    out_specs = (P(), P("fsdp", "tp"), P("tp"), P("fsdp", "tp"))
    return jax.shard_map(body, mesh=mesh, in_specs=in_specs, out_specs=out_specs, check_vma=False)
```

```python
import functools

import jax
import jax.numpy as jnp
from jax import lax
from jax.experimental import pallas as pl
from jax.experimental.pallas import tpu as pltpu
from jax.sharding import PartitionSpec as P

D = 4096
EPS = 1e-05
MESH = pl.DeviceIdType.MESH
F32 = jnp.float32
BF16 = jnp.bfloat16

DY = (1, 3, 2)
SZ = (1, 7)
PEERS = ((1, 0), (3, 0), (2, 0), (0, 1), (1, 1), (3, 1), (2, 1))
GATHER = (
    ("xe",), ("by", 1), ("bz", 0, 1, 0), ("bz", 1, 1, 0), ("az", 0, 1), ("az", 1, 1), ("by", 2), ("xo",),
    ("bz", 0, 1, 1), ("bz", 1, 1, 1), ("bz", 0, 2, 0), ("bz", 1, 2, 0), ("az", 0, 2), ("az", 1, 2), ("by", 3),
    ("xf", 1), ("xf", 0), ("bz", 0, 1, 2), ("bz", 1, 1, 2), ("bz", 0, 2, 1), ("bz", 1, 2, 1), ("ty",),
    ("bz", 0, 3, 0), ("bz", 1, 3, 0), ("az", 0, 3), ("az", 1, 3), ("xs", 1), ("xs", 0), ("iv", 1), ("bz", 0, 1, 3),
    ("bz", 1, 1, 3), ("nm", 1, 0), ("nm", 1, 1), ("nm", 1, 2), ("bz", 0, 2, 2), ("bz", 1, 2, 2), ("nm", 1, 3),
    ("nm", 1, 4), ("xf", 2), ("bz", 0, 3, 1), ("bz", 1, 3, 1), ("nm", 1, 5), ("nm", 1, 6), ("tz", 1), ("bz", 0, 4, 0),
    ("bz", 1, 2, 3), ("nm", 1, 7), ("az", 0, 4), ("xs", 2), ("iv", 0), ("nm", 0, 0), ("nm", 0, 1), ("bz", 1, 3, 2),
    ("bz", 0, 2, 3), ("nm", 0, 2), ("nm", 0, 3), ("nm", 0, 4), ("bz", 1, 3, 3), ("nm", 0, 5), ("nm", 0, 6),
    ("nm", 0, 7), ("bz", 0, 3, 2), ("bz", 1, 4, 2), ("lg", 0), ("lg", 7), ("lg", 1), ("lg", 6), ("lg", 2),
    ("bz", 0, 3, 3), ("bz", 0, 4, 1), ("lg", 3), ("bz", 1, 4, 3), ("tz", 2), ("lg", 5), ("lg", 4),
)
SCATTER = (
    ("hg", 4), ("ai", 4), ("bc", 0, 4, 0), ("bc", 1, 4, 1), ("hg", 3), ("ai", 3), ("bc", 0, 3, 1), ("ds", 0),
    ("tz", 3), ("hg", 5), ("ai", 5), ("bc", 1, 3, 0), ("bc", 0, 4, 2), ("bc", 1, 4, 2), ("ds", 1), ("du", 0),
    ("ds", 2), ("yr", 4), ("bc", 0, 3, 0), ("bc", 1, 3, 1), ("hg", 2), ("ai", 2), ("yr", 3), ("du", 1),
    ("bc", 0, 2, 1), ("hg", 6), ("ai", 6), ("yr", 5), ("bc", 1, 2, 0), ("bc", 0, 3, 2), ("bc", 1, 3, 2), ("ds", 3),
    ("tz", 4), ("a4",), ("du", 2), ("hg", 1), ("ai", 1), ("bc", 0, 2, 0), ("bc", 1, 2, 1), ("hg", 7), ("ai", 7),
    ("du", 3), ("yr", 2), ("gx",), ("qs",), ("bc", 0, 1, 1), ("bc", 1, 1, 0), ("xr", 1), ("xr", 2), ("yr", 6),
    ("ac", 0, 3), ("ac", 1, 3), ("hg", 0), ("ai", 0), ("bc", 0, 2, 2), ("bc", 1, 2, 2), ("bc", 0, 1, 0),
    ("bc", 1, 1, 1), ("yr", 1), ("yr", 7), ("ac", 0, 2), ("ac", 1, 2), ("bc", 0, 1, 2), ("bc", 1, 1, 2), ("yr", 0),
    ("qt",), ("gy",), ("bf", 0), ("bf", 1), ("al", 0), ("al", 1), ("bf", 2), ("gz",), ("bg",), ("af", 0), ("af", 1),
    ("bm",), ("fi",), ("gf",), ("gh",),
)


def kernel(
    hid, gain, hin_hbm, tgt_hbm, wgt_hbm,
    r_loss, r_gh, r_gg, r_hid,
    tgt, wgt, o_loss, o_gh, o_gg, o_hid, hin, hb, xg, nm, gg4, tw, ssq, invb, tgtb, wb, lg, ex, dl, dlt,
    st, qt, lseb, stat, pick, lser,
    ght, sbf, rbf, sba, rba, sa4, ra4, sa3, ra3, sa2, ra2, sb4, rb4, sbb, rbb, syb, ryb, fa, fb, ghs, ghr,
    dno, dns, dnr, dxs, dxr, dos, dor, rbx, gps, gxs, gxr, msg, ary, arz, tsum, tsum2, tot_y, tot_z,
    in_s, out_s, send_s,
    xh_r, tw_r, gn_r, hx_r, hh_r, hf_r, az_r, ay_r, by_r, bz_r, st_r, qt_r, ty_r, tz_r,
    rf_r, ra_r, rz_r, rl_r, rb_r, ry_r, fx_r, dc_r, d2_r, dx_r, do_r, gx_r, gy_r, gz_r,
):
    f = lax.axis_index("fsdp")
    t = lax.axis_index("tp")
    xl = f // 32
    z = (f // 4) % 8
    y = f % 4
    xh = t // 2
    c = t % 2
    x = xh * 2 + xl

    def dev(x_, y_, z_, c_):
        return (((x_ % 2) * 8 + z_) * 4 + y_, (x_ // 2) * 2 + c_)

    def at_x(dx, dc=0):
        return dev((x + dx) % 4, y, z, (c + dc) % 2)

    def at_y(dy):
        return dev(x, (y + dy) % 4, z, c)

    def at_z(dz):
        return dev(x, y, (z + dz) % 8, c)

    mate = dev(xh * 2 + (1 - xl), y, z, c)

    def yy(k):
        return (y + k) % 4

    def zz(k):
        return (z + k) % 8

    partners = [at_x(dx, dc) for dx, dc in PEERS] + [at_y(d) for d in DY] + [at_z(d) for d in SZ]
    barrier = pltpu.get_barrier_semaphore()
    for p in partners:
        pl.semaphore_signal(barrier, inc=1, device_id=p, device_id_type=MESH)
    in_hid = pltpu.make_async_copy(hid, xg.at[xl, t], in_s.at[0])
    in_head = pltpu.make_async_copy(hin_hbm, hin, in_s.at[1])
    in_small = [
        pltpu.make_async_copy(src, dst, in_s.at[2 + i])
        for i, (src, dst) in enumerate(((tgt_hbm, tgt), (wgt_hbm, wgt), (gain, gg4.at[t])))
    ]
    in_head.start()
    in_hid.start()
    for cp in in_small:
        cp.start()
    oth = pl.multiple_of((1 - xl) * 512, 512)
    own = pl.multiple_of(xl * 512, 512)
    in_head.wait()
    hb[z, y, xl] = hin[:, pl.ds(own, 512)]
    pl.semaphore_wait(barrier, len(partners))

    sent = [0, 0, 0]
    GATHER_S, SEND_S, X_S = range(3)

    def rc(src, dst, ss, rs, to):
        return pltpu.make_async_remote_copy(
            src_ref=src, dst_ref=dst, send_sem=ss, recv_sem=rs, device_id=to, device_id_type=MESH
        )

    def send(src, dst, group, rs, to):
        rc(src, dst, send_s.at[group], rs, to).start()
        size = jnp.dtype(src.dtype).itemsize
        for n in src.shape:
            size *= n
        sent[group] += size

    def got(dst, rs):
        rc(dst, dst, rs, rs, at_y(1)).wait_recv()

    def b_hop(s, d, k):
        yk = y if k == 0 else ywas(k - 1)
        ref = hb.at[zz(-SZ[s] * d), yk, xl]
        send(ref, ref, GATHER_S, bz_r.at[s, d, k], at_z(SZ[s]))

    def a_hop(s, d):
        ref = hb.at[zz(-SZ[s] * d), y, 1 - xl]
        send(ref, ref, GATHER_S, az_r.at[s, d], at_z(SZ[s]))

    def a_out(k):
        ref = hb.at[zz(k), y, 1 - xl]
        for j in range(3):
            send(ref, ref, GATHER_S, ay_r.at[k], at_y(DY[j]))

    def ywas(j):
        return yy(-DY[j])

    def limit(s, k):
        if k < 0:
            return 4 if s == 0 else 3
        return 4 if (k < 2) == (s == 0) else 3

    def ring_limit(s):
        return 4 if s == 0 else 3

    send(hin.at[:, pl.ds(oth, 512)], hb.at[z, y, xl], GATHER_S, xh_r, mate)
    def b_out(j):
        ref = hb.at[z, y, xl]
        send(ref, ref, GATHER_S, by_r.at[j], at_y(DY[j]))

    b_out(0)
    b_out(1)
    for s in range(2):
        b_hop(s, 0, 0)
    for cp in in_small:
        cp.wait()
    tw[xl, 0:2, :] = tgt[...].astype(F32)
    tw[xl, 2:4, :] = wgt[...].astype(F32)
    send(tw.at[xl], tw.at[xl], GATHER_S, tw_r, mate)
    GP = ((0, 1), (2, 0), (2, 1))
    for i, (dx, dc) in enumerate(GP):
        send(gg4.at[t], gg4.at[t], GATHER_S, gn_r, at_x(dx, dc))
    in_hid.wait()
    for i, dx, dc in ((3, 0, 1), (0, 1, 0), (1, 3, 0)):
        send(xg.at[xl, t], xg.at[xl, t], GATHER_S, hx_r.at[i], at_x(dx, dc))

    def ssq_block(xl_, t_):
        def step(i, carry):
            rows = pl.ds(pl.multiple_of(i * 32, 32), 32)
            v = xg[xl_, t_, rows, :].astype(F32)
            v = v * v
            acc = v[:, 0:128]
            for k in range(1, 8):
                acc = acc + v[:, k * 128:(k + 1) * 128]
            ssq[xl_, rows, :] += acc
            return carry
        lax.fori_loop(0, 8, step, 0, unroll=4)

    def col(row):
        return jnp.transpose(jnp.broadcast_to(row, (128, 128)))

    ssq[...] = jnp.zeros_like(ssq)
    ssq_block(xl, t)

    def tokens():
        got(tw.at[1 - xl], tw_r)
        tsum[...] = jnp.zeros_like(tsum)
        tsum[0:2, :] = tw[0, 2:4, :] + tw[1, 2:4, :]
        for j in range(3):
            send(tsum, tot_y.at[j], SEND_S, ty_r, at_y(DY[j]))
        for a in range(2):
            for k in range(2):
                tgtb[a, k * 128:(k + 1) * 128, :] = col(tw[a, k:k + 1, :])
                wb[a, k * 128:(k + 1) * 128, :] = col(tw[a, 2 + k:3 + k, :])

    def t_hop(src, s, d):
        send(src, tot_z.at[s, d], SEND_S, tz_r.at[s, d], at_z(SZ[s]))

    def do_ty():
        got(tot_y, ty_r)
        tsum2[...] = tsum[...] + tot_y[0] + tot_y[1] + tot_y[2]
        for s in range(2):
            t_hop(tsum2, s, 0)

    def do_tz(d):
        for s in range(2):
            if d <= ring_limit(s):
                got(tot_z.at[s, d - 1], tz_r.at[s, d - 1])
                if d < ring_limit(s):
                    t_hop(tot_z.at[s, d - 1], s, d)

    def do_xe():
        got(hb.at[z, y, 1 - xl], xh_r)
        a_hop(0, 0)
        a_hop(1, 0)
        b_out(2)
        a_out(0)

    def do_by(k):
        got(hb.at[z, ywas(k - 1), xl], by_r.at[k - 1])
        for s in range(2):
            b_hop(s, 0, k)

    def do_az(s, d):
        got(hb.at[zz(-SZ[s] * d), y, 1 - xl], az_r.at[s, d - 1])
        if d < limit(s, -1):
            a_hop(s, d)
        a_out((-SZ[s] * d) % 8)

    def do_bz(s, d, k):
        yk = y if k == 0 else ywas(k - 1)
        got(hb.at[zz(-SZ[s] * d), yk, xl], bz_r.at[s, d - 1, k])
        if d < limit(s, k):
            b_hop(s, d, k)

    def rows_of(i):
        return slice(i * 128, (i + 1) * 128)

    XD = (1, 3, 2)

    def xblock(i):
        xs = (x - XD[i] + 4) % 4
        return xs % 2, (xs // 2) * 2

    def do_xf(i):
        a, b = xblock(i)
        ref = xg.at[a, b + c]
        if i < 2:
            got(ref, hx_r.at[i])
            part = xg.at[a, b + c, rows_of(i)]
            send(part, part, GATHER_S, hh_r.at[i], at_x((1, 3)[i]))
        else:
            for h in range(2):
                got(xg.at[a, b + c, rows_of(h)], hh_r.at[h])
        send(ref, ref, GATHER_S, hf_r.at[i], at_x(0, 1))
        ssq_block(a, b + c)

    def do_xs(i):
        a, b = xblock(i)
        got(xg.at[a, b + 1 - c], hf_r.at[i])
        ssq_block(a, b + 1 - c)

    def do_xo():
        got(xg.at[xl, xh * 2 + 1 - c], hx_r.at[3])
        ssq_block(xl, xh * 2 + 1 - c)
        got(gg4.at[0:3], gn_r)

    def half(h):
        return (xl + h) % 2

    def do_iv(h):
        a = half(h)
        s_ = jnp.sum(ssq[a], axis=1, keepdims=True)
        invb[a] = jnp.broadcast_to(lax.rsqrt(s_ * (1.0 / D) + EPS), (256, 128))

    def do_nm(h, zb):
        a = half(h)
        t0 = zb // 4
        off = (zb % 4) * 256

        def step(i, carry):
            rows = pl.ds(pl.multiple_of(i * 32, 32), 32)
            out = pl.ds(pl.multiple_of(a * 256 + i * 32, 32), 32)
            inv = invb[a, rows, :]
            low = lax.broadcasted_iota(jnp.int32, (32, 128), 1) < 64
            for p in range(2):
                cols = slice(off + p * 128, off + (p + 1) * 128)
                u = xg[a, t0, rows, cols].astype(F32) * inv * gg4[t0, :, cols]
                v = xg[a, t0 + 2, rows, cols].astype(F32) * inv * gg4[t0 + 2, :, cols]
                ur = pltpu.roll(u, 64, 1)
                vr = pltpu.roll(v, 64, 1)
                nm[zb, out, (2 * p) * 128:(2 * p + 1) * 128] = jnp.where(low, u, vr).astype(BF16)
                nm[zb, out, (2 * p + 1) * 128:(2 * p + 2) * 128] = jnp.where(low, ur, v).astype(BF16)
            return carry
        lax.fori_loop(0, 8, step, 0, unroll=4)

    def do_lg(k):
        got(hb.at[0:3, 0, 0], ay_r.at[k])
        part = jnp.dot(nm[zz(k)], hb[zz(k)].reshape(512, 512), preferred_element_type=F32)
        if k == 0:
            lg[...] = part
        else:
            lg[...] += part

    steps = dict(
        xe=do_xe, by=do_by, az=do_az, bz=do_bz, xf=do_xf, xs=do_xs, xo=do_xo,
        iv=do_iv, nm=do_nm, lg=do_lg, ty=do_ty, tz=do_tz,
    )
    tokens_done = False
    for name, *arg in GATHER:
        steps[name](*arg)
        if name == "by" and not tokens_done:
            tokens_done = True
            tokens()

    col0 = (t * 1024 + xl * 512).astype(F32)
    me = x * 2 + c

    def stat_step(i, carry):
        rows = pl.ds(pl.multiple_of(i * 32, 32), 32)
        l = lg[rows, :]
        m = jnp.max(l, axis=1, keepdims=True)
        ev = jnp.exp(l - m)
        ex[rows, :] = ev
        e = jnp.sum(ev, axis=1, keepdims=True)
        lane = lax.broadcasted_iota(jnp.int32, (32, 128), 1)
        stat[rows, :] = jnp.where(lane == 0, m, jnp.where(lane == 1, e, 0.0))
        return carry

    lax.fori_loop(0, 16, stat_step, 0, unroll=4)
    for k in range(4):
        st[me, k] = jnp.transpose(stat[k * 128:(k + 1) * 128, :])[0:8, :]
    for i, (dx, dc) in enumerate(PEERS):
        send(st.at[me], st.at[me], SEND_S, st_r, at_x(dx, dc))

    def pick_step(i, carry):
        rows = pl.ds(pl.multiple_of(i * 32, 32), 32)
        a = i // 8
        tb = tgtb[a, pl.ds(pl.multiple_of((i % 8) * 32, 32), 32), :][:, 0:1] - col0
        cols = lax.broadcasted_iota(jnp.int32, (32, 512), 1).astype(F32)
        pk = jnp.sum(jnp.where(cols == tb, lg[rows, :], 0.0), axis=1, keepdims=True)
        pick[rows, :] = jnp.broadcast_to(pk, (32, 128))
        return carry

    lax.fori_loop(0, 16, pick_step, 0, unroll=4)
    got(st.at[0:7], st_r)
    allst = st[...]
    mx = jnp.max(allst[:, :, 0:1, :], axis=0)
    es = jnp.sum(allst[:, :, 1:2, :] * jnp.exp(allst[:, :, 0:1, :] - mx[None]), axis=0)
    lse = mx + jnp.log(es)
    lser[...] = lse
    for k in range(4):
        lseb[k * 128:(k + 1) * 128, :] = col(lse[k])

    def dl_step(i, carry):
        a = i // 8
        rows = pl.ds(pl.multiple_of((i % 8) * 32, 32), 32)
        g = pl.ds(pl.multiple_of(i * 32, 32), 32)
        tb = tgtb[a, rows, :][:, 0:1] - col0
        w = wb[a, rows, :][:, 0:1]
        cols = lax.broadcasted_iota(jnp.int32, (32, 512), 1).astype(F32)
        p = ex[g, :] * jnp.exp(stat[g, :][:, 0:1] - lseb[g, :][:, 0:1])
        d = (w * (p - jnp.where(cols == tb, 1.0, 0.0))).astype(BF16)
        dl[a, rows, :] = d
        return carry

    lax.fori_loop(0, 16, dl_step, 0, unroll=4)
    for a in range(2):
        dlt[:, a * 256:(a + 1) * 256] = jnp.transpose(dl[a])

    def do_qs():
        def step(i, carry):
            a = i // 8
            g = pl.ds(pl.multiple_of(i * 32, 32), 32)
            d = dl[a, pl.ds(pl.multiple_of((i % 8) * 32, 32), 32), :]
            q = jnp.sum(d.astype(F32) * lg[g, :], axis=1, keepdims=True)
            lane = lax.broadcasted_iota(jnp.int32, (32, 128), 1)
            stat[g, :] = jnp.where(lane == 0, q, pick[g, :])
            return carry
        lax.fori_loop(0, 16, step, 0, unroll=4)
        for k in range(4):
            qt[me, k] = jnp.transpose(stat[k * 128:(k + 1) * 128, :])[0:8, :]
        for i, (dx, dc) in enumerate(PEERS):
            send(qt.at[me], qt.at[me], SEND_S, qt_r, at_x(dx, dc))

    def a_rows(k, b, h):
        return pl.ds(pl.multiple_of((k * 4 + b) * 512 + h * 160, 32), 160)

    Q_AT = (384, 448, 320)

    def b_rows(k, q):
        first = Q_AT[q]
        return [ght[(k * 4 + b) * 512 + first:(k * 4 + b) * 512 + first + 64, :] for b in range(4)]

    def do_hg(k):
        g = jnp.dot(dlt[...], nm[zz(k)], preferred_element_type=F32)
        for b in range(4):
            ght[(k * 4 + b) * 512:(k * 4 + b + 1) * 512, :] = g[:, b * 128:(b + 1) * 128]
        for i in range(2):
            sbf[k, i] = ght[a_rows(k, yy(2), i), :].astype(BF16)
            send(sbf.at[k, i], rbf.at[k, i], SEND_S, rf_r.at[k], at_y(DY[i]))

    def do_ai(k):
        for i in range(2):
            sba[k, i, 1 - i] = ght[a_rows(k, yy(DY[i]), 1 - i), :].astype(BF16)
            send(sba.at[k, i, 1 - i], rba.at[k, i, 1 - i], SEND_S, ra_r.at[k, 0], at_y(DY[i]))

    def do_yr(k):
        got(rbf.at[k], rf_r.at[k])
        for i in range(2):
            sba[k, i, i] = (ght[a_rows(k, yy(DY[i]), i), :] + rbf[k, i].astype(F32)).astype(BF16)
            send(sba.at[k, i, i], rba.at[k, i, i], SEND_S, ra_r.at[k, 1], at_y(DY[i]))

    def do_bc(s, d, q):
        v = b_rows((SZ[s] * d) % 8, q)
        h = slice(s * 32, (s + 1) * 32)
        if q == 2 and d == 4:
            for b in range(4):
                sb4[s, b] = v[b][h].astype(BF16)
            send(sb4.at[s], rb4.at[s], SEND_S, rb_r.at[s, q, 3], at_z(SZ[s]))
            return
        if q == 2 and d == 3:
            got(rb4.at[s], rb_r.at[s, q, 3])
            for b in range(4):
                sbb[s, q, 2, b] = v[b].astype(BF16)
                sbb[s, q, 2, b, h] = (v[b][h] + rb4[s, b].astype(F32)).astype(BF16)
        else:
            if d < (4 if q == s else 3):
                got(rbb.at[s, q, d], rb_r.at[s, q, d])
                v = [v[b] + rbb[s, q, d, b].astype(F32) for b in range(4)]
            for b in range(4):
                sbb[s, q, d - 1, b] = v[b].astype(BF16)
        send(sbb.at[s, q, d - 1], rbb.at[s, q, d - 1], SEND_S, rb_r.at[s, q, d - 1], at_z(SZ[s]))

    def a_wait(k):
        for i in range(2):
            got(rba.at[k, 0], ra_r.at[k, i])

    def a_half(k, h):
        return ght[a_rows(k, y, h), :] + rba[k, 0, h].astype(F32) + rba[k, 1, h].astype(F32)

    def a_sum(k):
        a_wait(k)
        return [a_half(k, h) for h in range(2)]

    def do_a4():
        v = a_sum(4)
        for s in range(2):
            sa4[s] = v[s].astype(BF16)
            send(sa4.at[s], ra4.at[s], SEND_S, rz_r.at[s, 3], at_z(SZ[s]))

    def do_ac(s, d):
        v = a_sum((SZ[s] * d) % 8)
        if d == 3:
            got(ra4.at[s], rz_r.at[s, 3])
            v[s] = v[s] + ra4[s].astype(F32)
            for h in range(2):
                sa3[s, h] = v[h].astype(BF16)
            send(sa3.at[s], ra3.at[s], SEND_S, rz_r.at[s, 2], at_z(SZ[s]))
            return
        got(ra3.at[s], rz_r.at[s, 2])
        for h in range(2):
            sa2[s, 1, h] = v[h] + ra3[s, h].astype(F32)
            send(sa2.at[s, 1, h], ra2.at[s, 1, h], SEND_S, rl_r.at[s, 1, h], at_z(SZ[s]))

    def do_al(h):
        for s in range(2):
            if h == 0:
                a_wait(SZ[s])
            got(ra2.at[s, 1, h], rl_r.at[s, 1, h])
            sa2[s, 0, h] = a_half(SZ[s], h) + ra2[s, 1, h]
            send(sa2.at[s, 0, h], ra2.at[s, 0, h], SEND_S, rl_r.at[s, 0, h], at_z(SZ[s]))

    XO = (2, 1, 3, 0)

    def xdest(n):
        xs = (x + XO[n]) % 4
        return xs % 2, xs // 2

    def dn_part(out, n, cc):
        a, b = xdest(n)
        for i in range(4):
            h = hb[4 * cc + i, :, b].reshape(256, 512)
            out[n, :, i * 256:(i + 1) * 256] = lax.dot_general(
                dl[a], h, (((1,), (1,)), ((), ())), preferred_element_type=F32
            )

    def do_ds(n):
        dn_part(dns, n, 1 - c)
        send(dns.at[n], dnr.at[n], X_S, dc_r.at[n], at_x(0, 1))
        dn_part(dno, n, c)

    def x_out(i):
        src = dno.at[1 + i, rows_of(i)]
        send(src, rbx.at[i], X_S, dx_r.at[i], at_x((1, 3)[i]))

    def x_one(i):
        dos[i] = dno[1 + i, rows_of(1 - i), :].astype(BF16)
        send(dos.at[i], dor.at[1 - i], X_S, do_r.at[i], at_x((1, 3)[i]))

    def do_du(n):
        got(dnr.at[n], dc_r.at[n])
        a, b = xdest(n)
        tx = b * 2 + c

        def step(i, acc):
            rows = pl.ds(pl.multiple_of(i * 16, 16), 16)
            s_ = dno[n, rows, :] + dnr[n, rows, :]
            if n == 0:
                dxs[rows, :] = s_.astype(BF16)
            else:
                dno[n, rows, :] = s_
            xv = xg[a, tx, rows, :].astype(F32) * invb[a, rows, :][:, 0:1]
            pr = s_ * xv
            return acc + pr[0:8] + pr[8:16]
        acc = lax.fori_loop(0, 16, step, jnp.zeros((8, 1024), F32), unroll=2)
        gps[b * 2 + a] = jnp.sum(acc, axis=0, keepdims=True)
        if n == 0:
            for i in range(2):
                send(dxs.at[rows_of(i)], dxr.at[i], X_S, d2_r.at[i], at_x((1, 3)[i]))
        elif n == 1:
            x_one(0)
        elif n == 2:
            x_one(1)

    def do_xr(n):
        i = n - 1
        got(dxr.at[i], d2_r.at[i])
        dno[n, rows_of(i), :] = dno[n, rows_of(i), :] + dxr[i].astype(F32)
        x_out(i)

    results = []

    def result(src, dst, i):
        cp = pltpu.make_async_copy(src, dst, out_s.at[i])
        cp.start()
        results.append(cp)

    def do_gx():
        for b in range(2):
            gxs[b] = gps[2 * b] + gps[2 * b + 1]
        for i, dx in enumerate((1, 3, 2)):
            b = ((x + dx) % 4) // 2
            send(gxs.at[b], gxr.at[i], SEND_S, gx_r, at_x(dx))

    def do_gy():
        got(gxr, gx_r)
        msg[:, 0:1024] = gxs[xh] + gxr[0] + gxr[1] + gxr[2]
        for j in range(3):
            send(msg, ary.at[j], SEND_S, gy_r, at_y(DY[j]))

    def do_gz():
        got(ary.at[0:3], gy_r)
        ary[3] = msg[...] + ary[0] + ary[1] + ary[2]
        for d in range(1, 8):
            send(ary.at[3], arz.at[d - 1], SEND_S, gz_r, at_z(d))

    def total_inverse():
        tot = tsum2[...]
        for s in range(2):
            for d in range(ring_limit(s)):
                tot = tot + tot_z[s, d]
        return 1.0 / jnp.sum(jnp.sum(tot, axis=1, keepdims=True), axis=0, keepdims=True)

    def do_gf():
        got(arz, gz_r)
        g = ary[3]
        for d in range(7):
            g = g + arz[d]
        o_gg[...] = g[:, 0:1024] * inv_total
        o_loss[...] = jnp.sum(g[:, 1024:1152], axis=1, keepdims=True) * inv_total
        result(o_loss, r_loss, 0)
        result(o_gg, r_gg, 1)

    def do_qt():
        got(qt.at[0:7], qt_r)
        qsum = qt[0]
        for i in range(1, 8):
            qsum = qsum + qt[i]
        loss_row = jnp.zeros((1, 128), F32)
        for k in range(4):
            loss_row = loss_row + tw[k // 2, 2 + k % 2:3 + k % 2, :] * (lser[k] - qsum[k, 1:2, :])
            lseb[k * 128:(k + 1) * 128, :] = col(qsum[k, 0:1, :])
        msg[:, 1024:1152] = loss_row

    PARTS = tuple(slice(i * 128, (i + 1) * 128) for i in range(4))

    def turn(i, v):
        ft = jnp.transpose(v)
        for a in range(2):
            ghs[a, :, PARTS[i]] = ft[a * 64:(a + 1) * 64]
        send(ghs.at[1 - xl, :, PARTS[i]], ghr.at[:, PARTS[i]], SEND_S, fx_r.at[i], mate)

    def do_af(h):
        if h == 0:
            a_wait(0)
        v = a_half(0, h)
        for s in range(2):
            got(ra2.at[s, 0, h], rl_r.at[s, 0, h])
            v = v + ra2[s, 0, h]
        fa[h * 160:(h + 1) * 160, :] = v
        turn(h, fa[h * 128:(h + 1) * 128, :])

    def do_bf(q):
        v = b_rows(0, q)
        for s in range(2):
            got(rbb.at[s, q, 0], rb_r.at[s, q, 0])
            v = [v[b] + rbb[s, q, 0, b].astype(F32) for b in range(4)]
        for b in range(4):
            syb[q, b] = v[b]
        for j in range(3):
            src = syb.at[q, yy(DY[j])]
            send(src, ryb.at[q, j], SEND_S, ry_r.at[q], at_y(DY[j]))

    def b_sum(q):
        v = syb[q, y]
        got(ryb.at[q], ry_r.at[q])
        for j in range(3):
            v = v + ryb[q, j]
        return v

    def do_bg():
        for q in range(2):
            fb[q * 64:(q + 1) * 64, :] = b_sum(q)
        turn(3, fb[...])

    def do_bm():
        fa[320:384, :] = b_sum(2)
        turn(2, fa[256:384, :])

    def do_gh():
        o_gh[:, pl.ds(own, 512)] = ghs[xl] * inv_total
        for i in range(4):
            got(ghr.at[:, PARTS[i]], fx_r.at[i])
        o_gh[:, pl.ds(oth, 512)] = ghr[...] * inv_total
        result(o_gh, r_gh, 2)

    def do_fi():
        for i in range(2):
            got(rbx.at[i], dx_r.at[i])
            got(dor.at[1 - i], do_r.at[i])
        gt = gg4[t]

        def fin(i, carry):
            rows = pl.ds(pl.multiple_of(i * 16, 16), 16)
            qrow = pl.ds(pl.multiple_of(xl * 256 + i * 16, 16), 16)
            h = i // 8
            half_rows = pl.ds(pl.multiple_of((i % 8) * 16, 16), 16)
            dn = dno[3, rows, :] + rbx[h, half_rows, :] + dor[h, half_rows, :].astype(F32)
            inv = invb[xl, rows, :][:, 0:1]
            q = lseb[qrow, :][:, 0:1]
            xv = xg[xl, t, rows, :].astype(F32)
            u = inv * inv_total
            o_hid[rows, :] = (dn * gt * u - xv * (inv * u * q * (1.0 / D))).astype(BF16)
            return carry

        lax.fori_loop(0, 16, fin, 0, unroll=2)
        result(o_hid, r_hid, 3)

    steps = dict(
        ds=do_ds, hg=do_hg, bc=do_bc, du=do_du, a4=do_a4, ac=do_ac, xr=do_xr, gy=do_gy, gz=do_gz,
        gx=do_gx, gf=do_gf, qs=do_qs, qt=do_qt, tz=do_tz, yr=do_yr, ai=do_ai, al=do_al, af=do_af, bf=do_bf, bg=do_bg, bm=do_bm, gh=do_gh, fi=do_fi,
    )
    for name, *arg in SCATTER:
        steps[name](*arg)
        if name == "tz" and arg[0] == 4:
            inv_total = total_inverse()
    for group, size in enumerate(sent):
        whole = ght.at[pl.ds(0, size // 512)]
        rc(whole, whole, send_s.at[group], send_s.at[group], at_y(1)).wait_send()
    for cp in results:
        cp.wait()


def finish(*refs):
    copies = [pltpu.make_async_copy(refs[i], refs[4 + i], refs[8].at[i]) for i in range(4)]
    for cp in copies:
        cp.start()
    for cp in copies:
        cp.wait()


def body(hidden, gain, head, targets, row_weight):
    V = pltpu.VMEM
    S = pltpu.SemaphoreType.DMA
    hbm = pl.BlockSpec(memory_space=pl.ANY)
    scratch = [
        V((2, 128), jnp.int32),
        V((2, 128), jnp.int32),
        V((1, 1), F32),
        V((64, 1024), F32),
        V((1, 1024), F32),
        V((256, 1024), BF16),
        V((64, 1024), BF16),
        V((8, 4, 2, 64, 512), BF16),
        V((2, 4, 256, 1024), BF16),
        V((8, 512, 512), BF16),
        V((4, 1, 1024), F32),
        V((2, 8, 128), F32),
        V((2, 256, 128), F32),
        V((2, 256, 128), F32),
        V((2, 256, 128), F32),
        V((2, 256, 128), F32),
        V((512, 512), F32),
        V((512, 512), F32),
        V((2, 256, 512), BF16),
        V((512, 512), BF16),
        V((8, 4, 8, 128), F32),
        V((8, 4, 8, 128), F32),
        V((512, 128), F32),
        V((512, 128), F32),
        V((512, 128), F32),
        V((4, 1, 128), F32),
        V((16384, 128), F32),
        V((8, 2, 160, 128), BF16),
        V((8, 2, 160, 128), BF16),
        V((8, 2, 2, 160, 128), BF16),
        V((8, 2, 2, 160, 128), BF16),
        V((2, 160, 128), BF16),
        V((2, 160, 128), BF16),
        V((2, 2, 160, 128), BF16),
        V((2, 2, 160, 128), BF16),
        V((2, 2, 2, 160, 128), F32),
        V((2, 2, 2, 160, 128), F32),
        V((2, 4, 32, 128), BF16),
        V((2, 4, 32, 128), BF16),
        V((2, 3, 4, 4, 64, 128), BF16),
        V((2, 3, 4, 4, 64, 128), BF16),
        V((3, 4, 64, 128), F32),
        V((3, 3, 64, 128), F32),
        V((384, 128), F32),
        V((128, 128), F32),
        V((2, 64, 512), F32),
        V((64, 512), F32),
        V((4, 256, 1024), F32),
        V((4, 256, 1024), F32),
        V((4, 256, 1024), F32),
        V((256, 1024), BF16),
        V((2, 128, 1024), BF16),
        V((2, 128, 1024), BF16),
        V((2, 128, 1024), BF16),
        V((2, 128, 1024), F32),
        V((4, 1, 1024), F32),
        V((2, 1, 1024), F32),
        V((3, 1, 1024), F32),
        V((1, 1152), F32),
        V((4, 1, 1152), F32),
        V((7, 1, 1152), F32),
        V((8, 128), F32),
        V((8, 128), F32),
        V((3, 8, 128), F32),
        V((2, 4, 8, 128), F32),
        S((5,)),
        S((4,)),
        S((3,)),
    ]
    shapes = [
        (), (), (), (4,), (2,), (3,), (2, 4), (8,), (3,), (2, 4, 4),
        (), (), (), (2, 4), (8,), (8, 2), (2, 4), (2, 2, 2), (2, 3, 4), (3,), (4,),
        (4,), (2,), (2,), (2,), (), (), (),
    ]
    scratch += [S(sh) if sh else S for sh in shapes]
    loss, gh, gg, gx = pl.pallas_call(
        kernel,
        out_shape=(
            jax.ShapeDtypeStruct((1, 1), F32),
            jax.ShapeDtypeStruct((64, 1024), F32),
            jax.ShapeDtypeStruct((1, 1024), F32),
            jax.ShapeDtypeStruct((256, 1024), BF16),
        ),
        in_specs=[pl.BlockSpec(memory_space=pltpu.HBM)] * 5,
        out_specs=(hbm,) * 4,
        scratch_shapes=scratch,
        compiler_params=pltpu.CompilerParams(
            collective_id=0, has_side_effects=True, vmem_limit_bytes=53 << 20
        ),
    )(*[
        pltpu.with_memory_space_constraint(a, pltpu.HBM)
        for a in (hidden, gain.reshape(1, 1024), head, targets.reshape(2, 128), row_weight.reshape(2, 128))
    ])
    loss, gh, gg, gx = pl.pallas_call(
        finish,
        out_shape=tuple(jax.ShapeDtypeStruct(a.shape, a.dtype) for a in (loss, gh, gg, gx)),
        in_specs=[hbm] * 4,
        out_specs=(hbm,) * 4,
        scratch_shapes=[S((4,))],
        compiler_params=pltpu.CompilerParams(vmem_limit_bytes=2 << 20),
    )(loss, gh, gg, gx)
    return (loss.reshape(()), gh, gg.reshape(1024), gx)


def solution(mesh):
    in_specs = (P("fsdp", "tp"), P("tp"), P("fsdp", "tp"), P("fsdp"), P("fsdp"))
    out_specs = (P(), P("fsdp", "tp"), P("tp"), P("fsdp", "tp"))
    return jax.shard_map(body, mesh=mesh, in_specs=in_specs, out_specs=out_specs, check_vma=False)
```

```python
import functools

import jax
import jax.numpy as jnp
from jax import lax
from jax.experimental import pallas as pl
from jax.experimental.pallas import tpu as pltpu
from jax.sharding import PartitionSpec as P

D = 4096
EPS = 1e-05
MESH = pl.DeviceIdType.MESH
F32 = jnp.float32
BF16 = jnp.bfloat16

DY = (1, 3, 2)
SZ = (1, 7)
PEERS = ((1, 0), (3, 0), (2, 0), (0, 1), (1, 1), (3, 1), (2, 1))
GATHER = (
    ("xe",), ("by", 1), ("bz", 0, 1, 0), ("bz", 1, 1, 0), ("az", 0, 1), ("az", 1, 1), ("by", 2), ("xo",),
    ("bz", 0, 1, 1), ("bz", 1, 1, 1), ("bz", 0, 2, 0), ("bz", 1, 2, 0), ("az", 0, 2), ("az", 1, 2), ("by", 3),
    ("xf", 1), ("xf", 0), ("bz", 0, 1, 2), ("bz", 1, 1, 2), ("bz", 0, 2, 1), ("bz", 1, 2, 1), ("ty",),
    ("bz", 0, 3, 0), ("bz", 1, 3, 0), ("az", 0, 3), ("az", 1, 3), ("xs", 1), ("xs", 0), ("iv", 1), ("bz", 0, 1, 3),
    ("bz", 1, 1, 3), ("nm", 1, 0), ("nm", 1, 1), ("nm", 1, 2), ("bz", 0, 2, 2), ("bz", 1, 2, 2), ("nm", 1, 3),
    ("nm", 1, 4), ("xf", 2), ("bz", 0, 3, 1), ("bz", 1, 3, 1), ("nm", 1, 5), ("nm", 1, 6), ("tz", 1), ("bz", 0, 4, 0),
    ("bz", 1, 2, 3), ("nm", 1, 7), ("az", 0, 4), ("xs", 2), ("iv", 0), ("nm", 0, 0), ("nm", 0, 1), ("bz", 1, 3, 2),
    ("nm", 0, 2), ("nm", 0, 3), ("bz", 0, 2, 3), ("nm", 0, 4), ("bz", 1, 3, 3), ("nm", 0, 5), ("nm", 0, 6),
    ("nm", 0, 7), ("lg", 0), ("lg", 7), ("lg", 1), ("lg", 6), ("lg", 2), ("lg", 3), ("bz", 0, 3, 2), ("bz", 0, 3, 3),
    ("tz", 2), ("lg", 5), ("bz", 1, 4, 2), ("bz", 0, 4, 1), ("bz", 1, 4, 3), ("lg", 4),
)
SCATTER = (
    ("hg", 4), ("ai", 4), ("bc", 0, 4, 0), ("bc", 1, 4, 1), ("hg", 3), ("ai", 3), ("bc", 0, 3, 1), ("ds", 0),
    ("tz", 3), ("hg", 5), ("ai", 5), ("bc", 1, 3, 0), ("bc", 0, 4, 2), ("bc", 1, 4, 2), ("ds", 1), ("du", 0),
    ("ds", 2), ("yr", 4), ("bc", 0, 3, 0), ("bc", 1, 3, 1), ("hg", 2), ("ai", 2), ("yr", 3), ("du", 1),
    ("bc", 0, 2, 1), ("hg", 6), ("ai", 6), ("yr", 5), ("bc", 1, 2, 0), ("bc", 0, 3, 2), ("bc", 1, 3, 2), ("ds", 3),
    ("tz", 4), ("a4",), ("du", 2), ("hg", 1), ("ai", 1), ("bc", 0, 2, 0), ("bc", 1, 2, 1), ("hg", 7), ("ai", 7),
    ("du", 3), ("yr", 2), ("gx",), ("qs",), ("bc", 0, 1, 1), ("bc", 1, 1, 0), ("xr", 1), ("xr", 2), ("yr", 6),
    ("ac", 0, 3), ("ac", 1, 3), ("hg", 0), ("ai", 0), ("bc", 0, 2, 2), ("bc", 1, 2, 2), ("bc", 0, 1, 0),
    ("bc", 1, 1, 1), ("yr", 1), ("yr", 7), ("ac", 0, 2), ("ac", 1, 2), ("bc", 0, 1, 2), ("bc", 1, 1, 2), ("yr", 0),
    ("qt",), ("gy",), ("bf", 0), ("bf", 1), ("al", 0), ("al", 1), ("bf", 2), ("gz",), ("bg",), ("af", 0), ("af", 1),
    ("bm",), ("fi",), ("gf",), ("gh",),
)


def kernel(
    hid, gain, hin_hbm, tgt_hbm, wgt_hbm,
    r_loss, r_gh, r_gg, r_hid,
    tgt, wgt, o_loss, o_gh, o_gg, o_hid, hin, hb, xg, nm, gg4, tw, ssq, invb, tgtb, wb, lg, ex, dl, dlt,
    st, qt, lseb, stat, pick, lser,
    ght, sbf, rbf, sba, rba, sa4, ra4, sa3, ra3, sa2, ra2, sb4, rb4, sbb, rbb, syb, ryb, fa, fb, ghs, ghr,
    dno, dns, dnr, dxs, dxr, dos, dor, rbx, gps, gxs, gxr, msg, ary, arz, tsum, tsum2, tot_y, tot_z,
    in_s, out_s, send_s,
    xh_r, tw_r, gn_r, hx_r, hh_r, hf_r, az_r, ay_r, by_r, bz_r, st_r, qt_r, ty_r, tz_r,
    rf_r, ra_r, rz_r, rl_r, rb_r, ry_r, fx_r, dc_r, d2_r, dx_r, do_r, gx_r, gy_r, gz_r,
):
    f = lax.axis_index("fsdp")
    t = lax.axis_index("tp")
    xl = f // 32
    z = (f // 4) % 8
    y = f % 4
    xh = t // 2
    c = t % 2
    x = xh * 2 + xl

    def dev(x_, y_, z_, c_):
        return (((x_ % 2) * 8 + z_) * 4 + y_, (x_ // 2) * 2 + c_)

    def at_x(dx, dc=0):
        return dev((x + dx) % 4, y, z, (c + dc) % 2)

    def at_y(dy):
        return dev(x, (y + dy) % 4, z, c)

    def at_z(dz):
        return dev(x, y, (z + dz) % 8, c)

    mate = dev(xh * 2 + (1 - xl), y, z, c)

    def yy(k):
        return (y + k) % 4

    def zz(k):
        return (z + k) % 8

    partners = [at_x(dx, dc) for dx, dc in PEERS] + [at_y(d) for d in DY] + [at_z(d) for d in SZ]
    barrier = pltpu.get_barrier_semaphore()
    for p in partners:
        pl.semaphore_signal(barrier, inc=1, device_id=p, device_id_type=MESH)
    in_hid = pltpu.make_async_copy(hid, xg.at[xl, t], in_s.at[0])
    in_head = pltpu.make_async_copy(hin_hbm, hin, in_s.at[1])
    in_small = [
        pltpu.make_async_copy(src, dst, in_s.at[2 + i])
        for i, (src, dst) in enumerate(((tgt_hbm, tgt), (wgt_hbm, wgt), (gain, gg4.at[t])))
    ]
    in_head.start()
    in_hid.start()
    for cp in in_small:
        cp.start()
    oth = pl.multiple_of((1 - xl) * 512, 512)
    own = pl.multiple_of(xl * 512, 512)
    in_head.wait()
    hb[z, y, xl] = hin[:, pl.ds(own, 512)]
    pl.semaphore_wait(barrier, len(partners))

    sent = [0, 0, 0]
    GATHER_S, SEND_S, X_S = range(3)

    def rc(src, dst, ss, rs, to):
        return pltpu.make_async_remote_copy(
            src_ref=src, dst_ref=dst, send_sem=ss, recv_sem=rs, device_id=to, device_id_type=MESH
        )

    def send(src, dst, group, rs, to):
        rc(src, dst, send_s.at[group], rs, to).start()
        size = jnp.dtype(src.dtype).itemsize
        for n in src.shape:
            size *= n
        sent[group] += size

    def got(dst, rs):
        rc(dst, dst, rs, rs, at_y(1)).wait_recv()

    def b_hop(s, d, k):
        yk = y if k == 0 else ywas(k - 1)
        ref = hb.at[zz(-SZ[s] * d), yk, xl]
        send(ref, ref, GATHER_S, bz_r.at[s, d, k], at_z(SZ[s]))

    def a_hop(s, d):
        ref = hb.at[zz(-SZ[s] * d), y, 1 - xl]
        send(ref, ref, GATHER_S, az_r.at[s, d], at_z(SZ[s]))

    def a_out(k):
        ref = hb.at[zz(k), y, 1 - xl]
        for j in range(3):
            send(ref, ref, GATHER_S, ay_r.at[k], at_y(DY[j]))

    def ywas(j):
        return yy(-DY[j])

    def limit(s, k):
        if k < 0:
            return 4 if s == 0 else 3
        return 4 if (k < 2) == (s == 0) else 3

    def ring_limit(s):
        return 4 if s == 0 else 3

    send(hin.at[:, pl.ds(oth, 512)], hb.at[z, y, xl], GATHER_S, xh_r, mate)
    def b_out(j):
        ref = hb.at[z, y, xl]
        send(ref, ref, GATHER_S, by_r.at[j], at_y(DY[j]))

    b_out(0)
    b_out(1)
    for s in range(2):
        b_hop(s, 0, 0)
    for cp in in_small:
        cp.wait()
    tw[xl, 0:2, :] = tgt[...].astype(F32)
    tw[xl, 2:4, :] = wgt[...].astype(F32)
    send(tw.at[xl], tw.at[xl], GATHER_S, tw_r, mate)
    GP = ((0, 1), (2, 0), (2, 1))
    for i, (dx, dc) in enumerate(GP):
        send(gg4.at[t], gg4.at[t], GATHER_S, gn_r, at_x(dx, dc))
    in_hid.wait()
    for i, dx, dc in ((3, 0, 1), (0, 1, 0), (1, 3, 0)):
        send(xg.at[xl, t], xg.at[xl, t], GATHER_S, hx_r.at[i], at_x(dx, dc))

    def ssq_block(xl_, t_):
        def step(i, carry):
            rows = pl.ds(pl.multiple_of(i * 32, 32), 32)
            v = xg[xl_, t_, rows, :].astype(F32)
            v = v * v
            acc = v[:, 0:128]
            for k in range(1, 8):
                acc = acc + v[:, k * 128:(k + 1) * 128]
            ssq[xl_, rows, :] += acc
            return carry
        lax.fori_loop(0, 8, step, 0, unroll=4)

    def col(row):
        return jnp.transpose(jnp.broadcast_to(row, (128, 128)))

    ssq[...] = jnp.zeros_like(ssq)
    ssq_block(xl, t)

    def tokens():
        got(tw.at[1 - xl], tw_r)
        tsum[...] = jnp.zeros_like(tsum)
        tsum[0:2, :] = tw[0, 2:4, :] + tw[1, 2:4, :]
        for j in range(3):
            send(tsum, tot_y.at[j], SEND_S, ty_r, at_y(DY[j]))
        for a in range(2):
            for k in range(2):
                tgtb[a, k * 128:(k + 1) * 128, :] = col(tw[a, k:k + 1, :])
                wb[a, k * 128:(k + 1) * 128, :] = col(tw[a, 2 + k:3 + k, :])

    def t_hop(src, s, d):
        send(src, tot_z.at[s, d], SEND_S, tz_r.at[s, d], at_z(SZ[s]))

    def do_ty():
        got(tot_y, ty_r)
        tsum2[...] = tsum[...] + tot_y[0] + tot_y[1] + tot_y[2]
        for s in range(2):
            t_hop(tsum2, s, 0)

    def do_tz(d):
        for s in range(2):
            if d <= ring_limit(s):
                got(tot_z.at[s, d - 1], tz_r.at[s, d - 1])
                if d < ring_limit(s):
                    t_hop(tot_z.at[s, d - 1], s, d)

    def do_xe():
        got(hb.at[z, y, 1 - xl], xh_r)
        a_hop(0, 0)
        a_hop(1, 0)
        b_out(2)
        a_out(0)

    def do_by(k):
        got(hb.at[z, ywas(k - 1), xl], by_r.at[k - 1])
        for s in range(2):
            b_hop(s, 0, k)

    def do_az(s, d):
        got(hb.at[zz(-SZ[s] * d), y, 1 - xl], az_r.at[s, d - 1])
        if d < limit(s, -1):
            a_hop(s, d)
        a_out((-SZ[s] * d) % 8)

    def do_bz(s, d, k):
        yk = y if k == 0 else ywas(k - 1)
        got(hb.at[zz(-SZ[s] * d), yk, xl], bz_r.at[s, d - 1, k])
        if d < limit(s, k):
            b_hop(s, d, k)

    def rows_of(i):
        return slice(i * 128, (i + 1) * 128)

    XD = (1, 3, 2)

    def xblock(i):
        xs = (x - XD[i] + 4) % 4
        return xs % 2, (xs // 2) * 2

    def do_xf(i):
        a, b = xblock(i)
        ref = xg.at[a, b + c]
        if i < 2:
            got(ref, hx_r.at[i])
            part = xg.at[a, b + c, rows_of(i)]
            send(part, part, GATHER_S, hh_r.at[i], at_x((1, 3)[i]))
        else:
            for h in range(2):
                got(xg.at[a, b + c, rows_of(h)], hh_r.at[h])
        send(ref, ref, GATHER_S, hf_r.at[i], at_x(0, 1))
        ssq_block(a, b + c)

    def do_xs(i):
        a, b = xblock(i)
        got(xg.at[a, b + 1 - c], hf_r.at[i])
        ssq_block(a, b + 1 - c)

    def do_xo():
        got(xg.at[xl, xh * 2 + 1 - c], hx_r.at[3])
        ssq_block(xl, xh * 2 + 1 - c)
        got(gg4.at[0:3], gn_r)

    def half(h):
        return (xl + h) % 2

    def do_iv(h):
        a = half(h)
        s_ = jnp.sum(ssq[a], axis=1, keepdims=True)
        invb[a] = jnp.broadcast_to(lax.rsqrt(s_ * (1.0 / D) + EPS), (256, 128))

    def do_nm(h, zb):
        a = half(h)
        t0 = zb // 4
        off = (zb % 4) * 256

        def step(i, carry):
            rows = pl.ds(pl.multiple_of(i * 32, 32), 32)
            out = pl.ds(pl.multiple_of(a * 256 + i * 32, 32), 32)
            inv = invb[a, rows, :]
            low = lax.broadcasted_iota(jnp.int32, (32, 128), 1) < 64
            for p in range(2):
                cols = slice(off + p * 128, off + (p + 1) * 128)
                u = xg[a, t0, rows, cols].astype(F32) * inv * gg4[t0, :, cols]
                v = xg[a, t0 + 2, rows, cols].astype(F32) * inv * gg4[t0 + 2, :, cols]
                ur = pltpu.roll(u, 64, 1)
                vr = pltpu.roll(v, 64, 1)
                nm[zb, out, (2 * p) * 128:(2 * p + 1) * 128] = jnp.where(low, u, vr).astype(BF16)
                nm[zb, out, (2 * p + 1) * 128:(2 * p + 2) * 128] = jnp.where(low, ur, v).astype(BF16)
            return carry
        lax.fori_loop(0, 8, step, 0, unroll=4)

    def do_lg(k):
        got(hb.at[0:3, 0, 0], ay_r.at[k])
        part = jnp.dot(nm[zz(k)], hb[zz(k)].reshape(512, 512), preferred_element_type=F32)
        if k == 0:
            lg[...] = part
        else:
            lg[...] += part

    steps = dict(
        xe=do_xe, by=do_by, az=do_az, bz=do_bz, xf=do_xf, xs=do_xs, xo=do_xo,
        iv=do_iv, nm=do_nm, lg=do_lg, ty=do_ty, tz=do_tz,
    )
    tokens_done = False
    for name, *arg in GATHER:
        steps[name](*arg)
        if name == "by" and not tokens_done:
            tokens_done = True
            tokens()

    col0 = (t * 1024 + xl * 512).astype(F32)
    me = x * 2 + c

    def stat_step(i, carry):
        rows = pl.ds(pl.multiple_of(i * 32, 32), 32)
        l = lg[rows, :]
        m = jnp.max(l, axis=1, keepdims=True)
        ev = jnp.exp(l - m)
        ex[rows, :] = ev
        e = jnp.sum(ev, axis=1, keepdims=True)
        lane = lax.broadcasted_iota(jnp.int32, (32, 128), 1)
        stat[rows, :] = jnp.where(lane == 0, m, jnp.where(lane == 1, e, 0.0))
        return carry

    lax.fori_loop(0, 16, stat_step, 0, unroll=4)
    for k in range(4):
        st[me, k] = jnp.transpose(stat[k * 128:(k + 1) * 128, :])[0:8, :]
    for i, (dx, dc) in enumerate(PEERS):
        send(st.at[me], st.at[me], SEND_S, st_r, at_x(dx, dc))

    def pick_step(i, carry):
        rows = pl.ds(pl.multiple_of(i * 32, 32), 32)
        a = i // 8
        tb = tgtb[a, pl.ds(pl.multiple_of((i % 8) * 32, 32), 32), :][:, 0:1] - col0
        cols = lax.broadcasted_iota(jnp.int32, (32, 512), 1).astype(F32)
        pk = jnp.sum(jnp.where(cols == tb, lg[rows, :], 0.0), axis=1, keepdims=True)
        pick[rows, :] = jnp.broadcast_to(pk, (32, 128))
        return carry

    lax.fori_loop(0, 16, pick_step, 0, unroll=4)
    got(st.at[0:7], st_r)
    allst = st[...]
    mx = jnp.max(allst[:, :, 0:1, :], axis=0)
    es = jnp.sum(allst[:, :, 1:2, :] * jnp.exp(allst[:, :, 0:1, :] - mx[None]), axis=0)
    lse = mx + jnp.log(es)
    lser[...] = lse
    for k in range(4):
        lseb[k * 128:(k + 1) * 128, :] = col(lse[k])

    def dl_step(i, carry):
        a = i // 8
        rows = pl.ds(pl.multiple_of((i % 8) * 32, 32), 32)
        g = pl.ds(pl.multiple_of(i * 32, 32), 32)
        tb = tgtb[a, rows, :][:, 0:1] - col0
        w = wb[a, rows, :][:, 0:1]
        cols = lax.broadcasted_iota(jnp.int32, (32, 512), 1).astype(F32)
        p = ex[g, :] * jnp.exp(stat[g, :][:, 0:1] - lseb[g, :][:, 0:1])
        d = (w * (p - jnp.where(cols == tb, 1.0, 0.0))).astype(BF16)
        dl[a, rows, :] = d
        return carry

    lax.fori_loop(0, 16, dl_step, 0, unroll=4)
    for a in range(2):
        dlt[:, a * 256:(a + 1) * 256] = jnp.transpose(dl[a])

    def do_qs():
        def step(i, carry):
            a = i // 8
            g = pl.ds(pl.multiple_of(i * 32, 32), 32)
            d = dl[a, pl.ds(pl.multiple_of((i % 8) * 32, 32), 32), :]
            q = jnp.sum(d.astype(F32) * lg[g, :], axis=1, keepdims=True)
            lane = lax.broadcasted_iota(jnp.int32, (32, 128), 1)
            stat[g, :] = jnp.where(lane == 0, q, pick[g, :])
            return carry
        lax.fori_loop(0, 16, step, 0, unroll=4)
        for k in range(4):
            qt[me, k] = jnp.transpose(stat[k * 128:(k + 1) * 128, :])[0:8, :]
        for i, (dx, dc) in enumerate(PEERS):
            send(qt.at[me], qt.at[me], SEND_S, qt_r, at_x(dx, dc))

    def a_rows(k, b, h):
        return pl.ds(pl.multiple_of((k * 4 + b) * 512 + h * 160, 32), 160)

    Q_AT = (384, 448, 320)

    def b_rows(k, q):
        first = Q_AT[q]
        return [ght[(k * 4 + b) * 512 + first:(k * 4 + b) * 512 + first + 64, :] for b in range(4)]

    def do_hg(k):
        g = jnp.dot(dlt[...], nm[zz(k)], preferred_element_type=F32)
        for b in range(4):
            ght[(k * 4 + b) * 512:(k * 4 + b + 1) * 512, :] = g[:, b * 128:(b + 1) * 128]
        for i in range(2):
            sbf[k, i] = ght[a_rows(k, yy(2), i), :].astype(BF16)
            send(sbf.at[k, i], rbf.at[k, i], SEND_S, rf_r.at[k], at_y(DY[i]))

    def do_ai(k):
        for i in range(2):
            sba[k, i, 1 - i] = ght[a_rows(k, yy(DY[i]), 1 - i), :].astype(BF16)
            send(sba.at[k, i, 1 - i], rba.at[k, i, 1 - i], SEND_S, ra_r.at[k, 0], at_y(DY[i]))

    def do_yr(k):
        got(rbf.at[k], rf_r.at[k])
        for i in range(2):
            sba[k, i, i] = (ght[a_rows(k, yy(DY[i]), i), :] + rbf[k, i].astype(F32)).astype(BF16)
            send(sba.at[k, i, i], rba.at[k, i, i], SEND_S, ra_r.at[k, 1], at_y(DY[i]))

    def do_bc(s, d, q):
        v = b_rows((SZ[s] * d) % 8, q)
        h = slice(s * 32, (s + 1) * 32)
        if q == 2 and d == 4:
            for b in range(4):
                sb4[s, b] = v[b][h].astype(BF16)
            send(sb4.at[s], rb4.at[s], SEND_S, rb_r.at[s, q, 3], at_z(SZ[s]))
            return
        if q == 2 and d == 3:
            got(rb4.at[s], rb_r.at[s, q, 3])
            for b in range(4):
                sbb[s, q, 2, b] = v[b].astype(BF16)
                sbb[s, q, 2, b, h] = (v[b][h] + rb4[s, b].astype(F32)).astype(BF16)
        else:
            if d < (4 if q == s else 3):
                got(rbb.at[s, q, d], rb_r.at[s, q, d])
                v = [v[b] + rbb[s, q, d, b].astype(F32) for b in range(4)]
            for b in range(4):
                sbb[s, q, d - 1, b] = v[b].astype(BF16)
        send(sbb.at[s, q, d - 1], rbb.at[s, q, d - 1], SEND_S, rb_r.at[s, q, d - 1], at_z(SZ[s]))

    def a_wait(k):
        for i in range(2):
            got(rba.at[k, 0], ra_r.at[k, i])

    def a_half(k, h):
        return ght[a_rows(k, y, h), :] + rba[k, 0, h].astype(F32) + rba[k, 1, h].astype(F32)

    def a_sum(k):
        a_wait(k)
        return [a_half(k, h) for h in range(2)]

    def do_a4():
        v = a_sum(4)
        for s in range(2):
            sa4[s] = v[s].astype(BF16)
            send(sa4.at[s], ra4.at[s], SEND_S, rz_r.at[s, 3], at_z(SZ[s]))

    def do_ac(s, d):
        v = a_sum((SZ[s] * d) % 8)
        if d == 3:
            got(ra4.at[s], rz_r.at[s, 3])
            v[s] = v[s] + ra4[s].astype(F32)
            for h in range(2):
                sa3[s, h] = v[h].astype(BF16)
            send(sa3.at[s], ra3.at[s], SEND_S, rz_r.at[s, 2], at_z(SZ[s]))
            return
        got(ra3.at[s], rz_r.at[s, 2])
        for h in range(2):
            sa2[s, 1, h] = v[h] + ra3[s, h].astype(F32)
            send(sa2.at[s, 1, h], ra2.at[s, 1, h], SEND_S, rl_r.at[s, 1, h], at_z(SZ[s]))

    def do_al(h):
        for s in range(2):
            if h == 0:
                a_wait(SZ[s])
            got(ra2.at[s, 1, h], rl_r.at[s, 1, h])
            sa2[s, 0, h] = a_half(SZ[s], h) + ra2[s, 1, h]
            send(sa2.at[s, 0, h], ra2.at[s, 0, h], SEND_S, rl_r.at[s, 0, h], at_z(SZ[s]))

    XO = (2, 1, 3, 0)

    def xdest(n):
        xs = (x + XO[n]) % 4
        return xs % 2, xs // 2

    def dn_part(out, n, cc):
        a, b = xdest(n)
        for i in range(4):
            h = hb[4 * cc + i, :, b].reshape(256, 512)
            out[n, :, i * 256:(i + 1) * 256] = lax.dot_general(
                dl[a], h, (((1,), (1,)), ((), ())), preferred_element_type=F32
            )

    def do_ds(n):
        dn_part(dns, n, 1 - c)
        send(dns.at[n], dnr.at[n], X_S, dc_r.at[n], at_x(0, 1))
        dn_part(dno, n, c)

    def x_out(i):
        src = dno.at[1 + i, rows_of(i)]
        send(src, rbx.at[i], X_S, dx_r.at[i], at_x((1, 3)[i]))

    def x_one(i):
        dos[i] = dno[1 + i, rows_of(1 - i), :].astype(BF16)
        send(dos.at[i], dor.at[1 - i], X_S, do_r.at[i], at_x((1, 3)[i]))

    def do_du(n):
        got(dnr.at[n], dc_r.at[n])
        a, b = xdest(n)
        tx = b * 2 + c

        def step(i, acc):
            rows = pl.ds(pl.multiple_of(i * 16, 16), 16)
            s_ = dno[n, rows, :] + dnr[n, rows, :]
            if n == 0:
                dxs[rows, :] = s_.astype(BF16)
            else:
                dno[n, rows, :] = s_
            xv = xg[a, tx, rows, :].astype(F32) * invb[a, rows, :][:, 0:1]
            pr = s_ * xv
            return acc + pr[0:8] + pr[8:16]
        acc = lax.fori_loop(0, 16, step, jnp.zeros((8, 1024), F32), unroll=2)
        gps[b * 2 + a] = jnp.sum(acc, axis=0, keepdims=True)
        if n == 0:
            for i in range(2):
                send(dxs.at[rows_of(i)], dxr.at[i], X_S, d2_r.at[i], at_x((1, 3)[i]))
        elif n == 1:
            x_one(0)
        elif n == 2:
            x_one(1)

    def do_xr(n):
        i = n - 1
        got(dxr.at[i], d2_r.at[i])
        dno[n, rows_of(i), :] = dno[n, rows_of(i), :] + dxr[i].astype(F32)
        x_out(i)

    results = []

    def result(src, dst, i):
        cp = pltpu.make_async_copy(src, dst, out_s.at[i])
        cp.start()
        results.append(cp)

    def do_gx():
        for b in range(2):
            gxs[b] = gps[2 * b] + gps[2 * b + 1]
        for i, dx in enumerate((1, 3, 2)):
            b = ((x + dx) % 4) // 2
            send(gxs.at[b], gxr.at[i], SEND_S, gx_r, at_x(dx))

    def do_gy():
        got(gxr, gx_r)
        msg[:, 0:1024] = gxs[xh] + gxr[0] + gxr[1] + gxr[2]
        for j in range(3):
            send(msg, ary.at[j], SEND_S, gy_r, at_y(DY[j]))

    def do_gz():
        got(ary.at[0:3], gy_r)
        ary[3] = msg[...] + ary[0] + ary[1] + ary[2]
        for d in range(1, 8):
            send(ary.at[3], arz.at[d - 1], SEND_S, gz_r, at_z(d))

    def total_inverse():
        tot = tsum2[...]
        for s in range(2):
            for d in range(ring_limit(s)):
                tot = tot + tot_z[s, d]
        return 1.0 / jnp.sum(jnp.sum(tot, axis=1, keepdims=True), axis=0, keepdims=True)

    def do_gf():
        got(arz, gz_r)
        g = ary[3]
        for d in range(7):
            g = g + arz[d]
        o_gg[...] = g[:, 0:1024] * inv_total
        o_loss[...] = jnp.sum(g[:, 1024:1152], axis=1, keepdims=True) * inv_total
        result(o_loss, r_loss, 0)
        result(o_gg, r_gg, 1)

    def do_qt():
        got(qt.at[0:7], qt_r)
        qsum = qt[0]
        for i in range(1, 8):
            qsum = qsum + qt[i]
        loss_row = jnp.zeros((1, 128), F32)
        for k in range(4):
            loss_row = loss_row + tw[k // 2, 2 + k % 2:3 + k % 2, :] * (lser[k] - qsum[k, 1:2, :])
            lseb[k * 128:(k + 1) * 128, :] = col(qsum[k, 0:1, :])
        msg[:, 1024:1152] = loss_row

    PARTS = tuple(slice(i * 128, (i + 1) * 128) for i in range(4))

    def turn(i, v):
        ft = jnp.transpose(v)
        for a in range(2):
            ghs[a, :, PARTS[i]] = ft[a * 64:(a + 1) * 64]
        send(ghs.at[1 - xl, :, PARTS[i]], ghr.at[:, PARTS[i]], SEND_S, fx_r.at[i], mate)

    def do_af(h):
        if h == 0:
            a_wait(0)
        v = a_half(0, h)
        for s in range(2):
            got(ra2.at[s, 0, h], rl_r.at[s, 0, h])
            v = v + ra2[s, 0, h]
        fa[h * 160:(h + 1) * 160, :] = v
        turn(h, fa[h * 128:(h + 1) * 128, :])

    def do_bf(q):
        v = b_rows(0, q)
        for s in range(2):
            got(rbb.at[s, q, 0], rb_r.at[s, q, 0])
            v = [v[b] + rbb[s, q, 0, b].astype(F32) for b in range(4)]
        for b in range(4):
            syb[q, b] = v[b]
        for j in range(3):
            src = syb.at[q, yy(DY[j])]
            send(src, ryb.at[q, j], SEND_S, ry_r.at[q], at_y(DY[j]))

    def b_sum(q):
        v = syb[q, y]
        got(ryb.at[q], ry_r.at[q])
        for j in range(3):
            v = v + ryb[q, j]
        return v

    def do_bg():
        for q in range(2):
            fb[q * 64:(q + 1) * 64, :] = b_sum(q)
        turn(3, fb[...])

    def do_bm():
        fa[320:384, :] = b_sum(2)
        turn(2, fa[256:384, :])

    def do_gh():
        o_gh[:, pl.ds(own, 512)] = ghs[xl] * inv_total
        for i in range(4):
            got(ghr.at[:, PARTS[i]], fx_r.at[i])
        o_gh[:, pl.ds(oth, 512)] = ghr[...] * inv_total
        result(o_gh, r_gh, 2)

    def do_fi():
        for i in range(2):
            got(rbx.at[i], dx_r.at[i])
            got(dor.at[1 - i], do_r.at[i])
        gt = gg4[t]

        def fin(i, carry):
            rows = pl.ds(pl.multiple_of(i * 16, 16), 16)
            qrow = pl.ds(pl.multiple_of(xl * 256 + i * 16, 16), 16)
            h = i // 8
            half_rows = pl.ds(pl.multiple_of((i % 8) * 16, 16), 16)
            dn = dno[3, rows, :] + rbx[h, half_rows, :] + dor[h, half_rows, :].astype(F32)
            inv = invb[xl, rows, :][:, 0:1]
            q = lseb[qrow, :][:, 0:1]
            xv = xg[xl, t, rows, :].astype(F32)
            u = inv * inv_total
            o_hid[rows, :] = (dn * gt * u - xv * (inv * u * q * (1.0 / D))).astype(BF16)
            return carry

        lax.fori_loop(0, 16, fin, 0, unroll=2)
        result(o_hid, r_hid, 3)

    steps = dict(
        ds=do_ds, hg=do_hg, bc=do_bc, du=do_du, a4=do_a4, ac=do_ac, xr=do_xr, gy=do_gy, gz=do_gz,
        gx=do_gx, gf=do_gf, qs=do_qs, qt=do_qt, tz=do_tz, yr=do_yr, ai=do_ai, al=do_al, af=do_af, bf=do_bf, bg=do_bg, bm=do_bm, gh=do_gh, fi=do_fi,
    )
    for name, *arg in SCATTER:
        steps[name](*arg)
        if name == "tz" and arg[0] == 4:
            inv_total = total_inverse()
    for group, size in enumerate(sent):
        whole = ght.at[pl.ds(0, size // 512)]
        rc(whole, whole, send_s.at[group], send_s.at[group], at_y(1)).wait_send()
    for cp in results:
        cp.wait()


def finish(*refs):
    copies = [pltpu.make_async_copy(refs[i], refs[4 + i], refs[8].at[i]) for i in range(4)]
    for cp in copies:
        cp.start()
    for cp in copies:
        cp.wait()


def body(hidden, gain, head, targets, row_weight):
    V = pltpu.VMEM
    S = pltpu.SemaphoreType.DMA
    hbm = pl.BlockSpec(memory_space=pl.ANY)
    scratch = [
        V((2, 128), jnp.int32),
        V((2, 128), jnp.int32),
        V((1, 1), F32),
        V((64, 1024), F32),
        V((1, 1024), F32),
        V((256, 1024), BF16),
        V((64, 1024), BF16),
        V((8, 4, 2, 64, 512), BF16),
        V((2, 4, 256, 1024), BF16),
        V((8, 512, 512), BF16),
        V((4, 1, 1024), F32),
        V((2, 8, 128), F32),
        V((2, 256, 128), F32),
        V((2, 256, 128), F32),
        V((2, 256, 128), F32),
        V((2, 256, 128), F32),
        V((512, 512), F32),
        V((512, 512), F32),
        V((2, 256, 512), BF16),
        V((512, 512), BF16),
        V((8, 4, 8, 128), F32),
        V((8, 4, 8, 128), F32),
        V((512, 128), F32),
        V((512, 128), F32),
        V((512, 128), F32),
        V((4, 1, 128), F32),
        V((16384, 128), F32),
        V((8, 2, 160, 128), BF16),
        V((8, 2, 160, 128), BF16),
        V((8, 2, 2, 160, 128), BF16),
        V((8, 2, 2, 160, 128), BF16),
        V((2, 160, 128), BF16),
        V((2, 160, 128), BF16),
        V((2, 2, 160, 128), BF16),
        V((2, 2, 160, 128), BF16),
        V((2, 2, 2, 160, 128), F32),
        V((2, 2, 2, 160, 128), F32),
        V((2, 4, 32, 128), BF16),
        V((2, 4, 32, 128), BF16),
        V((2, 3, 4, 4, 64, 128), BF16),
        V((2, 3, 4, 4, 64, 128), BF16),
        V((3, 4, 64, 128), F32),
        V((3, 3, 64, 128), F32),
        V((384, 128), F32),
        V((128, 128), F32),
        V((2, 64, 512), F32),
        V((64, 512), F32),
        V((4, 256, 1024), F32),
        V((4, 256, 1024), F32),
        V((4, 256, 1024), F32),
        V((256, 1024), BF16),
        V((2, 128, 1024), BF16),
        V((2, 128, 1024), BF16),
        V((2, 128, 1024), BF16),
        V((2, 128, 1024), F32),
        V((4, 1, 1024), F32),
        V((2, 1, 1024), F32),
        V((3, 1, 1024), F32),
        V((1, 1152), F32),
        V((4, 1, 1152), F32),
        V((7, 1, 1152), F32),
        V((8, 128), F32),
        V((8, 128), F32),
        V((3, 8, 128), F32),
        V((2, 4, 8, 128), F32),
        S((5,)),
        S((4,)),
        S((3,)),
    ]
    shapes = [
        (), (), (), (4,), (2,), (3,), (2, 4), (8,), (3,), (2, 4, 4),
        (), (), (), (2, 4), (8,), (8, 2), (2, 4), (2, 2, 2), (2, 3, 4), (3,), (4,),
        (4,), (2,), (2,), (2,), (), (), (),
    ]
    scratch += [S(sh) if sh else S for sh in shapes]
    loss, gh, gg, gx = pl.pallas_call(
        kernel,
        out_shape=(
            jax.ShapeDtypeStruct((1, 1), F32),
            jax.ShapeDtypeStruct((64, 1024), F32),
            jax.ShapeDtypeStruct((1, 1024), F32),
            jax.ShapeDtypeStruct((256, 1024), BF16),
        ),
        in_specs=[pl.BlockSpec(memory_space=pltpu.HBM)] * 5,
        out_specs=(hbm,) * 4,
        scratch_shapes=scratch,
        compiler_params=pltpu.CompilerParams(
            collective_id=0, has_side_effects=True, vmem_limit_bytes=53 << 20
        ),
    )(*[
        pltpu.with_memory_space_constraint(a, pltpu.HBM)
        for a in (hidden, gain.reshape(1, 1024), head, targets.reshape(2, 128), row_weight.reshape(2, 128))
    ])
    loss, gh, gg, gx = pl.pallas_call(
        finish,
        out_shape=tuple(jax.ShapeDtypeStruct(a.shape, a.dtype) for a in (loss, gh, gg, gx)),
        in_specs=[hbm] * 4,
        out_specs=(hbm,) * 4,
        scratch_shapes=[S((4,))],
        compiler_params=pltpu.CompilerParams(vmem_limit_bytes=2 << 20),
    )(loss, gh, gg, gx)
    return (loss.reshape(()), gh, gg.reshape(1024), gx)


def solution(mesh):
    in_specs = (P("fsdp", "tp"), P("tp"), P("fsdp", "tp"), P("fsdp"), P("fsdp"))
    out_specs = (P(), P("fsdp", "tp"), P("tp"), P("fsdp", "tp"))
    return jax.shard_map(body, mesh=mesh, in_specs=in_specs, out_specs=out_specs, check_vma=False)
```
